32 devices in a mesh: seq: 8 (over z, y), head: 4 (over x, core).
Axes of the slice: x: 2, y: 2, z: 4, core: 2. Of those that a mesh axis runs over, the one named last changes fastest.
Arguments:
- hidden_in: bfloat16 [4, 2048, 768], P(None, ('seq', 'head')), may hold values from -5.2 to 5.2
- query_weight: bfloat16 [2, 768, 768], P(None, None, 'head'), may hold values from -0.21875 to 0.21875
- key_weight: bfloat16 [2, 768, 768], P(None, None, 'head'), may hold values from -0.21875 to 0.21875
- value_weight: bfloat16 [2, 768, 768], P(None, None, 'head'), may hold values from -0.21875 to 0.21875
- query_bias: float32 [2, 768], P(None, 'head'), may hold values from -3 to 3
- value_bias: float32 [2, 768], P(None, 'head'), may hold values from -3 to 3
- out_weight: bfloat16 [2, 768, 768], P(None, 'head'), may hold values from -0.4375 to 0.4375
- out_bias: float32 [2, 768], replicated, may hold values from -2 to 2
- conv_taps: float32 [2, 12, 65], P(None, 'head'), may hold values from -0.4 to 0.4
- up_weight: bfloat16 [2, 768, 3072], P(None, None, 'head'), may hold values from -0.21875 to 0.21875
- up_bias: float32 [2, 3072], P(None, 'head'), may hold values from -3 to 3
- down_weight: bfloat16 [2, 3072, 768], P(None, 'head'), may hold values from -0.109375 to 0.109375
- down_bias: float32 [2, 768], replicated, may hold values from -2 to 2
- gain_one: float32 [2, 768], replicated, may hold values from 0.5 to 1.5
- shift_one: float32 [2, 768], replicated, may hold values from -1 to 1
- gain_two: float32 [2, 768], replicated, may hold values from 0.5 to 1.5
- shift_two: float32 [2, 768], replicated, may hold values from -1 to 1
- out_grad: float32 [4, 2048, 768], P(None, ('seq', 'head')), may hold values from -6 to 6
- item_lengths: int32 [4, 4], replicated, may hold values from 0 to 2048, as said below
Outputs:
- layer_out: bfloat16 [4, 2048, 768], P(None, ('seq', 'head'))
- hidden_grad: float32 [4, 2048, 768], P(None, ('seq', 'head'))
- query_weight_grad: float32 [2, 768, 768], P(None, None, 'head')
- key_weight_grad: float32 [2, 768, 768], P(None, None, 'head')
- value_weight_grad: float32 [2, 768, 768], P(None, None, 'head')
- query_bias_grad: float32 [2, 768], P(None, 'head')
- value_bias_grad: float32 [2, 768], P(None, 'head')
- out_weight_grad: float32 [2, 768, 768], P(None, 'head')
- out_bias_grad: float32 [2, 768], replicated
- conv_taps_grad: float32 [2, 12, 65], P(None, 'head')
- up_weight_grad: float32 [2, 768, 3072], P(None, None, 'head')
- up_bias_grad: float32 [2, 3072], P(None, 'head')
- down_weight_grad: float32 [2, 3072, 768], P(None, 'head')
- down_bias_grad: float32 [2, 768], replicated
- gain_one_grad: float32 [2, 768], replicated
- shift_one_grad: float32 [2, 768], replicated
- gain_two_grad: float32 [2, 768], replicated
- shift_two_grad: float32 [2, 768], replicated
The draws below stay inside these ranges and needn't reach their ends.
Inputs may be any that keep to these rules, and one draw needn't show every extreme that they name: `item_lengths`: row r lists the lengths of the items packed into row r in order of position, then zeros; each length is 512 times a power of two, every item starts at a multiple of its own length, and the lengths of a row sum to 2048.
All inputs are finite; a program needn't handle non-finite values.
Results may differ from the reference program's by a relative error of at most 0.015.
Values may be sent and summed in bfloat16 or wider, within the bound.
No kernel may reach another device: no remote copies, remote signals or barrier semaphores. Data moves between devices by JAX's collectives and lax.ppermute only.
A program may use at most 192 MiB of HBM per device.

```python
import math
import jax
import jax.numpy as jnp
import numpy as np
from jax import lax

D = 768
HEADS = 12
LANDMARKS = 64
FF = 3072
KERNEL = 65
NS_STEPS = 6
LAYERS = 2
ROWS = 4
MIN_LEN = 512
HD = 768
RLEN = 2048
NIT = 4


def draw_hidden_in(key, part):
    key = jax.random.fold_in(key, 11)
    noise_key, amp_key, period_key, phase_key = jax.random.split(key, 4)
    noise = jax.random.truncated_normal(noise_key, -4.0, 4.0, (ROWS, RLEN, D), jnp.float32)
    amplitude = jax.random.uniform(amp_key, (4, D), jnp.float32, -0.6, 0.6)
    periods = MIN_LEN / 8.0 * 2.0 ** jax.random.uniform(period_key, (4, D), jnp.float32, 0.0, 6.0)
    phases = jax.random.uniform(phase_key, (ROWS, 4, D), jnp.float32, -math.pi, math.pi)
    positions = jnp.arange(RLEN, dtype=jnp.float32)
    smooth = jnp.zeros((ROWS, RLEN, D), jnp.float32)
    for wave_index in range(4):
        angle = 2.0 * math.pi * positions[None, :, None] / periods[wave_index][None, None, :] + phases[:, wave_index][:, None, :]
        smooth = smooth + amplitude[wave_index][None, None, :] * jnp.cos(angle)
    return (0.7 * noise + smooth).astype(jnp.bfloat16)


def draw_item_lengths(key, part):
    key = jax.random.fold_in(key, 23)
    split_key, row_key = jax.random.split(key)
    levels = NIT.bit_length() - 1
    leaves = np.arange(NIT)
    depth = jnp.zeros((ROWS, NIT), jnp.int32)
    alive = jnp.ones((ROWS, NIT), jnp.int32)
    for level_index in range(levels):
        coins = (jax.random.randint(jax.random.fold_in(split_key, level_index), (ROWS, 2 ** level_index), 0, 4) > 0).astype(jnp.int32)
        node_split = coins[:, leaves >> levels - level_index]
        alive = alive * node_split
        depth = depth + alive
    whole_row = jax.random.randint(row_key, (), 0, ROWS)
    depth = jnp.where((jnp.arange(ROWS) == whole_row)[:, None], 0, depth)
    size = jnp.right_shift(jnp.int32(NIT), depth)
    leaf_index = jnp.asarray(leaves, jnp.int32)[None, :]
    is_start = leaf_index % size == 0
    lengths = jnp.where(is_start, size * MIN_LEN, 0)
    order = jnp.argsort(jnp.where(is_start, leaf_index, NIT + leaf_index), axis=1, stable=True)
    return jnp.take_along_axis(lengths, order, axis=1).astype(jnp.int32)


def steps_of(rng, dims, cuts, smallest, largest):
    factor_of, own = 1.0, jax.random.fold_in(rng, 6)
    for axis_at, blocks in cuts:
        heights = jnp.exp(jax.random.uniform(jax.random.fold_in(own, axis_at), (blocks,), jnp.float32, smallest / len(cuts), largest / len(cuts)))
        factor_of = factor_of * jnp.repeat(heights, dims[axis_at] // blocks).reshape([-1 if axis == axis_at else 1 for axis in range(len(dims))])
    return factor_of


def gaussian(rng, shape, deviation, most, cuts=(), held_as=jnp.bfloat16):
    result = jax.random.normal(rng, shape, jnp.float32) * deviation
    if len(cuts) > 0:
        result = steps_of(rng, shape, cuts, -0.22, 0.18) * result
    return jnp.clip(result, min=-most, max=most).astype(held_as)


def setup_inputs(seed: int = 0) -> dict:
    splits = jax.random.split(jax.random.key(seed), 20)
    hidden_in = draw_hidden_in(jax.random.fold_in(splits[19], 71), 0)
    query_weight = gaussian(splits[1], (LAYERS, D, HD), D ** -0.5, 0.21875, ((2, 4),))
    key_weight = gaussian(splits[2], (LAYERS, D, HD), D ** -0.5, 0.21875, ((2, 4),))
    value_weight = gaussian(splits[3], (LAYERS, D, HD), D ** -0.5, 0.21875, ((2, 4),))
    query_bias = gaussian(splits[4], (LAYERS, HD), 0.5, 3.0, ((1, 4),), jnp.float32)
    value_bias = gaussian(splits[5], (LAYERS, HD), 0.5, 3.0, ((1, 4),), jnp.float32)
    out_weight = gaussian(splits[6], (LAYERS, HD, D), (HD // 4) ** -0.5, 0.4375, ((1, 4),))
    out_bias = gaussian(splits[7], (LAYERS, D), 0.3, 2.0, (), jnp.float32)
    conv_taps = gaussian(splits[8], (LAYERS, HEADS, KERNEL), 0.1, 0.4, ((1, 4),), jnp.float32)
    up_weight = gaussian(splits[9], (LAYERS, D, FF), D ** -0.5, 0.21875, ((2, 4),))
    up_bias = gaussian(splits[10], (LAYERS, FF), 0.5, 3.0, ((1, 4),), jnp.float32)
    down_weight = gaussian(splits[11], (LAYERS, FF, D), FF ** -0.5, 0.109375, ((1, 4),))
    down_bias = gaussian(splits[12], (LAYERS, D), 0.3, 2.0, (), jnp.float32)
    gain_one = jnp.clip(1.0 + 0.1 * jax.random.normal(splits[13], (LAYERS, D), jnp.float32), 0.5, 1.5)
    shift_one = gaussian(splits[14], (LAYERS, D), 0.2, 1.0, (), jnp.float32)
    gain_two = jnp.clip(1.0 + 0.1 * jax.random.normal(splits[15], (LAYERS, D), jnp.float32), 0.5, 1.5)
    shift_two = gaussian(splits[16], (LAYERS, D), 0.2, 1.0, (), jnp.float32)
    out_grad = gaussian(splits[17], (ROWS, RLEN, D), 1.0, 6.0, ((1, 32),), jnp.float32)
    item_lengths = draw_item_lengths(jax.random.fold_in(splits[19], 71), 0)
    return dict(hidden_in=hidden_in, query_weight=query_weight, key_weight=key_weight, value_weight=value_weight, query_bias=query_bias, value_bias=value_bias, out_weight=out_weight, out_bias=out_bias, conv_taps=conv_taps, up_weight=up_weight, up_bias=up_bias, down_weight=down_weight, down_bias=down_bias, gain_one=gain_one, shift_one=shift_one, gain_two=gain_two, shift_two=shift_two, out_grad=out_grad, item_lengths=item_lengths)


HIGHEST = lax.Precision.HIGHEST
EPSILON = 1e-05
FLOOR_TOP = -1e+30

@jax.custom_vjp
def low(v):
    return lax.optimization_barrier(v.astype(jnp.bfloat16)).astype(jnp.float32)

@jax.custom_vjp
def low_back(v):
    return v

def low_keep(v):
    return (low(v), None)

def low_pass(kept, grad):
    return (grad,)

def back_keep(v):
    return (v, None)

def back_low(kept, grad):
    return (low(grad),)
low.defvjp(low_keep, low_pass)
low_back.defvjp(back_keep, back_low)

def layer_norm(values, gain, offset):
    centred = values - lax.optimization_barrier(jnp.mean(values, axis=-1, keepdims=True))
    variance = lax.optimization_barrier(jnp.mean(centred * centred, axis=-1, keepdims=True))
    return centred * lax.rsqrt(variance + EPSILON) * gain + offset

def pseudo_inverse(matrix):
    columns = lax.optimization_barrier(jnp.sum(matrix, axis=-2))
    bound = lax.optimization_barrier(jnp.sum(columns ** 8, axis=-1)) ** 0.125
    iterate = jnp.swapaxes(matrix, -1, -2) / bound[..., None, None]
    identity = jnp.eye(matrix.shape[-1], dtype=matrix.dtype)
    for step_index in range(NS_STEPS):
        product = jnp.matmul(matrix, iterate, precision=HIGHEST)
        inner = jnp.matmul(product, 7.0 * identity - product, precision=HIGHEST)
        middle = jnp.matmul(product, 15.0 * identity - inner, precision=HIGHEST)
        iterate = 0.25 * jnp.matmul(iterate, 13.0 * identity - middle, precision=HIGHEST)
    return iterate

def project(values, weight):
    return jnp.einsum('rpd,dc->rpc', values, weight, precision=HIGHEST)

def item_positions(item_lengths):
    lengths = item_lengths.astype(jnp.int32)
    ends = jnp.cumsum(lengths, axis=1).astype(jnp.int32)
    starts = (ends - lengths).astype(jnp.int32)
    positions = jnp.arange(RLEN, dtype=jnp.int32)
    owner = lax.optimization_barrier(jnp.sum((ends[:, None, :] <= positions[None, :, None]).astype(jnp.int32), axis=2)).astype(jnp.int32)
    segment = (jnp.maximum(lengths, LANDMARKS) // LANDMARKS).astype(jnp.int32)
    own_start = jnp.take_along_axis(starts, owner, axis=1)
    own_segment = jnp.take_along_axis(segment, owner, axis=1)
    slots = (owner * LANDMARKS + (positions[None, :] - own_start) // own_segment).astype(jnp.int32)
    block_owner = owner[:, ::MIN_LEN]
    return (owner, slots, segment, block_owner)

def row_pool(values, slots):
    return jax.ops.segment_sum(values, slots, num_segments=NIT * LANDMARKS)

def nystrom(queries, tok_keys, tok_values, conv_taps, layout):
    owner, slots, segment, block_owner = layout
    batch_rows = queries.shape[0]
    heads = conv_taps.shape[0]
    head_dim = queries.shape[-1] // heads
    scale = head_dim ** (-0.5)
    shape4 = (batch_rows, RLEN, heads, head_dim)
    queries = queries.reshape(shape4)
    tok_keys = tok_keys.reshape(shape4)
    tok_values = tok_values.reshape(shape4)
    counts = jnp.repeat(segment, LANDMARKS, axis=1).astype(jnp.float32)

    def pooled(values):
        sums = jax.vmap(row_pool)(values, slots)
        return low((sums / counts[:, :, None, None]).reshape(batch_rows, NIT, LANDMARKS, heads, head_dim))
    land_q = pooled(queries)
    land_k = pooled(tok_keys)
    blocks = RLEN // MIN_LEN
    block_shape = (batch_rows, blocks, MIN_LEN, heads, head_dim)
    query_blocks = queries.reshape(block_shape)
    key_blocks = tok_keys.reshape(block_shape)
    value_blocks = tok_values.reshape(block_shape)
    index_five = block_owner[:, :, None, None, None]
    index_four = block_owner[:, :, None, None]
    member = block_owner[:, :, None] == jnp.arange(NIT, dtype=jnp.int32)[None, None, :]
    member_float = member.astype(jnp.float32)
    block_land_q = jnp.take_along_axis(land_q, index_five, axis=1)
    far_scores = jnp.einsum('rbjhe,rbthe->rbjht', block_land_q, key_blocks, precision=HIGHEST) * scale
    block_top = lax.optimization_barrier(jnp.max(far_scores, axis=-1))
    block_total = lax.optimization_barrier(jnp.sum(jnp.exp(far_scores - block_top[..., None]), axis=-1))
    item_top = lax.optimization_barrier(jnp.max(jnp.where(member[:, :, :, None, None], block_top[:, :, None], FLOOR_TOP), axis=1))
    top_of_block = jnp.take_along_axis(item_top, index_four, axis=1)
    item_total = jnp.einsum('rbk,rbjh->rkjh', member_float, block_total * jnp.exp(block_top - top_of_block), precision=HIGHEST)
    total_of_block = jnp.take_along_axis(item_total, index_four, axis=1)
    far_probs = jnp.exp(far_scores - top_of_block[..., None]) / total_of_block[..., None]
    block_mix = jnp.einsum('rbjht,rbthe->rbjhe', far_probs, value_blocks, precision=HIGHEST)
    weighted = jnp.einsum('rbk,rbjhe->rkjhe', member_float, block_mix, precision=HIGHEST)
    land_scores = jnp.einsum('rkjhe,rkihe->rkhji', land_q, land_k, precision=HIGHEST) * scale
    inverse = pseudo_inverse(jax.nn.softmax(land_scores, axis=-1))
    land_out = jnp.einsum('rkhji,rkihe->rkjhe', inverse, weighted, precision=HIGHEST)
    block_land_k = jnp.take_along_axis(land_k, index_five, axis=1)
    block_out = jnp.take_along_axis(land_out, index_five, axis=1)
    near_scores = jnp.einsum('rbthe,rbjhe->rbthj', query_blocks, block_land_k, precision=HIGHEST) * scale
    near_probs = jax.nn.softmax(near_scores, axis=-1)
    mixed = jnp.einsum('rbthj,rbjhe->rbthe', near_probs, block_out, precision=HIGHEST).reshape(shape4)
    taps = conv_taps.shape[1]
    half = (taps - 1) // 2
    padded = jnp.pad(tok_values, ((0, 0), (half, half), (0, 0), (0, 0)))
    owner_pad = jnp.pad(owner, ((0, 0), (half, half)), constant_values=-1)
    conv_out = jnp.zeros(shape4, jnp.float32)
    for tap_index in range(taps):
        same = (owner_pad[:, tap_index:tap_index + RLEN] == owner)[:, :, None, None]
        shifted = jnp.where(same, padded[:, tap_index:tap_index + RLEN], 0.0)
        conv_out = conv_out + conv_taps[:, tap_index][None, None, :, None] * shifted
    return (mixed + conv_out).reshape(batch_rows, RLEN, heads * head_dim)

def one_layer(hidden, params, layout):
    query_weight, key_weight, value_weight, query_bias, value_bias, out_weight, out_bias, conv_taps, up_weight, up_bias, down_weight, down_bias, gain_one, shift_one, gain_two, shift_two = params
    xa = low(hidden)
    queries = low_back(project(xa, query_weight) + query_bias)
    tok_keys = low_back(project(xa, key_weight))
    tok_values = low(low_back(project(xa, value_weight) + value_bias))
    att_low = low(nystrom(queries, tok_keys, tok_values, conv_taps, layout))
    attn_out = low_back(project(att_low, out_weight) + out_bias)
    normed = layer_norm(hidden + attn_out, gain_one, shift_one)
    up_pre = low_back(project(low(normed), up_weight) + up_bias)
    gelu_low = low(jax.nn.gelu(up_pre, approximate=False))
    mlp_out = low_back(project(gelu_low, down_weight) + down_bias)
    return layer_norm(normed + mlp_out, gain_two, shift_two)

def reference(hidden_in, query_weight, key_weight, value_weight, query_bias, value_bias, out_weight, out_bias, conv_taps, up_weight, up_bias, down_weight, down_bias, gain_one, shift_one, gain_two, shift_two, out_grad, item_lengths):
    layout = item_positions(item_lengths)
    weights = tuple((array.astype(jnp.float32) for array in (query_weight, key_weight, value_weight, query_bias, value_bias, out_weight, out_bias, conv_taps, up_weight, up_bias, down_weight, down_bias, gain_one, shift_one, gain_two, shift_two)))

    def forward(start, *params):
        hidden = start
        for layer_index in range(LAYERS):
            hidden = one_layer(hidden, tuple((array[layer_index] for array in params)), layout)
        return hidden
    final, pull = jax.vjp(forward, hidden_in.astype(jnp.float32), *weights)
    grads = pull(out_grad.astype(jnp.float32))
    return (final.astype(jnp.bfloat16), grads[0], grads[1], grads[2], grads[3], grads[4], grads[5], grads[6], grads[7], grads[8], grads[9], grads[10], grads[11], grads[12], grads[13], grads[14], grads[15], grads[16])
```

```python
import functools

import jax
import jax.numpy as jnp
from jax import lax
from jax.experimental import pallas as pl
from jax.experimental.pallas import tpu as pltpu
from jax.sharding import PartitionSpec as P

LANDMARKS = 64
NS_STEPS = 6


HIGHEST = lax.Precision.HIGHEST
EPSILON = 1e-05
FLOOR_TOP = -1e30
LOW = jnp.bfloat16
GROUP = ((0, 2), (1, 0), (1, 2))


def layer_norm(values, gain, offset):
    centred = values - jnp.mean(values, axis=-1, keepdims=True)
    variance = jnp.mean(centred * centred, axis=-1, keepdims=True)
    return centred * lax.rsqrt(variance + EPSILON) * gain + offset


def exchange(values, seq_mask, head_mask):
    if seq_mask == 0:
        count = lax.axis_size("head")
        return lax.ppermute(values, "head", [(i, i ^ head_mask) for i in range(count)])
    if head_mask == 0:
        count = lax.axis_size("seq")
        return lax.ppermute(values, "seq", [(i, i ^ seq_mask) for i in range(count)])
    heads = lax.axis_size("head")
    route = []
    for s in range(lax.axis_size("seq")):
        for h in range(heads):
            route.append((s * heads + h, (s ^ seq_mask) * heads + (h ^ head_mask)))
    return lax.ppermute(values, ("seq", "head"), route)


def rank_shift(values, step):
    heads = lax.axis_size("head")
    ranks = lax.axis_size("seq") * (heads // 2)
    route = []
    for rank in range(ranks):
        target = rank + step
        if 0 <= target < ranks:
            for core in range(2):
                source_dev = (rank // 2) * heads + (rank % 2) * 2 + core
                target_dev = (target // 2) * heads + (target % 2) * 2 + core
                route.append((source_dev, target_dev))
    return lax.ppermute(values, ("seq", "head"), route)


def place():
    seq = lax.axis_index("seq")
    head = lax.axis_index("head")
    return seq, head // 2, head % 2


def pair_join(values, axis):
    core = place()[2]
    other = exchange(values, 0, 1)
    low = jnp.where(core == 0, values, other)
    high = jnp.where(core == 0, other, values)
    return jnp.concatenate([low, high], axis=axis)


def pair_collect(terms):
    core = place()[2]
    half = terms.shape[1] // 2
    low, high = terms[:, :half], terms[:, half:]
    mine = jnp.where(core == 0, low, high)
    theirs = jnp.where(core == 0, high, low).astype(jnp.bfloat16)
    return mine + exchange(theirs, 0, 1).astype(jnp.float32)


def group_index():
    seq, across, core = place()
    return across + 2 * (seq % 2)


def upper_levels():
    levels = (lax.axis_size("seq") // 2).bit_length() - 1
    return [(low, min(2, levels - low)) for low in range(0, levels, 2)]


def nn(one, two, precision=None):
    return lax.dot_general(
        one, two, (((1,), (0,)), ((), ())), precision, preferred_element_type=jnp.float32
    )


def nt(one, two, precision=None):
    return lax.dot_general(
        one, two, (((1,), (1,)), ((), ())), precision, preferred_element_type=jnp.float32
    )


def tn(one, two, precision=None):
    return lax.dot_general(
        one, two, (((0,), (0,)), ((), ())), precision, preferred_element_type=jnp.float32
    )


def on_core(kernel, outs, scalars, *arrays):
    shapes = tuple(jax.ShapeDtypeStruct(shape, dtype) for shape, dtype in outs)
    specs = [pl.BlockSpec(memory_space=pltpu.SMEM)] if scalars is not None else []
    specs += [pl.BlockSpec(memory_space=pltpu.VMEM)] * len(arrays)
    given = ((scalars,) if scalars is not None else ()) + arrays
    return pl.pallas_call(
        kernel,
        out_shape=shapes,
        in_specs=specs,
        out_specs=tuple(pl.BlockSpec(memory_space=pltpu.VMEM) for _ in outs),
        compiler_params=pltpu.CompilerParams(vmem_limit_bytes=48 * 1024 * 1024),
    )(*given)


def tokens_of(row, tok_row):
    return pl.ds(pl.multiple_of(row * tok_row, tok_row), tok_row)


def lanes(shape):
    return lax.broadcasted_iota(jnp.int32, shape, len(shape) - 1)


def join_pool_kernel(spot, own, other, pool, full, one, two, three, four):
    rows, piece, model = own.shape
    tok_row = 2 * piece
    core = spot[1]
    half = model // 2
    for row in range(rows):
        mine = pl.multiple_of(row * tok_row + core * piece, piece)
        theirs = pl.multiple_of(row * tok_row + (1 - core) * piece, piece)
        full[pl.ds(mine, piece), :] = own[row]
        full[pl.ds(theirs, piece), :] = other[row]
    side = pl.ds(pl.multiple_of(core * half, half), half)
    for step, out in enumerate((one, two, three, four)):
        row = spot[0] ^ step
        block = full[tokens_of(row, tok_row), side]
        out[...] = nn(pool[row], block).astype(LOW)


def rim_blocks(block_of, rows, tok_row, half):
    low, high = None, None
    for row in range(rows):
        block = block_of(row).astype(jnp.float32)
        lane = lanes(block.shape)
        first = block if row == 0 else pltpu.roll(block, row * half, 1)
        shift = (row * half + half) % tok_row
        last = block if shift == 0 else pltpu.roll(block, shift, 1)
        inside = lane // half == row
        low = jnp.where(inside, first, 0.0 if low is None else low)
        high = jnp.where(inside, last, 0.0 if high is None else high)
    return low.astype(LOW), high.astype(LOW)


def far_kernel(half, spot, qkv, land, one, two, three, four, low, high):
    width = qkv.shape[0] // 3
    head_dim = LANDMARKS
    heads = width // head_dim
    tok_row = qkv.shape[1] // 4
    scale = head_dim ** (-0.5)
    for step, out in enumerate((one, two, three, four)):
        here = tokens_of(spot[0] ^ step, tok_row)
        logs = jnp.zeros((LANDMARKS, out.shape[1] - width), jnp.float32)
        lane = lanes(logs.shape)
        for head in range(heads):
            cols = slice(head * head_dim, (head + 1) * head_dim)
            keys = qkv[width + head * head_dim : width + (head + 1) * head_dim, here]
            values = qkv[2 * width + head * head_dim : 2 * width + (head + 1) * head_dim, here]
            land_q = land[step * LANDMARKS : (step + 1) * LANDMARKS, cols]
            scores = nn(land_q, keys) * scale
            top = jnp.max(scores, axis=1, keepdims=True)
            grown = jnp.exp(scores - top)
            total = jnp.sum(grown, axis=1, keepdims=True)
            out[:, cols] = nt(grown.astype(LOW), values) / total
            logs = jnp.where(lane == head, top + jnp.log(total), logs)
        out[:, width:] = logs
    low[...], high[...] = rim_blocks(
        lambda row: qkv[2 * width :, row * tok_row : (row + 1) * tok_row], 4, tok_row, half
    )


def merged(flags, pieces, width):
    head_dim = LANDMARKS
    mixes, logs = [], []
    for head in range(width // head_dim):
        cols = slice(head * head_dim, (head + 1) * head_dim)
        column = slice(width + head, width + head + 1)
        log = [pieces[0][:, column]]
        for index, piece in enumerate(pieces[1:]):
            log.append(jnp.where(flags[index] > 0, piece[:, column], FLOOR_TOP))
        top = functools.reduce(jnp.maximum, log)
        shares = [jnp.exp(value - top) for value in log]
        total = functools.reduce(jnp.add, shares)
        mix = sum(share * piece[:, cols] for share, piece in zip(shares, pieces))
        mixes.append(mix / total)
        logs.append(top + jnp.log(total))
    return mixes, logs


def merge_kernel(count, flags, *refs):
    out = refs[count]
    width = out.shape[1] - 128
    mixes, logs = merged(flags, refs[:count], width)
    packed = jnp.zeros((LANDMARKS, 128), jnp.float32)
    lane = lanes(packed.shape)
    for head, (mix, log) in enumerate(zip(mixes, logs)):
        out[:, head * LANDMARKS : (head + 1) * LANDMARKS] = mix
        packed = jnp.where(lane == head, log, packed)
    out[:, width:] = packed


def packed_parts(columns):
    packed = jnp.zeros((LANDMARKS, 128), jnp.float32)
    lane = lanes(packed.shape)
    for head, column in enumerate(columns):
        for part in range(3):
            rounded = column.astype(LOW).astype(jnp.float32)
            packed = jnp.where(lane == head + 8 * part, rounded, packed)
            column = column - rounded
    return packed.astype(LOW)


def unpacked_part(packed, head):
    packed = packed.astype(jnp.float32)
    return (
        packed[:, head : head + 1]
        + packed[:, head + 8 : head + 9]
        + packed[:, head + 16 : head + 17]
    )


def land_out_kernel(count, flags, *refs):
    inverse, out, weighted = refs[count:]
    width = weighted.shape[1]
    mixes, logs = merged(flags, refs[:count], width)
    for head, mix in enumerate(mixes):
        cols = slice(head * LANDMARKS, (head + 1) * LANDMARKS)
        weighted[:, cols] = mix
        out[:, cols] = nn(inverse[head], mix, HIGHEST).astype(LOW)
    out[:, width:] = packed_parts(logs)


def inverse_kernel(land, amats, inverses, products, seconds, thirds):
    width = land.shape[1] // 2
    heads = width // LANDMARKS
    scale = LANDMARKS ** (-0.5)
    shape = (LANDMARKS, LANDMARKS)
    rows = lax.broadcasted_iota(jnp.int32, shape, 0)
    eye = (rows == lanes(shape)).astype(jnp.float32)
    matrices, iterates = [], []
    for head in range(heads):
        cols = slice(head * LANDMARKS, (head + 1) * LANDMARKS)
        keys = slice(width + head * LANDMARKS, width + (head + 1) * LANDMARKS)
        scores = nt(land[:LANDMARKS, cols], land[:LANDMARKS, keys]) * scale
        grown = jnp.exp(scores - jnp.max(scores, axis=1, keepdims=True))
        matrix = grown / jnp.sum(grown, axis=1, keepdims=True)
        columns = jnp.sum(matrix, axis=0, keepdims=True)
        square = columns * columns
        fourth = square * square
        bound = jnp.sum(fourth * fourth, axis=1, keepdims=True)
        bound = jnp.exp(jnp.log(bound) * 0.125)
        amats[head] = matrix
        matrices.append(matrix)
        iterates.append(matrix.T / bound)
    for step in range(NS_STEPS):
        product = [nn(a, z, HIGHEST) for a, z in zip(matrices, iterates)]
        inner = [nn(p, 7.0 * eye - p, HIGHEST) for p in product]
        second = [15.0 * eye - value for value in inner]
        third = [13.0 * eye - nn(p, m, HIGHEST) for p, m in zip(product, second)]
        for head in range(heads):
            inverses[step * heads + head] = iterates[head]
            products[step * heads + head] = product[head]
            seconds[step * heads + head] = second[head]
            thirds[step * heads + head] = third[head]
        iterates = [0.25 * nn(z, m, HIGHEST) for z, m in zip(iterates, third)]
    for head in range(heads):
        inverses[NS_STEPS * heads + head] = iterates[head]


def band_blocks(line, tok_row, half):
    span = line.shape[1]
    wide = jnp.broadcast_to(line, (tok_row, span))
    middle = pltpu.roll(wide, 0, 1, stride=1, stride_axis=0)[:, :tok_row]
    short = jnp.broadcast_to(line, (half, span))
    low = pltpu.roll(short, span - half, 1, stride=1, stride_axis=0)[:, :tok_row]
    high = pltpu.roll(short, tok_row, 1, stride=1, stride_axis=0)[:, :tok_row]
    reps = tok_row // half
    return [
        part.astype(LOW)
        for part in (middle, jnp.concatenate([low] * reps, 0), jnp.concatenate([high] * reps, 0))
    ]


def near_kernel(half, spot, qkv, low, high, rims, land, one, two, three, four, line, out):
    width = qkv.shape[0] // 3
    tok_row = qkv.shape[1] // 4
    head_dim = LANDMARKS
    scale = head_dim ** (-0.5)
    low_all = low[...].astype(jnp.float32) * rims[0:1, :]
    high_all = high[...].astype(jnp.float32) * rims[1:2, :]
    lane = lanes((head_dim, tok_row)) // half
    bands = [band_blocks(line[h : h + 1, :], tok_row, half) for h in range(width // head_dim)]
    for step, mixed in enumerate((one, two, three, four)):
        row = spot[0] ^ step
        here = tokens_of(row, tok_row)
        land_rows = slice(step * LANDMARKS, (step + 1) * LANDMARKS)
        for head in range(width // head_dim):
            cols = slice(head * head_dim, (head + 1) * head_dim)
            keys = slice(width + head * head_dim, width + (head + 1) * head_dim)
            queries = qkv[cols, here]
            scores = nn(land[land_rows, keys], queries) * scale
            grown = jnp.exp(scores - jnp.max(scores, axis=0, keepdims=True))
            probs = grown / jnp.sum(grown, axis=0, keepdims=True)
            total = tn(mixed[:, cols], probs.astype(LOW))
            values = qkv[2 * width + head * head_dim : 2 * width + (head + 1) * head_dim, here]
            total = total + nn(values, bands[head][0])
            mine = lane == row
            total = total + nn(jnp.where(mine, low_all[cols, :], 0.0).astype(LOW), bands[head][1])
            total = total + nn(jnp.where(mine, high_all[cols, :], 0.0).astype(LOW), bands[head][2])
            out[cols, here] = total.astype(LOW)


def near_back_kernel(half, spot, qkv, grads, land, *refs):
    mixes, queries_out = refs[:4], refs[4]
    land_outs, land_keys, low, high = refs[5:9], refs[9:13], refs[13], refs[14]
    width = qkv.shape[0] // 3
    tok_row = qkv.shape[1] // 4
    head_dim = LANDMARKS
    scale = head_dim ** (-0.5)
    for step in range(4):
        here = tokens_of(spot[0] ^ step, tok_row)
        land_rows = slice(step * LANDMARKS, (step + 1) * LANDMARKS)
        for head in range(width // head_dim):
            cols = slice(head * head_dim, (head + 1) * head_dim)
            keys = slice(width + head * head_dim, width + (head + 1) * head_dim)
            queries = qkv[cols, here]
            land_k = land[land_rows, keys]
            scores = nn(land_k, queries) * scale
            grown = jnp.exp(scores - jnp.max(scores, axis=0, keepdims=True))
            probs = grown / jnp.sum(grown, axis=0, keepdims=True)
            grad = grads[cols, here]
            grad_probs = nn(mixes[step][:, cols], grad)
            inner = jnp.sum(grad_probs * probs, axis=0, keepdims=True)
            grad_scores = (probs * (grad_probs - inner) * scale).astype(LOW)
            queries_out[cols, here] = tn(land_k, grad_scores)
            land_keys[step][:, cols] = nt(grad_scores, queries).astype(LOW)
            land_outs[step][:, cols] = nt(probs.astype(LOW), grad).astype(LOW)
    low[...], high[...] = rim_blocks(
        lambda row: grads[:, row * tok_row : (row + 1) * tok_row], 4, tok_row, half
    )


def conv_back_kernel(half, qkv, grads, low, high, grad_low, grad_high, rims, line, out, taps):
    width = qkv.shape[0] // 3
    tok_row = qkv.shape[1] // 4
    head_dim = LANDMARKS
    span = line.shape[1]
    low_all = low[...].astype(jnp.float32) * rims[0:1, :]
    high_all = high[...].astype(jnp.float32) * rims[1:2, :]
    grad_low_all = grad_low[...].astype(jnp.float32) * rims[0:1, :]
    grad_high_all = grad_high[...].astype(jnp.float32) * rims[1:2, :]
    lane = lanes((head_dim, tok_row)) // half
    square = (tok_row, tok_row)
    turned = (lax.broadcasted_iota(jnp.int32, square, 0) + lanes(square) == tok_row - 1).astype(LOW)
    wide = lanes((tok_row, span))
    for head in range(width // head_dim):
        cols = slice(head * head_dim, (head + 1) * head_dim)
        bands = band_blocks(line[head : head + 1, :], tok_row, half)
        fields = [jnp.zeros(square, jnp.float32) for _ in range(3)]
        for row in range(4):
            here = slice(row * tok_row, (row + 1) * tok_row)
            mine = lane == row

            def rim(block):
                return jnp.where(mine, block[cols, :], 0.0).astype(LOW)

            grad = grads[cols, here]
            values = qkv[2 * width + head * head_dim : 2 * width + (head + 1) * head_dim, here]
            total = nn(grad, bands[0]) + nn(rim(grad_low_all), bands[1])
            out[cols, here] = total + nn(rim(grad_high_all), bands[2])
            backward = nn(grad, turned).astype(LOW)
            for index, block in enumerate((values, rim(low_all), rim(high_all))):
                fields[index] = fields[index] + tn(backward, block)
        ends = []
        for field in fields[1:]:
            folded = field + pltpu.roll(field, 2 * half, 1)
            folded = folded + pltpu.roll(folded, half, 1)
            ends.append(jnp.concatenate([folded, folded], axis=1))
        whole = jnp.concatenate([fields[0], jnp.zeros(square, jnp.float32)], axis=1)
        whole = pltpu.roll(whole, half, 1)
        whole = jnp.where(wide < half, ends[0], whole)
        right = (wide >= half + tok_row) & (wide < 2 * half + tok_row)
        whole = jnp.where(right, ends[1], whole)
        whole = pltpu.roll(whole, span - tok_row + 1, 1, stride=1, stride_axis=0)
        taps[head : head + 1, :] = jnp.sum(whole, axis=0, keepdims=True)[:, :128]


def mixture_grad_kernel(grads, inverse, weighted, out):
    width = grads.shape[1]
    inner = []
    for head in range(width // LANDMARKS):
        cols = slice(head * LANDMARKS, (head + 1) * LANDMARKS)
        value = tn(inverse[head], grads[:, cols], HIGHEST).astype(LOW)
        out[:, cols] = value
        product = value.astype(jnp.float32) * weighted[:, cols]
        inner.append(jnp.sum(product, axis=1, keepdims=True))
    out[:, width:] = packed_parts(inner)


def inverse_back_kernel(
    grads, weighted, land, amats, inverses, products, seconds, thirds, out
):
    width = grads.shape[1]
    heads = width // LANDMARKS
    scale = LANDMARKS ** (-0.5)
    shape = (LANDMARKS, LANDMARKS)
    rows = lax.broadcasted_iota(jnp.int32, shape, 0)
    eye = (rows == lanes(shape)).astype(jnp.float32)
    every = range(heads)
    columns = [slice(head * LANDMARKS, (head + 1) * LANDMARKS) for head in every]
    grad = [nt(grads[:, c], weighted[:, c], HIGHEST) for c in columns]
    matrices = [amats[head] for head in every]
    total = [jnp.zeros(shape, jnp.float32) for _ in every]
    for step in reversed(range(NS_STEPS)):
        z = [inverses[step * heads + head] for head in every]
        p = [products[step * heads + head] for head in every]
        m2 = [seconds[step * heads + head] for head in every]
        m3 = [thirds[step * heads + head] for head in every]
        g3 = [-0.25 * tn(z[i], grad[i], HIGHEST) for i in every]
        gz = [0.25 * nt(grad[i], m3[i], HIGHEST) for i in every]
        g2 = [-tn(p[i], g3[i], HIGHEST) for i in every]
        gp = [nt(g3[i], m2[i], HIGHEST) for i in every]
        g1 = [tn(p[i], g2[i], HIGHEST) for i in every]
        gp = [gp[i] + nt(g2[i], 7.0 * eye - p[i], HIGHEST) - g1[i] for i in every]
        total = [total[i] + nt(gp[i], z[i], HIGHEST) for i in every]
        grad = [gz[i] + tn(matrices[i], gp[i], HIGHEST) for i in every]
    for head in every:
        matrix = matrices[head]
        sums = jnp.sum(matrix, axis=0, keepdims=True)
        square = sums * sums
        fourth = square * square
        bound = jnp.sum(fourth * fourth, axis=1, keepdims=True)
        bound = jnp.exp(jnp.log(bound) * 0.125)
        first = inverses[head]
        lost = jnp.sum(grad[head] * first, axis=1, keepdims=True)
        lost = -jnp.sum(lost, axis=0, keepdims=True) / bound
        ratio = sums / bound
        cube = ratio * ratio * ratio
        value = total[head] + grad[head].T / bound + lost * (cube * cube * ratio)
        inner = jnp.sum(value * matrix, axis=1, keepdims=True)
        scores = matrix * (value - inner) * scale
        keys = slice(width + head * LANDMARKS, width + (head + 1) * LANDMARKS)
        land_q = land[:LANDMARKS, columns[head]].astype(jnp.float32)
        land_k = land[:LANDMARKS, keys].astype(jnp.float32)
        out[:, columns[head]] = nn(scores, land_k, HIGHEST)
        out[:, keys] = tn(scores, land_q, HIGHEST)


def far_back_kernel(spot, qkv, land, conv, *refs):
    mixes, grads, near_keys = refs[:4], refs[4:8], refs[8:12]
    keys_out, values_out, parts = refs[12], refs[13], refs[14:18]
    width = qkv.shape[0] // 3
    tok_row = qkv.shape[1] // 4
    head_dim = LANDMARKS
    scale = head_dim ** (-0.5)
    for step in range(4):
        here = tokens_of(spot[0] ^ step, tok_row)
        land_rows = slice(step * LANDMARKS, (step + 1) * LANDMARKS)
        for head in range(width // head_dim):
            cols = slice(head * head_dim, (head + 1) * head_dim)
            keys = qkv[width + head * head_dim : width + (head + 1) * head_dim, here]
            values = qkv[2 * width + head * head_dim : 2 * width + (head + 1) * head_dim, here]
            land_q = land[land_rows, cols]
            log = unpacked_part(mixes[step][:, width:], head)
            inner = unpacked_part(grads[step][:, width:], head)
            probs = jnp.exp(nn(land_q, keys) * scale - log)
            grad = grads[step][:, cols]
            scores = (probs * (nn(grad, values) - inner) * scale).astype(LOW)
            parts[step][:, cols] = nt(scores, keys).astype(LOW)
            keys_out[cols, here] = tn(land_q, scores)
            values_out[cols, here] = (conv[cols, here] + tn(grad, probs.astype(LOW))).astype(LOW)
        parts[step][:, width:] = near_keys[step][...]


def token_grad_kernel(spot, near, far, values, pool, one, two, three, four, out):
    width = near.shape[0]
    tok_row = near.shape[1] // 4
    for step, grads in enumerate((one, two, three, four)):
        row = spot[0] ^ step
        here = tokens_of(row, tok_row)
        share = pool[row]
        out[:width, here] = (near[:, here] + tn(grads[:, :width], share)).astype(LOW)
        out[width : 2 * width, here] = (far[:, here] + tn(grads[:, width:], share)).astype(LOW)
    out[2 * width :, :] = values[...]


def send_rows(pieces):
    got = [exchange(piece, s, h) for piece, (s, h) in zip(pieces[1:], GROUP)]
    return [pieces[0]] + got


def spread_row(row):
    return [row] + [exchange(row, s, h) for s, h in GROUP]


def item_sum(pieces, layout):
    span = layout["span"]
    dtype = pieces[0].dtype
    pieces = [piece.astype(jnp.float32) for piece in send_rows(pieces)]
    total = (pieces[0] + pieces[1]) + (pieces[2] + pieces[3])
    for low, bits in upper_levels():
        sent = total.astype(dtype)
        near = exchange(sent, 2 << low, 0).astype(jnp.float32)
        pair = total + jnp.where(span > 4 << low, near, 0.0)
        if bits == 2:
            far = exchange(sent, 4 << low, 0).astype(jnp.float32)
            cross = exchange(sent, 6 << low, 0).astype(jnp.float32)
            pair = pair + jnp.where(span > 8 << low, far + cross, 0.0)
        total = pair
    return total


def land_mixture(pieces, inverse, layout):
    span = layout["span"]
    width = pieces[0].shape[1] - 128
    pieces = send_rows(pieces)
    flags = jnp.ones((3,), jnp.int32)
    for low, bits in upper_levels():
        call = functools.partial(merge_kernel, len(pieces))
        (row,) = on_core(call, [(pieces[0].shape, jnp.float32)], flags, *pieces)
        pieces = [row] + [exchange(row, m << (low + 1), 0) for m in range(1, 1 << bits)]
        wide = (span > 8 << low).astype(jnp.int32)
        flags = jnp.stack([(span > 4 << low).astype(jnp.int32), wide, wide])
    outs = [(pieces[0].shape, LOW), ((LANDMARKS, width), jnp.float32)]
    call = functools.partial(land_out_kernel, len(pieces))
    return on_core(call, outs, flags, *pieces, inverse)


def item_layout(item_lengths, tok_row, half):
    seq, across, core = place()
    rank = seq * 2 + across
    ends = jnp.cumsum(item_lengths, axis=1)
    starts = ends - item_lengths
    first_token = rank * tok_row
    chosen = (starts <= first_token) & (first_token < ends)
    length = jnp.sum(jnp.where(chosen, item_lengths, 0), axis=1)
    begin = jnp.sum(jnp.where(chosen, starts, 0), axis=1)
    segment = length // LANDMARKS
    first_rank = begin // tok_row
    spans = length // tok_row
    positions = first_token + jnp.arange(tok_row)
    marks = (positions[None, :] - begin[:, None]) // segment[:, None]
    hits = marks[:, None, :] == jnp.arange(LANDMARKS)[None, :, None]
    share = 1.0 / segment.astype(jnp.float32)
    pool = jnp.where(hits, share[:, None, None], 0.0).astype(LOW)
    left_open = rank > first_rank
    right_open = rank + 1 < first_rank + spans
    rims = jnp.repeat(jnp.stack([left_open, right_open]).astype(jnp.float32), half, axis=1)
    me = group_index()
    return dict(
        span=lax.dynamic_index_in_dim(spans, me, 0, keepdims=False),
        pool=pool,
        rims=jnp.pad(rims, ((0, 6), (0, 0))),
        spot=jnp.stack([me, core]).astype(jnp.int32),
    )


def dot(spec, one, two):
    return jnp.einsum(spec, one, two, preferred_element_type=jnp.float32)


def ordered(mine, other, axis):
    across = place()[1]
    low = jnp.where(across == 0, mine, other)
    high = jnp.where(across == 0, other, mine)
    return jnp.stack([low, high], axis=axis)


def fetch_small(query_bias, value_bias, conv_taps, up_bias):
    layers = query_bias.shape[0]
    flat = [a.reshape(layers, -1) for a in (query_bias, value_bias, conv_taps, up_bias)]
    sizes = [a.shape[1] for a in flat]
    packed = jnp.concatenate(flat, axis=1)
    other = exchange(jnp.pad(packed, ((0, 0), (0, -packed.shape[1] % 128))), 0, 2)
    rest, at = [], 0
    for size in sizes:
        rest.append(other[:, at : at + size])
        at += size
    heads = conv_taps.shape[1]
    q_bias = ordered(query_bias, rest[0], 1).reshape(layers, -1)
    v_bias = ordered(value_bias, rest[1], 1).reshape(layers, -1)
    taps = ordered(conv_taps, rest[2].reshape(conv_taps.shape), 1).reshape(layers, 2 * heads, -1)
    return q_bias, v_bias, taps, rest[3]


def fetch_layer(query_weight, key_weight, value_weight, out_weight, up_weight, down_weight):
    mine = jnp.concatenate([query_weight.T, key_weight.T, value_weight.T, out_weight], axis=0)
    other = exchange(mine, 0, 2)
    split = (4, -1, mine.shape[1])
    attn = ordered(mine.reshape(split), other.reshape(split), 1)
    attn = attn.reshape(2 * mine.shape[0], mine.shape[1])
    split_at = attn.shape[0] * 3 // 4
    return dict(
        qkv=attn[:split_at],
        out=attn[split_at:],
        up=[up_weight, exchange(up_weight, 0, 2)],
        down=[down_weight, exchange(down_weight, 0, 2)],
    )


def tap_lines(taps):
    count = taps.shape[1]
    half = (count - 1) // 2
    gap = jnp.zeros((taps.shape[0], 256 - count), jnp.float32)
    flipped = taps[:, ::-1]
    lines = [jnp.concatenate([t[:, half:], gap, t[:, :half]], axis=1) for t in (flipped, taps)]
    pad = -taps.shape[0] % 8
    return [jnp.pad(line, ((0, pad), (0, 0))) for line in lines]


def layer_forward(hidden, params, layout):
    weights = params["weights"]
    spot = layout["spot"]
    batch_rows, piece, model = hidden.shape
    tok_row = 2 * piece
    tokens = batch_rows * tok_row
    width = weights["out"].shape[0]
    half = params["half"]
    quarter = [((LANDMARKS, model // 2), LOW)] * 4
    x_low = hidden.astype(LOW)
    x_full, *pooled = on_core(
        join_pool_kernel,
        [((tokens, model), LOW)] + quarter,
        spot,
        x_low,
        exchange(x_low, 0, 1),
        layout["pool"],
    )
    pooled = jnp.concatenate(spread_row(item_sum(pooled, layout).astype(LOW)), axis=0)
    pooled = pair_join(pooled, 1)
    bias_q, bias_v = params["q_bias"], params["v_bias"]
    no_bias = jnp.zeros_like(bias_q)
    column = jnp.concatenate([bias_q, no_bias, bias_v])[:, None]
    qkv = (nt(weights["qkv"], x_full) + column).astype(LOW)
    land = nt(pooled, weights["qkv"][: 2 * width]) + jnp.concatenate([bias_q, no_bias])
    land = land.astype(LOW)
    heads = width // LANDMARKS
    message = [((LANDMARKS, width + 128), jnp.float32)] * 4
    rim = [((width, batch_rows * half), LOW)] * 2
    *parts, low, high = on_core(
        functools.partial(far_kernel, half), message + rim, spot, qkv, land
    )
    low, high = rank_shift(high, 1), rank_shift(low, -1)
    square = (LANDMARKS, LANDMARKS)
    steps = ((NS_STEPS * heads,) + square, jnp.float32)
    own_land = land[:LANDMARKS]
    chain = on_core(
        inverse_kernel,
        [
            ((heads,) + square, jnp.float32),
            (((NS_STEPS + 1) * heads,) + square, jnp.float32),
            steps,
            steps,
            steps,
        ],
        None,
        own_land,
    )
    inverse = chain[1][NS_STEPS * heads :]
    own_out, weighted = land_mixture(parts, inverse, layout)
    mixes = spread_row(own_out)
    (att_low,) = on_core(
        functools.partial(near_kernel, half),
        [((width, tokens), LOW)],
        spot,
        qkv,
        low,
        high,
        layout["rims"],
        land,
        *mixes,
        params["lines"][0],
    )
    terms = tn(att_low, weights["out"]).reshape(batch_rows, tok_row, model)
    resid_one = hidden + (pair_collect(terms) + params["out_bias"])
    normed = layer_norm(resid_one, params["gain_one"], params["shift_one"])
    h_full = pair_join(normed.astype(LOW), 1).reshape(tokens, model)
    gelu_low, slopes = [], []
    for weight, bias in zip(weights["up"], params["up_bias"]):
        up_pre = nn(h_full, weight) + bias
        area = 0.5 * (1.0 + lax.erf(up_pre * 0.7071067811865476))
        bell = jnp.exp(-0.5 * up_pre * up_pre) * 0.3989422804014327
        gelu_low.append((up_pre * area).astype(LOW))
        slopes.append((area + up_pre * bell).astype(LOW))
    down = weights["down"]
    terms = nn(gelu_low[0], down[0]) + nn(gelu_low[1], down[1])
    mlp_out = pair_collect(terms.reshape(batch_rows, tok_row, model)) + params["down_bias"]
    resid_two = normed + mlp_out
    result = layer_norm(resid_two, params["gain_two"], params["shift_two"])
    kept = dict(
        x_full=x_full,
        qkv=qkv,
        land=land,
        own_land=own_land,
        rims=(low, high),
        chain=chain,
        inverse=inverse,
        weighted=weighted,
        mixes=mixes,
        att_low=att_low,
        resid_one=resid_one,
        h_full=h_full,
        gelu_low=gelu_low,
        slopes=slopes,
        resid_two=resid_two,
    )
    return result, kept


def layer_backward(grad_out, kept, params, layout):
    weights = params["weights"]
    spot = layout["spot"]
    batch_rows, piece, model = grad_out.shape
    tok_row = 2 * piece
    tokens = batch_rows * tok_row
    width = weights["out"].shape[0]
    half = params["half"]
    unused_two, pull_two = jax.vjp(
        layer_norm, kept["resid_two"], params["gain_two"], params["shift_two"]
    )
    grad_two, grad_gain_two, grad_shift_two = pull_two(grad_out)
    grad_mlp = grad_two.astype(LOW)
    grad_down_bias = jnp.sum(grad_mlp.astype(jnp.float32), axis=(0, 1))
    grad_mlp_full = pair_join(grad_mlp, 1).reshape(tokens, model)
    grad_up = [
        (nt(grad_mlp_full, weight) * slope.astype(jnp.float32)).astype(LOW)
        for weight, slope in zip(weights["down"], kept["slopes"])
    ]
    up = weights["up"]
    terms = nt(grad_up[0], up[0]) + nt(grad_up[1], up[1])
    grad_normed = grad_two + pair_collect(terms.reshape(batch_rows, tok_row, model))
    down_sum = reduce_big([tn(g, grad_mlp_full) for g in kept["gelu_low"]])
    up_sum = reduce_big([tn(kept["h_full"], g) for g in grad_up])
    grad_up_bias = [jnp.sum(g.astype(jnp.float32), axis=0) for g in grad_up]
    unused_one, pull_one = jax.vjp(
        layer_norm, kept["resid_one"], params["gain_one"], params["shift_one"]
    )
    grad_one, grad_gain_one, grad_shift_one = pull_one(grad_normed)
    grad_attn = grad_one.astype(LOW)
    grad_out_bias = jnp.sum(grad_attn.astype(jnp.float32), axis=(0, 1))
    grad_attn_full = pair_join(grad_attn, 1).reshape(tokens, model)
    grad_att = nt(weights["out"], grad_attn_full).astype(LOW)
    qkv, land, mixes = kept["qkv"], kept["land"], kept["mixes"]
    row = [((LANDMARKS, width), LOW)]
    rim = [((width, batch_rows * half), LOW)] * 2
    near_queries, *rest = on_core(
        functools.partial(near_back_kernel, half),
        [((width, tokens), jnp.float32)] + row * 8 + rim,
        spot,
        qkv,
        grad_att,
        land,
        *mixes,
    )
    near_outs, near_keys, (low, high) = rest[:4], rest[4:8], rest[8:]
    low, high = rank_shift(high, 1), rank_shift(low, -1)
    own_grad = item_sum(near_outs, layout)
    (own_mix_grad,) = on_core(
        mixture_grad_kernel,
        [((LANDMARKS, width + 128), LOW)],
        None,
        own_grad,
        kept["inverse"],
        kept["weighted"],
    )
    mix_grads = spread_row(own_mix_grad)
    grad_out_weight = nn(kept["att_low"], grad_attn_full)
    out_sum = reduce_big(split_across(grad_out_weight.reshape(1, width, model)))
    conv_grad, tap_grad = on_core(
        functools.partial(conv_back_kernel, half),
        [((width, tokens), jnp.float32), ((8, 128), jnp.float32)],
        None,
        qkv,
        grad_att,
        *kept["rims"],
        low,
        high,
        layout["rims"],
        params["lines"][1],
    )
    far_keys, values_low, *parts = on_core(
        far_back_kernel,
        [((width, tokens), jnp.float32), ((width, tokens), LOW)]
        + [((LANDMARKS, 2 * width), LOW)] * 4,
        spot,
        qkv,
        land,
        conv_grad,
        *mixes,
        *mix_grads,
        *near_keys,
    )
    (own_land_grad,) = on_core(
        inverse_back_kernel,
        [((LANDMARKS, 2 * width), jnp.float32)],
        None,
        own_grad,
        kept["weighted"],
        kept["own_land"],
        *kept["chain"],
    )
    own_land_grad = item_sum(parts, layout) + own_land_grad
    land_grads = spread_row(own_land_grad.astype(LOW))
    (grad_qkv,) = on_core(
        token_grad_kernel,
        [((3 * width, tokens), LOW)],
        spot,
        near_queries,
        far_keys,
        values_low,
        layout["pool"],
        *land_grads,
    )
    terms = tn(grad_qkv, weights["qkv"]).reshape(batch_rows, tok_row, model)
    grad_hidden = grad_one + pair_collect(terms)
    grad_weight = nn(grad_qkv, kept["x_full"]).reshape(3, width, model)
    qkv_sum = reduce_big(split_across(grad_weight))
    grad_bias = jnp.sum(grad_qkv.astype(jnp.float32), axis=1)
    heads = width // LANDMARKS
    mids = [
        split_flat(grad_bias[:width]),
        split_flat(grad_bias[2 * width :]),
        split_flat(tap_grad[:heads, : 2 * half + 1]),
        grad_up_bias,
    ]
    smalls = [
        grad_out_bias,
        grad_down_bias,
        grad_gain_one,
        grad_shift_one,
        grad_gain_two,
        grad_shift_two,
    ]
    return grad_hidden, (qkv_sum, out_sum, up_sum, down_sum), mids, smalls


def split_flat(values):
    across = place()[1]
    half = values.shape[0] // 2
    low, high = values[:half], values[half:]
    return [jnp.where(across == 0, low, high), jnp.where(across == 0, high, low)]


def split_across(values):
    across = place()[1]
    half = values.shape[1] // 2
    model = values.shape[2]
    low = values[:, :half].reshape(-1, model)
    high = values[:, half:].reshape(-1, model)
    return [jnp.where(across == 0, low, high), jnp.where(across == 0, high, low)]


def halve(values, mask):
    side = (lax.axis_index("seq") // mask) % 2
    half = values.shape[0] // 2
    low, high = values[:half], values[half:]
    keep = jnp.where(side == 0, low, high)
    sent = jnp.where(side == 0, high, low)
    return (keep.astype(jnp.float32) + exchange(sent, mask, 0).astype(jnp.float32)).astype(LOW)


def double(values, mask):
    side = (lax.axis_index("seq") // mask) % 2
    other = exchange(values, mask, 0)
    low = jnp.where(side == 0, values, other)
    high = jnp.where(side == 0, other, values)
    return jnp.concatenate([low, high], axis=0)


def reduce_big(pair):
    mine, theirs = pair
    got = exchange(theirs.astype(LOW), 0, 2).astype(jnp.float32)
    total = (mine + got).astype(LOW)
    masks = [1 << i for i in range(lax.axis_size("seq").bit_length() - 1)]
    rows = total.shape[0]
    extra = -rows % (2 * lax.axis_size("seq"))
    if extra:
        total = jnp.pad(total, ((0, extra), (0, 0)))
    middle = total.shape[0] // 2
    done = []
    for part, order in ((total[:middle], masks), (total[middle:], masks[1:] + masks[:1])):
        for mask in order:
            part = halve(part, mask)
        for mask in reversed(order):
            part = double(part, mask)
        done.append(part)
    return jnp.concatenate(done, axis=0)[:rows].astype(jnp.float32)


def seq_sum(values):
    mask = 1
    while mask < lax.axis_size("seq"):
        values = values + exchange(values, mask, 0)
        mask *= 2
    return values


def reduce_small(mid, small):
    mine = jnp.concatenate([m[0].reshape(-1) for m in mid])
    theirs = jnp.concatenate([m[1].reshape(-1) for m in mid])
    every = jnp.concatenate([s.reshape(-1) for s in small])
    count, extra = every.shape[0], mine.shape[0]
    pad = -(count + extra) % 1024
    got = exchange(jnp.pad(jnp.concatenate([every, theirs]), (0, pad)), 0, 2)
    total = jnp.pad(jnp.concatenate([every, mine]), (0, pad)) + got
    total = seq_sum(total)
    every = total[:count]
    every = every + exchange(every, 0, 1)
    mids, at = [], count
    for m in mid:
        mids.append(total[at : at + m[0].size].reshape(m[0].shape))
        at += m[0].size
    smalls, at = [], 0
    for s in small:
        smalls.append(every[at : at + s.size].reshape(s.shape))
        at += s.size
    return mids, smalls


def on_device(
    hidden_in,
    query_weight,
    key_weight,
    value_weight,
    query_bias,
    value_bias,
    out_weight,
    out_bias,
    conv_taps,
    up_weight,
    up_bias,
    down_weight,
    down_bias,
    gain_one,
    shift_one,
    gain_two,
    shift_two,
    out_grad,
    item_lengths,
):
    tok_row = hidden_in.shape[1] * 2
    half = (conv_taps.shape[2] - 1) // 2
    layout = item_layout(item_lengths, tok_row, half)
    q_bias, v_bias, taps, other_up = fetch_small(query_bias, value_bias, conv_taps, up_bias)
    params = []
    for i in range(2):
        params.append(
            dict(
                weights=fetch_layer(
                    query_weight[i],
                    key_weight[i],
                    value_weight[i],
                    out_weight[i],
                    up_weight[i],
                    down_weight[i],
                ),
                half=half,
                q_bias=q_bias[i],
                v_bias=v_bias[i],
                lines=tap_lines(taps[i]),
                up_bias=[up_bias[i], other_up[i]],
                out_bias=out_bias[i],
                down_bias=down_bias[i],
                gain_one=gain_one[i],
                shift_one=shift_one[i],
                gain_two=gain_two[i],
                shift_two=shift_two[i],
            )
        )
    hidden = hidden_in.astype(jnp.float32)
    kept = [None, None]
    for i in range(2):
        hidden, kept[i] = layer_forward(hidden, params[i], layout)
    grad = out_grad
    big, mid, small = [None, None], [None, None], [None, None]
    for i in (1, 0):
        grad, big[i], mid_i, small_i = layer_backward(grad, kept[i], params[i], layout)
        mid[i], small[i] = reduce_small(mid_i, small_i)
    mids = [jnp.stack([one, two]) for one, two in zip(*mid)]
    smalls = [jnp.stack([one, two]) for one, two in zip(*small)]
    width = query_weight.shape[2]
    qkv = jnp.stack([big[0][0], big[1][0]]).reshape(2, 3, width, -1)
    qkv = [jnp.swapaxes(qkv[:, i], 1, 2) for i in range(3)]
    outs, ups, downs = [jnp.stack([big[0][i], big[1][i]]) for i in (1, 2, 3)]
    return (
        hidden.astype(LOW),
        grad,
        qkv[0],
        qkv[1],
        qkv[2],
        mids[0],
        mids[1],
        outs,
        smalls[0],
        mids[2].reshape(conv_taps.shape),
        ups,
        mids[3],
        downs,
        smalls[1],
        smalls[2],
        smalls[3],
        smalls[4],
        smalls[5],
    )


def solution(mesh):
    placed = (
        P(None, ("seq", "head"), None),
        P(None, None, "head"),
        P(None, None, "head"),
        P(None, None, "head"),
        P(None, "head"),
        P(None, "head"),
        P(None, "head", None),
        P(),
        P(None, "head", None),
        P(None, None, "head"),
        P(None, "head"),
        P(None, "head", None),
        P(),
        P(),
        P(),
        P(),
        P(),
        P(None, ("seq", "head"), None),
        P(),
    )
    return jax.shard_map(
        on_device,
        mesh=mesh,
        in_specs=placed,
        out_specs=(
            P(None, ("seq", "head"), None),
            P(None, ("seq", "head"), None),
            P(None, None, "head"),
            P(None, None, "head"),
            P(None, None, "head"),
            P(None, "head"),
            P(None, "head"),
            P(None, "head", None),
            P(),
            P(None, "head", None),
            P(None, None, "head"),
            P(None, "head"),
            P(None, "head", None),
            P(),
            P(),
            P(),
            P(),
            P(),
        ),
        check_vma=False,
    )
```

```python
import functools

import jax
import jax.numpy as jnp
from jax import lax
from jax.experimental import pallas as pl
from jax.experimental.pallas import tpu as pltpu
from jax.sharding import PartitionSpec as P

LANDMARKS = 64
NS_STEPS = 6


HIGHEST = lax.Precision.HIGHEST
EPSILON = 1e-05
FLOOR_TOP = -1e30
LOW = jnp.bfloat16
GROUP = ((0, 2), (1, 0), (1, 2))


def layer_norm(values, gain, offset):
    centred = values - jnp.mean(values, axis=-1, keepdims=True)
    variance = jnp.mean(centred * centred, axis=-1, keepdims=True)
    return centred * lax.rsqrt(variance + EPSILON) * gain + offset


def exchange(values, seq_mask, head_mask):
    if seq_mask == 0:
        count = lax.axis_size("head")
        return lax.ppermute(values, "head", [(i, i ^ head_mask) for i in range(count)])
    if head_mask == 0:
        count = lax.axis_size("seq")
        return lax.ppermute(values, "seq", [(i, i ^ seq_mask) for i in range(count)])
    heads = lax.axis_size("head")
    route = []
    for s in range(lax.axis_size("seq")):
        for h in range(heads):
            route.append((s * heads + h, (s ^ seq_mask) * heads + (h ^ head_mask)))
    return lax.ppermute(values, ("seq", "head"), route)


def rank_shift(values, step):
    heads = lax.axis_size("head")
    ranks = lax.axis_size("seq") * (heads // 2)
    route = []
    for rank in range(ranks):
        target = rank + step
        if 0 <= target < ranks:
            for core in range(2):
                source_dev = (rank // 2) * heads + (rank % 2) * 2 + core
                target_dev = (target // 2) * heads + (target % 2) * 2 + core
                route.append((source_dev, target_dev))
    return lax.ppermute(values, ("seq", "head"), route)


def place():
    seq = lax.axis_index("seq")
    head = lax.axis_index("head")
    return seq, head // 2, head % 2


def pair_join(values, axis):
    core = place()[2]
    other = exchange(values, 0, 1)
    low = jnp.where(core == 0, values, other)
    high = jnp.where(core == 0, other, values)
    return jnp.concatenate([low, high], axis=axis)


def pair_collect(terms):
    core = place()[2]
    half = terms.shape[1] // 2
    low, high = terms[:, :half], terms[:, half:]
    mine = jnp.where(core == 0, low, high)
    theirs = jnp.where(core == 0, high, low).astype(jnp.bfloat16)
    return mine + exchange(theirs, 0, 1).astype(jnp.float32)


def group_index():
    seq, across, core = place()
    return across + 2 * (seq % 2)


def upper_levels():
    levels = (lax.axis_size("seq") // 2).bit_length() - 1
    return [(low, min(2, levels - low)) for low in range(0, levels, 2)]


def nn(one, two, precision=None):
    return lax.dot_general(
        one, two, (((1,), (0,)), ((), ())), precision, preferred_element_type=jnp.float32
    )


def nt(one, two, precision=None):
    return lax.dot_general(
        one, two, (((1,), (1,)), ((), ())), precision, preferred_element_type=jnp.float32
    )


def tn(one, two, precision=None):
    return lax.dot_general(
        one, two, (((0,), (0,)), ((), ())), precision, preferred_element_type=jnp.float32
    )


def on_core(kernel, outs, scalars, *arrays):
    shapes = tuple(jax.ShapeDtypeStruct(shape, dtype) for shape, dtype in outs)
    specs = [pl.BlockSpec(memory_space=pltpu.SMEM)] if scalars is not None else []
    specs += [pl.BlockSpec(memory_space=pltpu.VMEM)] * len(arrays)
    given = ((scalars,) if scalars is not None else ()) + arrays
    return pl.pallas_call(
        kernel,
        out_shape=shapes,
        in_specs=specs,
        out_specs=tuple(pl.BlockSpec(memory_space=pltpu.VMEM) for _ in outs),
        compiler_params=pltpu.CompilerParams(vmem_limit_bytes=48 * 1024 * 1024),
    )(*given)


def tokens_of(row, tok_row):
    return pl.ds(pl.multiple_of(row * tok_row, tok_row), tok_row)


def lanes(shape):
    return lax.broadcasted_iota(jnp.int32, shape, len(shape) - 1)


def join_pool_kernel(spot, own, other, pool, full, one, two, three, four):
    rows, piece, model = own.shape
    tok_row = 2 * piece
    core = spot[1]
    half = model // 2
    for row in range(rows):
        mine = pl.multiple_of(row * tok_row + core * piece, piece)
        theirs = pl.multiple_of(row * tok_row + (1 - core) * piece, piece)
        full[pl.ds(mine, piece), :] = own[row]
        full[pl.ds(theirs, piece), :] = other[row]
    side = pl.ds(pl.multiple_of(core * half, half), half)
    for step, out in enumerate((one, two, three, four)):
        row = spot[0] ^ step
        block = full[tokens_of(row, tok_row), side]
        out[...] = nn(pool[row], block).astype(LOW)


def rim_blocks(block_of, rows, tok_row, half):
    low, high = None, None
    for row in range(rows):
        block = block_of(row).astype(jnp.float32)
        lane = lanes(block.shape)
        first = block if row == 0 else pltpu.roll(block, row * half, 1)
        shift = (row * half + half) % tok_row
        last = block if shift == 0 else pltpu.roll(block, shift, 1)
        inside = lane // half == row
        low = jnp.where(inside, first, 0.0 if low is None else low)
        high = jnp.where(inside, last, 0.0 if high is None else high)
    return low.astype(LOW), high.astype(LOW)


def far_kernel(half, spot, qkv, land, one, two, three, four, low, high):
    width = qkv.shape[0] // 3
    head_dim = LANDMARKS
    heads = width // head_dim
    tok_row = qkv.shape[1] // 4
    scale = head_dim ** (-0.5)
    for step, out in enumerate((one, two, three, four)):
        here = tokens_of(spot[0] ^ step, tok_row)
        logs = jnp.zeros((LANDMARKS, out.shape[1] - width), jnp.float32)
        lane = lanes(logs.shape)
        for head in range(heads):
            cols = slice(head * head_dim, (head + 1) * head_dim)
            keys = qkv[width + head * head_dim : width + (head + 1) * head_dim, here]
            values = qkv[2 * width + head * head_dim : 2 * width + (head + 1) * head_dim, here]
            land_q = land[step * LANDMARKS : (step + 1) * LANDMARKS, cols]
            scores = nn(land_q, keys) * scale
            top = jnp.max(scores, axis=1, keepdims=True)
            grown = jnp.exp(scores - top)
            total = jnp.sum(grown, axis=1, keepdims=True)
            out[:, cols] = nt(grown.astype(LOW), values) / total
            logs = jnp.where(lane == head, top + jnp.log(total), logs)
        out[:, width:] = logs
    low[...], high[...] = rim_blocks(
        lambda row: qkv[2 * width :, row * tok_row : (row + 1) * tok_row], 4, tok_row, half
    )


def merged(flags, pieces, width):
    head_dim = LANDMARKS
    mixes, logs = [], []
    for head in range(width // head_dim):
        cols = slice(head * head_dim, (head + 1) * head_dim)
        column = slice(width + head, width + head + 1)
        log = [pieces[0][:, column]]
        for index, piece in enumerate(pieces[1:]):
            log.append(jnp.where(flags[index] > 0, piece[:, column], FLOOR_TOP))
        top = functools.reduce(jnp.maximum, log)
        shares = [jnp.exp(value - top) for value in log]
        total = functools.reduce(jnp.add, shares)
        mix = sum(share * piece[:, cols] for share, piece in zip(shares, pieces))
        mixes.append(mix / total)
        logs.append(top + jnp.log(total))
    return mixes, logs


def merge_kernel(count, flags, *refs):
    out = refs[count]
    width = out.shape[1] - 128
    mixes, logs = merged(flags, refs[:count], width)
    packed = jnp.zeros((LANDMARKS, 128), jnp.float32)
    lane = lanes(packed.shape)
    for head, (mix, log) in enumerate(zip(mixes, logs)):
        out[:, head * LANDMARKS : (head + 1) * LANDMARKS] = mix
        packed = jnp.where(lane == head, log, packed)
    out[:, width:] = packed


def packed_parts(columns):
    packed = jnp.zeros((LANDMARKS, 128), jnp.float32)
    lane = lanes(packed.shape)
    for head, column in enumerate(columns):
        for part in range(3):
            rounded = column.astype(LOW).astype(jnp.float32)
            packed = jnp.where(lane == head + 8 * part, rounded, packed)
            column = column - rounded
    return packed.astype(LOW)


def unpacked_part(packed, head):
    packed = packed.astype(jnp.float32)
    return (
        packed[:, head : head + 1]
        + packed[:, head + 8 : head + 9]
        + packed[:, head + 16 : head + 17]
    )


def land_out_kernel(count, flags, *refs):
    inverse, out, weighted = refs[count:]
    width = weighted.shape[1]
    mixes, logs = merged(flags, refs[:count], width)
    for head, mix in enumerate(mixes):
        cols = slice(head * LANDMARKS, (head + 1) * LANDMARKS)
        weighted[:, cols] = mix
        out[:, cols] = nn(inverse[head], mix, HIGHEST).astype(LOW)
    out[:, width:] = packed_parts(logs)


def inverse_kernel(land, amats, inverses, products, seconds, thirds):
    width = land.shape[1] // 2
    heads = width // LANDMARKS
    scale = LANDMARKS ** (-0.5)
    shape = (LANDMARKS, LANDMARKS)
    rows = lax.broadcasted_iota(jnp.int32, shape, 0)
    eye = (rows == lanes(shape)).astype(jnp.float32)
    matrices, iterates = [], []
    for head in range(heads):
        cols = slice(head * LANDMARKS, (head + 1) * LANDMARKS)
        keys = slice(width + head * LANDMARKS, width + (head + 1) * LANDMARKS)
        scores = nt(land[:LANDMARKS, cols], land[:LANDMARKS, keys]) * scale
        grown = jnp.exp(scores - jnp.max(scores, axis=1, keepdims=True))
        matrix = grown / jnp.sum(grown, axis=1, keepdims=True)
        columns = jnp.sum(matrix, axis=0, keepdims=True)
        square = columns * columns
        fourth = square * square
        bound = jnp.sum(fourth * fourth, axis=1, keepdims=True)
        bound = jnp.exp(jnp.log(bound) * 0.125)
        amats[head] = matrix
        matrices.append(matrix)
        iterates.append(matrix.T / bound)
    for step in range(NS_STEPS):
        product = [nn(a, z, HIGHEST) for a, z in zip(matrices, iterates)]
        inner = [nn(p, 7.0 * eye - p, HIGHEST) for p in product]
        second = [15.0 * eye - value for value in inner]
        third = [13.0 * eye - nn(p, m, HIGHEST) for p, m in zip(product, second)]
        for head in range(heads):
            inverses[step * heads + head] = iterates[head]
            products[step * heads + head] = product[head]
            seconds[step * heads + head] = second[head]
            thirds[step * heads + head] = third[head]
        iterates = [0.25 * nn(z, m, HIGHEST) for z, m in zip(iterates, third)]
    for head in range(heads):
        inverses[NS_STEPS * heads + head] = iterates[head]


def band_blocks(line, tok_row, half):
    span = line.shape[1]
    wide = jnp.broadcast_to(line, (tok_row, span))
    middle = pltpu.roll(wide, 0, 1, stride=1, stride_axis=0)[:, :tok_row]
    short = jnp.broadcast_to(line, (half, span))
    low = pltpu.roll(short, span - half, 1, stride=1, stride_axis=0)[:, :tok_row]
    high = pltpu.roll(short, tok_row, 1, stride=1, stride_axis=0)[:, :tok_row]
    reps = tok_row // half
    return [
        part.astype(LOW)
        for part in (middle, jnp.concatenate([low] * reps, 0), jnp.concatenate([high] * reps, 0))
    ]


def near_kernel(half, spot, qkv, low, high, rims, land, one, two, three, four, line, out):
    width = qkv.shape[0] // 3
    tok_row = qkv.shape[1] // 4
    head_dim = LANDMARKS
    scale = head_dim ** (-0.5)
    low_all = low[...].astype(jnp.float32) * rims[0:1, :]
    high_all = high[...].astype(jnp.float32) * rims[1:2, :]
    lane = lanes((head_dim, tok_row)) // half
    bands = [band_blocks(line[h : h + 1, :], tok_row, half) for h in range(width // head_dim)]
    for step, mixed in enumerate((one, two, three, four)):
        row = spot[0] ^ step
        here = tokens_of(row, tok_row)
        land_rows = slice(step * LANDMARKS, (step + 1) * LANDMARKS)
        for head in range(width // head_dim):
            cols = slice(head * head_dim, (head + 1) * head_dim)
            keys = slice(width + head * head_dim, width + (head + 1) * head_dim)
            queries = qkv[cols, here]
            scores = nn(land[land_rows, keys], queries) * scale
            grown = jnp.exp(scores - jnp.max(scores, axis=0, keepdims=True))
            probs = grown / jnp.sum(grown, axis=0, keepdims=True)
            total = tn(mixed[:, cols], probs.astype(LOW))
            values = qkv[2 * width + head * head_dim : 2 * width + (head + 1) * head_dim, here]
            total = total + nn(values, bands[head][0])
            mine = lane == row
            total = total + nn(jnp.where(mine, low_all[cols, :], 0.0).astype(LOW), bands[head][1])
            total = total + nn(jnp.where(mine, high_all[cols, :], 0.0).astype(LOW), bands[head][2])
            out[cols, here] = total.astype(LOW)


def near_back_kernel(half, spot, qkv, grads, land, *refs):
    mixes, queries_out = refs[:4], refs[4]
    land_outs, land_keys, low, high = refs[5:9], refs[9:13], refs[13], refs[14]
    width = qkv.shape[0] // 3
    tok_row = qkv.shape[1] // 4
    head_dim = LANDMARKS
    scale = head_dim ** (-0.5)
    for step in range(4):
        here = tokens_of(spot[0] ^ step, tok_row)
        land_rows = slice(step * LANDMARKS, (step + 1) * LANDMARKS)
        for head in range(width // head_dim):
            cols = slice(head * head_dim, (head + 1) * head_dim)
            keys = slice(width + head * head_dim, width + (head + 1) * head_dim)
            queries = qkv[cols, here]
            land_k = land[land_rows, keys]
            scores = nn(land_k, queries) * scale
            grown = jnp.exp(scores - jnp.max(scores, axis=0, keepdims=True))
            probs = grown / jnp.sum(grown, axis=0, keepdims=True)
            grad = grads[cols, here]
            grad_probs = nn(mixes[step][:, cols], grad)
            inner = jnp.sum(grad_probs * probs, axis=0, keepdims=True)
            grad_scores = (probs * (grad_probs - inner) * scale).astype(LOW)
            queries_out[cols, here] = tn(land_k, grad_scores)
            land_keys[step][:, cols] = nt(grad_scores, queries).astype(LOW)
            land_outs[step][:, cols] = nt(probs.astype(LOW), grad).astype(LOW)
    low[...], high[...] = rim_blocks(
        lambda row: grads[:, row * tok_row : (row + 1) * tok_row], 4, tok_row, half
    )


def conv_back_kernel(half, qkv, grads, low, high, grad_low, grad_high, rims, line, out, taps):
    width = qkv.shape[0] // 3
    tok_row = qkv.shape[1] // 4
    head_dim = LANDMARKS
    span = line.shape[1]
    low_all = low[...].astype(jnp.float32) * rims[0:1, :]
    high_all = high[...].astype(jnp.float32) * rims[1:2, :]
    grad_low_all = grad_low[...].astype(jnp.float32) * rims[0:1, :]
    grad_high_all = grad_high[...].astype(jnp.float32) * rims[1:2, :]
    lane = lanes((head_dim, tok_row)) // half
    square = (tok_row, tok_row)
    turned = (lax.broadcasted_iota(jnp.int32, square, 0) + lanes(square) == tok_row - 1).astype(LOW)
    wide = lanes((tok_row, span))
    for head in range(width // head_dim):
        cols = slice(head * head_dim, (head + 1) * head_dim)
        bands = band_blocks(line[head : head + 1, :], tok_row, half)
        fields = [jnp.zeros(square, jnp.float32) for _ in range(3)]
        for row in range(4):
            here = slice(row * tok_row, (row + 1) * tok_row)
            mine = lane == row

            def rim(block):
                return jnp.where(mine, block[cols, :], 0.0).astype(LOW)

            grad = grads[cols, here]
            values = qkv[2 * width + head * head_dim : 2 * width + (head + 1) * head_dim, here]
            total = nn(grad, bands[0]) + nn(rim(grad_low_all), bands[1])
            out[cols, here] = total + nn(rim(grad_high_all), bands[2])
            backward = nn(grad, turned).astype(LOW)
            for index, block in enumerate((values, rim(low_all), rim(high_all))):
                fields[index] = fields[index] + tn(backward, block)
        ends = []
        for field in fields[1:]:
            folded = field + pltpu.roll(field, 2 * half, 1)
            folded = folded + pltpu.roll(folded, half, 1)
            ends.append(jnp.concatenate([folded, folded], axis=1))
        whole = jnp.concatenate([fields[0], jnp.zeros(square, jnp.float32)], axis=1)
        whole = pltpu.roll(whole, half, 1)
        whole = jnp.where(wide < half, ends[0], whole)
        right = (wide >= half + tok_row) & (wide < 2 * half + tok_row)
        whole = jnp.where(right, ends[1], whole)
        whole = pltpu.roll(whole, span - tok_row + 1, 1, stride=1, stride_axis=0)
        taps[head : head + 1, :] = jnp.sum(whole, axis=0, keepdims=True)[:, :128]


def mixture_grad_kernel(grads, inverse, weighted, out):
    width = grads.shape[1]
    inner = []
    for head in range(width // LANDMARKS):
        cols = slice(head * LANDMARKS, (head + 1) * LANDMARKS)
        value = tn(inverse[head], grads[:, cols], HIGHEST).astype(LOW)
        out[:, cols] = value
        product = value.astype(jnp.float32) * weighted[:, cols]
        inner.append(jnp.sum(product, axis=1, keepdims=True))
    out[:, width:] = packed_parts(inner)


def inverse_back_kernel(
    grads, weighted, land, amats, inverses, products, seconds, thirds, out
):
    width = grads.shape[1]
    heads = width // LANDMARKS
    scale = LANDMARKS ** (-0.5)
    shape = (LANDMARKS, LANDMARKS)
    rows = lax.broadcasted_iota(jnp.int32, shape, 0)
    eye = (rows == lanes(shape)).astype(jnp.float32)
    every = range(heads)
    columns = [slice(head * LANDMARKS, (head + 1) * LANDMARKS) for head in every]
    grad = [nt(grads[:, c], weighted[:, c], HIGHEST) for c in columns]
    matrices = [amats[head] for head in every]
    total = [jnp.zeros(shape, jnp.float32) for _ in every]
    for step in reversed(range(NS_STEPS)):
        z = [inverses[step * heads + head] for head in every]
        p = [products[step * heads + head] for head in every]
        m2 = [seconds[step * heads + head] for head in every]
        m3 = [thirds[step * heads + head] for head in every]
        g3 = [-0.25 * tn(z[i], grad[i], HIGHEST) for i in every]
        gz = [0.25 * nt(grad[i], m3[i], HIGHEST) for i in every]
        g2 = [-tn(p[i], g3[i], HIGHEST) for i in every]
        gp = [nt(g3[i], m2[i], HIGHEST) for i in every]
        g1 = [tn(p[i], g2[i], HIGHEST) for i in every]
        gp = [gp[i] + nt(g2[i], 7.0 * eye - p[i], HIGHEST) - g1[i] for i in every]
        total = [total[i] + nt(gp[i], z[i], HIGHEST) for i in every]
        grad = [gz[i] + tn(matrices[i], gp[i], HIGHEST) for i in every]
    for head in every:
        matrix = matrices[head]
        sums = jnp.sum(matrix, axis=0, keepdims=True)
        square = sums * sums
        fourth = square * square
        bound = jnp.sum(fourth * fourth, axis=1, keepdims=True)
        bound = jnp.exp(jnp.log(bound) * 0.125)
        first = inverses[head]
        lost = jnp.sum(grad[head] * first, axis=1, keepdims=True)
        lost = -jnp.sum(lost, axis=0, keepdims=True) / bound
        ratio = sums / bound
        cube = ratio * ratio * ratio
        value = total[head] + grad[head].T / bound + lost * (cube * cube * ratio)
        inner = jnp.sum(value * matrix, axis=1, keepdims=True)
        scores = matrix * (value - inner) * scale
        keys = slice(width + head * LANDMARKS, width + (head + 1) * LANDMARKS)
        land_q = land[:LANDMARKS, columns[head]].astype(jnp.float32)
        land_k = land[:LANDMARKS, keys].astype(jnp.float32)
        out[:, columns[head]] = nn(scores, land_k, HIGHEST)
        out[:, keys] = tn(scores, land_q, HIGHEST)


def far_back_kernel(spot, qkv, land, conv, *refs):
    mixes, grads, near_keys = refs[:4], refs[4:8], refs[8:12]
    keys_out, values_out, parts = refs[12], refs[13], refs[14:18]
    width = qkv.shape[0] // 3
    tok_row = qkv.shape[1] // 4
    head_dim = LANDMARKS
    scale = head_dim ** (-0.5)
    for step in range(4):
        here = tokens_of(spot[0] ^ step, tok_row)
        land_rows = slice(step * LANDMARKS, (step + 1) * LANDMARKS)
        for head in range(width // head_dim):
            cols = slice(head * head_dim, (head + 1) * head_dim)
            keys = qkv[width + head * head_dim : width + (head + 1) * head_dim, here]
            values = qkv[2 * width + head * head_dim : 2 * width + (head + 1) * head_dim, here]
            land_q = land[land_rows, cols]
            log = unpacked_part(mixes[step][:, width:], head)
            inner = unpacked_part(grads[step][:, width:], head)
            probs = jnp.exp(nn(land_q, keys) * scale - log)
            grad = grads[step][:, cols]
            scores = (probs * (nn(grad, values) - inner) * scale).astype(LOW)
            parts[step][:, cols] = nt(scores, keys).astype(LOW)
            keys_out[cols, here] = tn(land_q, scores)
            values_out[cols, here] = (conv[cols, here] + tn(grad, probs.astype(LOW))).astype(LOW)
        parts[step][:, width:] = near_keys[step][...]


def token_grad_kernel(spot, near, far, values, pool, one, two, three, four, out):
    width = near.shape[0]
    tok_row = near.shape[1] // 4
    for step, grads in enumerate((one, two, three, four)):
        row = spot[0] ^ step
        here = tokens_of(row, tok_row)
        share = pool[row]
        out[:width, here] = (near[:, here] + tn(grads[:, :width], share)).astype(LOW)
        out[width : 2 * width, here] = (far[:, here] + tn(grads[:, width:], share)).astype(LOW)
    out[2 * width :, :] = values[...]


def send_rows(pieces):
    got = [exchange(piece, s, h) for piece, (s, h) in zip(pieces[1:], GROUP)]
    return [pieces[0]] + got


def spread_row(row):
    return [row] + [exchange(row, s, h) for s, h in GROUP]


def item_sum(pieces, layout):
    span = layout["span"]
    dtype = pieces[0].dtype
    pieces = [piece.astype(jnp.float32) for piece in send_rows(pieces)]
    total = (pieces[0] + pieces[1]) + (pieces[2] + pieces[3])
    for low, bits in upper_levels():
        sent = total.astype(dtype)
        near = exchange(sent, 2 << low, 0).astype(jnp.float32)
        pair = total + jnp.where(span > 4 << low, near, 0.0)
        if bits == 2:
            far = exchange(sent, 4 << low, 0).astype(jnp.float32)
            cross = exchange(sent, 6 << low, 0).astype(jnp.float32)
            pair = pair + jnp.where(span > 8 << low, far + cross, 0.0)
        total = pair
    return total


def land_mixture(pieces, inverse, layout):
    span = layout["span"]
    width = pieces[0].shape[1] - 128
    pieces = send_rows(pieces)
    flags = jnp.ones((3,), jnp.int32)
    for low, bits in upper_levels():
        call = functools.partial(merge_kernel, len(pieces))
        (row,) = on_core(call, [(pieces[0].shape, jnp.float32)], flags, *pieces)
        pieces = [row] + [exchange(row, m << (low + 1), 0) for m in range(1, 1 << bits)]
        wide = (span > 8 << low).astype(jnp.int32)
        flags = jnp.stack([(span > 4 << low).astype(jnp.int32), wide, wide])
    outs = [(pieces[0].shape, LOW), ((LANDMARKS, width), jnp.float32)]
    call = functools.partial(land_out_kernel, len(pieces))
    return on_core(call, outs, flags, *pieces, inverse)


def item_layout(item_lengths, tok_row, half):
    seq, across, core = place()
    rank = seq * 2 + across
    ends = jnp.cumsum(item_lengths, axis=1)
    starts = ends - item_lengths
    first_token = rank * tok_row
    chosen = (starts <= first_token) & (first_token < ends)
    length = jnp.sum(jnp.where(chosen, item_lengths, 0), axis=1)
    begin = jnp.sum(jnp.where(chosen, starts, 0), axis=1)
    segment = length // LANDMARKS
    first_rank = begin // tok_row
    spans = length // tok_row
    positions = first_token + jnp.arange(tok_row)
    marks = (positions[None, :] - begin[:, None]) // segment[:, None]
    hits = marks[:, None, :] == jnp.arange(LANDMARKS)[None, :, None]
    share = 1.0 / segment.astype(jnp.float32)
    pool = jnp.where(hits, share[:, None, None], 0.0).astype(LOW)
    left_open = rank > first_rank
    right_open = rank + 1 < first_rank + spans
    rims = jnp.repeat(jnp.stack([left_open, right_open]).astype(jnp.float32), half, axis=1)
    me = group_index()
    return dict(
        span=lax.dynamic_index_in_dim(spans, me, 0, keepdims=False),
        pool=pool,
        rims=jnp.pad(rims, ((0, 6), (0, 0))),
        spot=jnp.stack([me, core]).astype(jnp.int32),
    )


def dot(spec, one, two):
    return jnp.einsum(spec, one, two, preferred_element_type=jnp.float32)


def ordered(mine, other, axis):
    across = place()[1]
    low = jnp.where(across == 0, mine, other)
    high = jnp.where(across == 0, other, mine)
    return jnp.stack([low, high], axis=axis)


def fetch_small(query_bias, value_bias, conv_taps, up_bias):
    layers = query_bias.shape[0]
    flat = [a.reshape(layers, -1) for a in (query_bias, value_bias, conv_taps, up_bias)]
    sizes = [a.shape[1] for a in flat]
    packed = jnp.concatenate(flat, axis=1)
    other = exchange(jnp.pad(packed, ((0, 0), (0, -packed.shape[1] % 128))), 0, 2)
    rest, at = [], 0
    for size in sizes:
        rest.append(other[:, at : at + size])
        at += size
    heads = conv_taps.shape[1]
    q_bias = ordered(query_bias, rest[0], 1).reshape(layers, -1)
    v_bias = ordered(value_bias, rest[1], 1).reshape(layers, -1)
    taps = ordered(conv_taps, rest[2].reshape(conv_taps.shape), 1).reshape(layers, 2 * heads, -1)
    return q_bias, v_bias, taps, ordered(up_bias, rest[3], 1)


def across_gather(values):
    return lax.all_gather(values, "head", axis=0, axis_index_groups=[[0, 2], [1, 3]])


def fetch_layer(query_weight, key_weight, value_weight, out_weight, up_weight, down_weight):
    mine = jnp.concatenate([query_weight.T, key_weight.T, value_weight.T, out_weight], axis=0)
    other = exchange(mine, 0, 2)
    split = (4, -1, mine.shape[1])
    attn = ordered(mine.reshape(split), other.reshape(split), 1)
    attn = attn.reshape(2 * mine.shape[0], mine.shape[1])
    split_at = attn.shape[0] * 3 // 4
    ffn = across_gather(jnp.concatenate([up_weight, down_weight], axis=0))
    return dict(
        qkv=attn[:split_at],
        out=attn[split_at:],
        up=ffn[:, : up_weight.shape[0]],
        down=ffn[:, up_weight.shape[0] :],
    )


def tap_lines(taps):
    count = taps.shape[1]
    half = (count - 1) // 2
    gap = jnp.zeros((taps.shape[0], 256 - count), jnp.float32)
    flipped = taps[:, ::-1]
    lines = [jnp.concatenate([t[:, half:], gap, t[:, :half]], axis=1) for t in (flipped, taps)]
    pad = -taps.shape[0] % 8
    return [jnp.pad(line, ((0, pad), (0, 0))) for line in lines]


def layer_forward(hidden, params, layout):
    weights = params["weights"]
    spot = layout["spot"]
    batch_rows, piece, model = hidden.shape
    tok_row = 2 * piece
    tokens = batch_rows * tok_row
    width = weights["out"].shape[0]
    half = params["half"]
    quarter = [((LANDMARKS, model // 2), LOW)] * 4
    x_low = hidden.astype(LOW)
    x_full, *pooled = on_core(
        join_pool_kernel,
        [((tokens, model), LOW)] + quarter,
        spot,
        x_low,
        exchange(x_low, 0, 1),
        layout["pool"],
    )
    pooled = jnp.concatenate(spread_row(item_sum(pooled, layout).astype(LOW)), axis=0)
    pooled = pair_join(pooled, 1)
    bias_q, bias_v = params["q_bias"], params["v_bias"]
    no_bias = jnp.zeros_like(bias_q)
    column = jnp.concatenate([bias_q, no_bias, bias_v])[:, None]
    qkv = (nt(weights["qkv"], x_full) + column).astype(LOW)
    land = nt(pooled, weights["qkv"][: 2 * width]) + jnp.concatenate([bias_q, no_bias])
    land = land.astype(LOW)
    heads = width // LANDMARKS
    message = [((LANDMARKS, width + 128), jnp.float32)] * 4
    rim = [((width, batch_rows * half), LOW)] * 2
    *parts, low, high = on_core(
        functools.partial(far_kernel, half), message + rim, spot, qkv, land
    )
    low, high = rank_shift(high, 1), rank_shift(low, -1)
    square = (LANDMARKS, LANDMARKS)
    steps = ((NS_STEPS * heads,) + square, jnp.float32)
    own_land = land[:LANDMARKS]
    chain = on_core(
        inverse_kernel,
        [
            ((heads,) + square, jnp.float32),
            (((NS_STEPS + 1) * heads,) + square, jnp.float32),
            steps,
            steps,
            steps,
        ],
        None,
        own_land,
    )
    inverse = chain[1][NS_STEPS * heads :]
    own_out, weighted = land_mixture(parts, inverse, layout)
    mixes = spread_row(own_out)
    (att_low,) = on_core(
        functools.partial(near_kernel, half),
        [((width, tokens), LOW)],
        spot,
        qkv,
        low,
        high,
        layout["rims"],
        land,
        *mixes,
        params["lines"][0],
    )
    terms = tn(att_low, weights["out"]).reshape(batch_rows, tok_row, model)
    resid_one = hidden + (pair_collect(terms) + params["out_bias"])
    normed = layer_norm(resid_one, params["gain_one"], params["shift_one"])
    h_full = pair_join(normed.astype(LOW), 1).reshape(tokens, model)
    up_pre = dot("td,gdf->gtf", h_full, weights["up"]) + params["up_bias"][:, None, :]
    area = 0.5 * (1.0 + lax.erf(up_pre * 0.7071067811865476))
    bell = jnp.exp(-0.5 * up_pre * up_pre) * 0.3989422804014327
    gelu_low = (up_pre * area).astype(LOW)
    slopes = (area + up_pre * bell).astype(LOW)
    terms = dot("gtf,gfd->td", gelu_low, weights["down"])
    mlp_out = pair_collect(terms.reshape(batch_rows, tok_row, model)) + params["down_bias"]
    resid_two = normed + mlp_out
    result = layer_norm(resid_two, params["gain_two"], params["shift_two"])
    kept = dict(
        x_full=x_full,
        qkv=qkv,
        land=land,
        own_land=own_land,
        rims=(low, high),
        chain=chain,
        inverse=inverse,
        weighted=weighted,
        mixes=mixes,
        att_low=att_low,
        resid_one=resid_one,
        h_full=h_full,
        gelu_low=gelu_low,
        slopes=slopes,
        resid_two=resid_two,
    )
    return result, kept


def layer_backward(grad_out, kept, params, layout):
    weights = params["weights"]
    spot = layout["spot"]
    batch_rows, piece, model = grad_out.shape
    tok_row = 2 * piece
    tokens = batch_rows * tok_row
    width = weights["out"].shape[0]
    half = params["half"]
    unused_two, pull_two = jax.vjp(
        layer_norm, kept["resid_two"], params["gain_two"], params["shift_two"]
    )
    grad_two, grad_gain_two, grad_shift_two = pull_two(grad_out)
    grad_mlp = grad_two.astype(LOW)
    grad_down_bias = jnp.sum(grad_mlp.astype(jnp.float32), axis=(0, 1))
    grad_mlp_full = pair_join(grad_mlp, 1).reshape(tokens, model)
    grad_up = dot("td,gfd->gtf", grad_mlp_full, weights["down"])
    grad_up = (grad_up * kept["slopes"].astype(jnp.float32)).astype(LOW)
    terms = dot("gtf,gdf->td", grad_up, weights["up"])
    grad_normed = grad_two + pair_collect(terms.reshape(batch_rows, tok_row, model))
    down_grad = across_sum(sides(dot("gtf,td->gfd", kept["gelu_low"], grad_mlp_full)))
    up_grad = across_sum(sides(dot("td,gtf->gdf", kept["h_full"], grad_up)))
    grad_up_bias = sides(jnp.sum(grad_up.astype(jnp.float32), axis=1))
    unused_one, pull_one = jax.vjp(
        layer_norm, kept["resid_one"], params["gain_one"], params["shift_one"]
    )
    grad_one, grad_gain_one, grad_shift_one = pull_one(grad_normed)
    grad_attn = grad_one.astype(LOW)
    grad_out_bias = jnp.sum(grad_attn.astype(jnp.float32), axis=(0, 1))
    grad_attn_full = pair_join(grad_attn, 1).reshape(tokens, model)
    grad_att = nt(weights["out"], grad_attn_full).astype(LOW)
    qkv, land, mixes = kept["qkv"], kept["land"], kept["mixes"]
    row = [((LANDMARKS, width), LOW)]
    rim = [((width, batch_rows * half), LOW)] * 2
    near_queries, *rest = on_core(
        functools.partial(near_back_kernel, half),
        [((width, tokens), jnp.float32)] + row * 8 + rim,
        spot,
        qkv,
        grad_att,
        land,
        *mixes,
    )
    near_outs, near_keys, (low, high) = rest[:4], rest[4:8], rest[8:]
    low, high = rank_shift(high, 1), rank_shift(low, -1)
    own_grad = item_sum(near_outs, layout)
    (own_mix_grad,) = on_core(
        mixture_grad_kernel,
        [((LANDMARKS, width + 128), LOW)],
        None,
        own_grad,
        kept["inverse"],
        kept["weighted"],
    )
    mix_grads = spread_row(own_mix_grad)
    grad_out_weight = nn(kept["att_low"], grad_attn_full)
    out_grad = across_sum(split_across(grad_out_weight.reshape(1, width, model)))
    conv_grad, tap_grad = on_core(
        functools.partial(conv_back_kernel, half),
        [((width, tokens), jnp.float32), ((8, 128), jnp.float32)],
        None,
        qkv,
        grad_att,
        *kept["rims"],
        low,
        high,
        layout["rims"],
        params["lines"][1],
    )
    far_keys, values_low, *parts = on_core(
        far_back_kernel,
        [((width, tokens), jnp.float32), ((width, tokens), LOW)]
        + [((LANDMARKS, 2 * width), LOW)] * 4,
        spot,
        qkv,
        land,
        conv_grad,
        *mixes,
        *mix_grads,
        *near_keys,
    )
    (own_land_grad,) = on_core(
        inverse_back_kernel,
        [((LANDMARKS, 2 * width), jnp.float32)],
        None,
        own_grad,
        kept["weighted"],
        kept["own_land"],
        *kept["chain"],
    )
    own_land_grad = item_sum(parts, layout) + own_land_grad
    land_grads = spread_row(own_land_grad.astype(LOW))
    (grad_qkv,) = on_core(
        token_grad_kernel,
        [((3 * width, tokens), LOW)],
        spot,
        near_queries,
        far_keys,
        values_low,
        layout["pool"],
        *land_grads,
    )
    terms = tn(grad_qkv, weights["qkv"]).reshape(batch_rows, tok_row, model)
    grad_hidden = grad_one + pair_collect(terms)
    grad_weight = nn(grad_qkv, kept["x_full"]).reshape(3, width, model)
    qkv_grad = across_sum(split_across(grad_weight))
    grad_bias = jnp.sum(grad_qkv.astype(jnp.float32), axis=1)
    heads = width // LANDMARKS
    mids = [
        split_flat(grad_bias[:width]),
        split_flat(grad_bias[2 * width :]),
        split_flat(tap_grad[:heads, : 2 * half + 1]),
        grad_up_bias,
    ]
    smalls = [
        grad_out_bias,
        grad_down_bias,
        grad_gain_one,
        grad_shift_one,
        grad_gain_two,
        grad_shift_two,
    ]
    return grad_hidden, (qkv_grad, out_grad, up_grad, down_grad), mids, smalls


def sides(values):
    across = place()[1]
    return [jnp.where(across == 0, values[0], values[1]), jnp.where(across == 0, values[1], values[0])]


def across_sum(pair):
    mine, theirs = pair
    got = exchange(theirs.astype(LOW), 0, 2).astype(jnp.float32)
    return (mine + got).astype(LOW)


def split_flat(values):
    across = place()[1]
    half = values.shape[0] // 2
    low, high = values[:half], values[half:]
    return [jnp.where(across == 0, low, high), jnp.where(across == 0, high, low)]


def split_across(values):
    across = place()[1]
    half = values.shape[1] // 2
    model = values.shape[2]
    low = values[:, :half].reshape(-1, model)
    high = values[:, half:].reshape(-1, model)
    return [jnp.where(across == 0, low, high), jnp.where(across == 0, high, low)]


def halve(values, mask):
    side = (lax.axis_index("seq") // mask) % 2
    half = values.shape[0] // 2
    low, high = values[:half], values[half:]
    keep = jnp.where(side == 0, low, high)
    sent = jnp.where(side == 0, high, low)
    return (keep.astype(jnp.float32) + exchange(sent, mask, 0).astype(jnp.float32)).astype(LOW)


def double(values, mask):
    side = (lax.axis_index("seq") // mask) % 2
    other = exchange(values, mask, 0)
    low = jnp.where(side == 0, values, other)
    high = jnp.where(side == 0, other, values)
    return jnp.concatenate([low, high], axis=0)


def reduce_big(total):
    masks = [1 << i for i in range(lax.axis_size("seq").bit_length() - 1)]
    rows = total.shape[0]
    extra = -rows % (2 * lax.axis_size("seq"))
    if extra:
        total = jnp.pad(total, ((0, extra), (0, 0)))
    middle = total.shape[0] // 2
    done = []
    for part, order in ((total[:middle], masks), (total[middle:], masks[1:] + masks[:1])):
        for mask in order:
            part = halve(part, mask)
        for mask in reversed(order):
            part = double(part, mask)
        done.append(part)
    return jnp.concatenate(done, axis=0)[:rows]


def seq_sum(values):
    mask = 1
    while mask < lax.axis_size("seq"):
        values = values + exchange(values, mask, 0)
        mask *= 2
    return values


def reduce_small(mid, small):
    mine = jnp.concatenate([m[0].reshape(-1) for m in mid])
    theirs = jnp.concatenate([m[1].reshape(-1) for m in mid])
    every = jnp.concatenate([s.reshape(-1) for s in small])
    count, extra = every.shape[0], mine.shape[0]
    pad = -(count + extra) % 1024
    got = exchange(jnp.pad(jnp.concatenate([every, theirs]), (0, pad)), 0, 2)
    total = jnp.pad(jnp.concatenate([every, mine]), (0, pad)) + got
    total = seq_sum(total)
    every = total[:count]
    every = every + exchange(every, 0, 1)
    mids, at = [], count
    for m in mid:
        mids.append(total[at : at + m[0].size].reshape(m[0].shape))
        at += m[0].size
    smalls, at = [], 0
    for s in small:
        smalls.append(every[at : at + s.size].reshape(s.shape))
        at += s.size
    return mids, smalls


def on_device(
    hidden_in,
    query_weight,
    key_weight,
    value_weight,
    query_bias,
    value_bias,
    out_weight,
    out_bias,
    conv_taps,
    up_weight,
    up_bias,
    down_weight,
    down_bias,
    gain_one,
    shift_one,
    gain_two,
    shift_two,
    out_grad,
    item_lengths,
):
    tok_row = hidden_in.shape[1] * 2
    half = (conv_taps.shape[2] - 1) // 2
    layout = item_layout(item_lengths, tok_row, half)
    q_bias, v_bias, taps, both_up = fetch_small(query_bias, value_bias, conv_taps, up_bias)
    params = []
    for i in range(2):
        params.append(
            dict(
                weights=fetch_layer(
                    query_weight[i],
                    key_weight[i],
                    value_weight[i],
                    out_weight[i],
                    up_weight[i],
                    down_weight[i],
                ),
                half=half,
                q_bias=q_bias[i],
                v_bias=v_bias[i],
                lines=tap_lines(taps[i]),
                up_bias=both_up[i],
                out_bias=out_bias[i],
                down_bias=down_bias[i],
                gain_one=gain_one[i],
                shift_one=shift_one[i],
                gain_two=gain_two[i],
                shift_two=shift_two[i],
            )
        )
    hidden = hidden_in.astype(jnp.float32)
    kept = [None, None]
    for i in range(2):
        hidden, kept[i] = layer_forward(hidden, params[i], layout)
    grad = out_grad
    big, mid, small = [None, None], [None, None], [None, None]
    for i in (1, 0):
        grad, grads, mid[i], small[i] = layer_backward(grad, kept[i], params[i], layout)
        if i == 1:
            big[i] = lax.psum(grads, "seq")
        else:
            qkv_grad, out_grad_one, up_grad, down_grad = grads
            rows = [out_grad_one.shape[0], up_grad.shape[0]]
            early = reduce_big(jnp.concatenate([out_grad_one, up_grad, down_grad], axis=0))
            late = reduce_big(qkv_grad)
            big[i] = (
                late,
                early[: rows[0]],
                early[rows[0] : rows[0] + rows[1]],
                early[rows[0] + rows[1] :],
            )
    mids, smalls = reduce_small(
        [[jnp.stack(m) for m in zip(*pairs)] for pairs in zip(*mid)],
        [jnp.stack(pair) for pair in zip(*small)],
    )
    width = query_weight.shape[2]
    qkv = jnp.stack([big[0][0], big[1][0]]).reshape(2, 3, width, -1)
    qkv = [jnp.swapaxes(qkv[:, i], 1, 2).astype(jnp.float32) for i in range(3)]
    outs, ups, downs = [
        jnp.stack([big[0][i], big[1][i]]).astype(jnp.float32) for i in (1, 2, 3)
    ]
    return (
        hidden.astype(LOW),
        grad,
        qkv[0],
        qkv[1],
        qkv[2],
        mids[0],
        mids[1],
        outs,
        smalls[0],
        mids[2].reshape(conv_taps.shape),
        ups,
        mids[3],
        downs,
        smalls[1],
        smalls[2],
        smalls[3],
        smalls[4],
        smalls[5],
    )


def solution(mesh):
    placed = (
        P(None, ("seq", "head"), None),
        P(None, None, "head"),
        P(None, None, "head"),
        P(None, None, "head"),
        P(None, "head"),
        P(None, "head"),
        P(None, "head", None),
        P(),
        P(None, "head", None),
        P(None, None, "head"),
        P(None, "head"),
        P(None, "head", None),
        P(),
        P(),
        P(),
        P(),
        P(),
        P(None, ("seq", "head"), None),
        P(),
    )
    return jax.shard_map(
        on_device,
        mesh=mesh,
        in_specs=placed,
        out_specs=(
            P(None, ("seq", "head"), None),
            P(None, ("seq", "head"), None),
            P(None, None, "head"),
            P(None, None, "head"),
            P(None, None, "head"),
            P(None, "head"),
            P(None, "head"),
            P(None, "head", None),
            P(),
            P(None, "head", None),
            P(None, None, "head"),
            P(None, "head"),
            P(None, "head", None),
            P(),
            P(),
            P(),
            P(),
            P(),
        ),
        check_vma=False,
    )
```

```python
import functools

import jax
import jax.numpy as jnp
from jax import lax
from jax.experimental import pallas as pl
from jax.experimental.pallas import tpu as pltpu
from jax.sharding import PartitionSpec as P

LANDMARKS = 64
NS_STEPS = 6


HIGHEST = lax.Precision.HIGHEST
EPSILON = 1e-05
FLOOR_TOP = -1e30
LOW = jnp.bfloat16
GROUP = ((0, 2), (1, 0), (1, 2))


def layer_norm(values, gain, offset):
    centred = values - jnp.mean(values, axis=-1, keepdims=True)
    variance = jnp.mean(centred * centred, axis=-1, keepdims=True)
    return centred * lax.rsqrt(variance + EPSILON) * gain + offset


def exchange(values, seq_mask, head_mask):
    if seq_mask == 0:
        count = lax.axis_size("head")
        return lax.ppermute(values, "head", [(i, i ^ head_mask) for i in range(count)])
    if head_mask == 0:
        count = lax.axis_size("seq")
        return lax.ppermute(values, "seq", [(i, i ^ seq_mask) for i in range(count)])
    heads = lax.axis_size("head")
    route = []
    for s in range(lax.axis_size("seq")):
        for h in range(heads):
            route.append((s * heads + h, (s ^ seq_mask) * heads + (h ^ head_mask)))
    return lax.ppermute(values, ("seq", "head"), route)


def rank_shift(values, step):
    heads = lax.axis_size("head")
    ranks = lax.axis_size("seq") * (heads // 2)
    route = []
    for rank in range(ranks):
        target = rank + step
        if 0 <= target < ranks:
            for core in range(2):
                source_dev = (rank // 2) * heads + (rank % 2) * 2 + core
                target_dev = (target // 2) * heads + (target % 2) * 2 + core
                route.append((source_dev, target_dev))
    return lax.ppermute(values, ("seq", "head"), route)


def place():
    seq = lax.axis_index("seq")
    head = lax.axis_index("head")
    return seq, head // 2, head % 2


def pair_join(values, axis):
    core = place()[2]
    other = exchange(values, 0, 1)
    low = jnp.where(core == 0, values, other)
    high = jnp.where(core == 0, other, values)
    return jnp.concatenate([low, high], axis=axis)


def pair_collect(terms):
    core = place()[2]
    half = terms.shape[1] // 2
    low, high = terms[:, :half], terms[:, half:]
    mine = jnp.where(core == 0, low, high)
    theirs = jnp.where(core == 0, high, low).astype(jnp.bfloat16)
    return mine + exchange(theirs, 0, 1).astype(jnp.float32)


def group_index():
    seq, across, core = place()
    return across + 2 * (seq % 2)


def upper_levels():
    levels = (lax.axis_size("seq") // 2).bit_length() - 1
    return [(low, min(2, levels - low)) for low in range(0, levels, 2)]


def nn(one, two, precision=None):
    return lax.dot_general(
        one, two, (((1,), (0,)), ((), ())), precision, preferred_element_type=jnp.float32
    )


def nt(one, two, precision=None):
    return lax.dot_general(
        one, two, (((1,), (1,)), ((), ())), precision, preferred_element_type=jnp.float32
    )


def tn(one, two, precision=None):
    return lax.dot_general(
        one, two, (((0,), (0,)), ((), ())), precision, preferred_element_type=jnp.float32
    )


def on_core(kernel, outs, scalars, *arrays, us=1):
    shapes = tuple(jax.ShapeDtypeStruct(shape, dtype) for shape, dtype in outs)
    specs = [pl.BlockSpec(memory_space=pltpu.SMEM)] if scalars is not None else []
    specs += [pl.BlockSpec(memory_space=pltpu.VMEM)] * len(arrays)
    given = ((scalars,) if scalars is not None else ()) + arrays
    return pl.pallas_call(
        kernel,
        out_shape=shapes,
        in_specs=specs,
        out_specs=tuple(pl.BlockSpec(memory_space=pltpu.VMEM) for _ in outs),
        compiler_params=pltpu.CompilerParams(vmem_limit_bytes=48 * 1024 * 1024),
        cost_estimate=pl.CostEstimate(
            flops=us * 10**9, bytes_accessed=us * 3 * 10**6, transcendentals=0
        ),
    )(*given)


def tokens_of(row, tok_row):
    return pl.ds(pl.multiple_of(row * tok_row, tok_row), tok_row)


def lanes(shape):
    return lax.broadcasted_iota(jnp.int32, shape, len(shape) - 1)


def join_pool_kernel(spot, own, other, pool, full, one, two, three, four):
    rows, piece, model = own.shape
    tok_row = 2 * piece
    core = spot[1]
    half = model // 2
    for row in range(rows):
        mine = pl.multiple_of(row * tok_row + core * piece, piece)
        theirs = pl.multiple_of(row * tok_row + (1 - core) * piece, piece)
        full[pl.ds(mine, piece), :] = own[row]
        full[pl.ds(theirs, piece), :] = other[row]
    side = pl.ds(pl.multiple_of(core * half, half), half)
    for step, out in enumerate((one, two, three, four)):
        row = spot[0] ^ step
        block = full[tokens_of(row, tok_row), side]
        out[...] = nn(pool[row], block).astype(LOW)


def rim_blocks(block_of, rows, tok_row, half):
    low, high = None, None
    for row in range(rows):
        block = block_of(row).astype(jnp.float32)
        lane = lanes(block.shape)
        first = block if row == 0 else pltpu.roll(block, row * half, 1)
        shift = (row * half + half) % tok_row
        last = block if shift == 0 else pltpu.roll(block, shift, 1)
        inside = lane // half == row
        low = jnp.where(inside, first, 0.0 if low is None else low)
        high = jnp.where(inside, last, 0.0 if high is None else high)
    return low.astype(LOW), high.astype(LOW)


def far_kernel(half, spot, qkv, land, one, two, three, four, low, high):
    width = qkv.shape[0] // 3
    head_dim = LANDMARKS
    heads = width // head_dim
    tok_row = qkv.shape[1] // 4
    scale = head_dim ** (-0.5)
    for step, out in enumerate((one, two, three, four)):
        here = tokens_of(spot[0] ^ step, tok_row)
        logs = jnp.zeros((LANDMARKS, out.shape[1] - width), jnp.float32)
        lane = lanes(logs.shape)
        for head in range(heads):
            cols = slice(head * head_dim, (head + 1) * head_dim)
            keys = qkv[width + head * head_dim : width + (head + 1) * head_dim, here]
            values = qkv[2 * width + head * head_dim : 2 * width + (head + 1) * head_dim, here]
            land_q = land[step * LANDMARKS : (step + 1) * LANDMARKS, cols]
            scores = nn(land_q, keys) * scale
            top = jnp.max(scores, axis=1, keepdims=True)
            grown = jnp.exp(scores - top)
            total = jnp.sum(grown, axis=1, keepdims=True)
            out[:, cols] = nt(grown.astype(LOW), values) / total
            logs = jnp.where(lane == head, top + jnp.log(total), logs)
        out[:, width:] = logs
    low[...], high[...] = rim_blocks(
        lambda row: qkv[2 * width :, row * tok_row : (row + 1) * tok_row], 4, tok_row, half
    )


def merged(flags, pieces, width):
    head_dim = LANDMARKS
    mixes, logs = [], []
    for head in range(width // head_dim):
        cols = slice(head * head_dim, (head + 1) * head_dim)
        column = slice(width + head, width + head + 1)
        log = [pieces[0][:, column]]
        for index, piece in enumerate(pieces[1:]):
            log.append(jnp.where(flags[index] > 0, piece[:, column], FLOOR_TOP))
        top = functools.reduce(jnp.maximum, log)
        shares = [jnp.exp(value - top) for value in log]
        total = functools.reduce(jnp.add, shares)
        mix = sum(share * piece[:, cols] for share, piece in zip(shares, pieces))
        mixes.append(mix / total)
        logs.append(top + jnp.log(total))
    return mixes, logs


def merge_kernel(count, flags, *refs):
    out = refs[count]
    width = out.shape[1] - 128
    mixes, logs = merged(flags, refs[:count], width)
    packed = jnp.zeros((LANDMARKS, 128), jnp.float32)
    lane = lanes(packed.shape)
    for head, (mix, log) in enumerate(zip(mixes, logs)):
        out[:, head * LANDMARKS : (head + 1) * LANDMARKS] = mix
        packed = jnp.where(lane == head, log, packed)
    out[:, width:] = packed


def packed_parts(columns):
    packed = jnp.zeros((LANDMARKS, 128), jnp.float32)
    lane = lanes(packed.shape)
    for head, column in enumerate(columns):
        for part in range(3):
            rounded = column.astype(LOW).astype(jnp.float32)
            packed = jnp.where(lane == head + 8 * part, rounded, packed)
            column = column - rounded
    return packed.astype(LOW)


def unpacked_part(packed, head):
    packed = packed.astype(jnp.float32)
    return (
        packed[:, head : head + 1]
        + packed[:, head + 8 : head + 9]
        + packed[:, head + 16 : head + 17]
    )


def land_out_kernel(count, flags, *refs):
    inverse, out, weighted = refs[count:]
    width = weighted.shape[1]
    mixes, logs = merged(flags, refs[:count], width)
    for head, mix in enumerate(mixes):
        cols = slice(head * LANDMARKS, (head + 1) * LANDMARKS)
        weighted[:, cols] = mix
        out[:, cols] = nn(inverse[head], mix, HIGHEST).astype(LOW)
    out[:, width:] = packed_parts(logs)


def inverse_kernel(land, amats, inverses, products, seconds, thirds):
    width = land.shape[1] // 2
    heads = width // LANDMARKS
    scale = LANDMARKS ** (-0.5)
    shape = (LANDMARKS, LANDMARKS)
    rows = lax.broadcasted_iota(jnp.int32, shape, 0)
    eye = (rows == lanes(shape)).astype(jnp.float32)
    matrices, iterates = [], []
    for head in range(heads):
        cols = slice(head * LANDMARKS, (head + 1) * LANDMARKS)
        keys = slice(width + head * LANDMARKS, width + (head + 1) * LANDMARKS)
        scores = nt(land[:LANDMARKS, cols], land[:LANDMARKS, keys]) * scale
        grown = jnp.exp(scores - jnp.max(scores, axis=1, keepdims=True))
        matrix = grown / jnp.sum(grown, axis=1, keepdims=True)
        columns = jnp.sum(matrix, axis=0, keepdims=True)
        square = columns * columns
        fourth = square * square
        bound = jnp.sum(fourth * fourth, axis=1, keepdims=True)
        bound = jnp.exp(jnp.log(bound) * 0.125)
        amats[head] = matrix
        matrices.append(matrix)
        iterates.append(matrix.T / bound)
    for step in range(NS_STEPS):
        product = [nn(a, z, HIGHEST) for a, z in zip(matrices, iterates)]
        inner = [nn(p, 7.0 * eye - p, HIGHEST) for p in product]
        second = [15.0 * eye - value for value in inner]
        third = [13.0 * eye - nn(p, m, HIGHEST) for p, m in zip(product, second)]
        for head in range(heads):
            inverses[step * heads + head] = iterates[head]
            products[step * heads + head] = product[head]
            seconds[step * heads + head] = second[head]
            thirds[step * heads + head] = third[head]
        iterates = [0.25 * nn(z, m, HIGHEST) for z, m in zip(iterates, third)]
    for head in range(heads):
        inverses[NS_STEPS * heads + head] = iterates[head]


def band_blocks(line, tok_row, half):
    span = line.shape[1]
    wide = jnp.broadcast_to(line, (tok_row, span))
    middle = pltpu.roll(wide, 0, 1, stride=1, stride_axis=0)[:, :tok_row]
    short = jnp.broadcast_to(line, (half, span))
    low = pltpu.roll(short, span - half, 1, stride=1, stride_axis=0)[:, :tok_row]
    high = pltpu.roll(short, tok_row, 1, stride=1, stride_axis=0)[:, :tok_row]
    reps = tok_row // half
    return [
        part.astype(LOW)
        for part in (middle, jnp.concatenate([low] * reps, 0), jnp.concatenate([high] * reps, 0))
    ]


def near_kernel(half, spot, qkv, low, high, rims, land, one, two, three, four, line, out):
    width = qkv.shape[0] // 3
    tok_row = qkv.shape[1] // 4
    head_dim = LANDMARKS
    scale = head_dim ** (-0.5)
    low_all = low[...].astype(jnp.float32) * rims[0:1, :]
    high_all = high[...].astype(jnp.float32) * rims[1:2, :]
    lane = lanes((head_dim, tok_row)) // half
    bands = [band_blocks(line[h : h + 1, :], tok_row, half) for h in range(width // head_dim)]
    for step, mixed in enumerate((one, two, three, four)):
        row = spot[0] ^ step
        here = tokens_of(row, tok_row)
        land_rows = slice(step * LANDMARKS, (step + 1) * LANDMARKS)
        for head in range(width // head_dim):
            cols = slice(head * head_dim, (head + 1) * head_dim)
            keys = slice(width + head * head_dim, width + (head + 1) * head_dim)
            queries = qkv[cols, here]
            scores = nn(land[land_rows, keys], queries) * scale
            grown = jnp.exp(scores - jnp.max(scores, axis=0, keepdims=True))
            probs = grown / jnp.sum(grown, axis=0, keepdims=True)
            total = tn(mixed[:, cols], probs.astype(LOW))
            values = qkv[2 * width + head * head_dim : 2 * width + (head + 1) * head_dim, here]
            total = total + nn(values, bands[head][0])
            mine = lane == row
            total = total + nn(jnp.where(mine, low_all[cols, :], 0.0).astype(LOW), bands[head][1])
            total = total + nn(jnp.where(mine, high_all[cols, :], 0.0).astype(LOW), bands[head][2])
            out[cols, here] = total.astype(LOW)


def near_back_kernel(half, spot, qkv, grads, land, *refs):
    mixes, queries_out = refs[:4], refs[4]
    land_outs, land_keys, low, high = refs[5:9], refs[9:13], refs[13], refs[14]
    width = qkv.shape[0] // 3
    tok_row = qkv.shape[1] // 4
    head_dim = LANDMARKS
    scale = head_dim ** (-0.5)
    for step in range(4):
        here = tokens_of(spot[0] ^ step, tok_row)
        land_rows = slice(step * LANDMARKS, (step + 1) * LANDMARKS)
        for head in range(width // head_dim):
            cols = slice(head * head_dim, (head + 1) * head_dim)
            keys = slice(width + head * head_dim, width + (head + 1) * head_dim)
            queries = qkv[cols, here]
            land_k = land[land_rows, keys]
            scores = nn(land_k, queries) * scale
            grown = jnp.exp(scores - jnp.max(scores, axis=0, keepdims=True))
            probs = grown / jnp.sum(grown, axis=0, keepdims=True)
            grad = grads[cols, here]
            grad_probs = nn(mixes[step][:, cols], grad)
            inner = jnp.sum(grad_probs * probs, axis=0, keepdims=True)
            grad_scores = (probs * (grad_probs - inner) * scale).astype(LOW)
            queries_out[cols, here] = tn(land_k, grad_scores)
            land_keys[step][:, cols] = nt(grad_scores, queries).astype(LOW)
            land_outs[step][:, cols] = nt(probs.astype(LOW), grad).astype(LOW)
    low[...], high[...] = rim_blocks(
        lambda row: grads[:, row * tok_row : (row + 1) * tok_row], 4, tok_row, half
    )


def conv_back_kernel(half, qkv, grads, low, high, grad_low, grad_high, rims, line, out, taps):
    width = qkv.shape[0] // 3
    tok_row = qkv.shape[1] // 4
    head_dim = LANDMARKS
    span = line.shape[1]
    low_all = low[...].astype(jnp.float32) * rims[0:1, :]
    high_all = high[...].astype(jnp.float32) * rims[1:2, :]
    grad_low_all = grad_low[...].astype(jnp.float32) * rims[0:1, :]
    grad_high_all = grad_high[...].astype(jnp.float32) * rims[1:2, :]
    lane = lanes((head_dim, tok_row)) // half
    square = (tok_row, tok_row)
    turned = (lax.broadcasted_iota(jnp.int32, square, 0) + lanes(square) == tok_row - 1).astype(LOW)
    wide = lanes((tok_row, span))
    for head in range(width // head_dim):
        cols = slice(head * head_dim, (head + 1) * head_dim)
        bands = band_blocks(line[head : head + 1, :], tok_row, half)
        fields = [jnp.zeros(square, jnp.float32) for _ in range(3)]
        for row in range(4):
            here = slice(row * tok_row, (row + 1) * tok_row)
            mine = lane == row

            def rim(block):
                return jnp.where(mine, block[cols, :], 0.0).astype(LOW)

            grad = grads[cols, here]
            values = qkv[2 * width + head * head_dim : 2 * width + (head + 1) * head_dim, here]
            total = nn(grad, bands[0]) + nn(rim(grad_low_all), bands[1])
            out[cols, here] = total + nn(rim(grad_high_all), bands[2])
            backward = nn(grad, turned).astype(LOW)
            for index, block in enumerate((values, rim(low_all), rim(high_all))):
                fields[index] = fields[index] + tn(backward, block)
        ends = []
        for field in fields[1:]:
            folded = field + pltpu.roll(field, 2 * half, 1)
            folded = folded + pltpu.roll(folded, half, 1)
            ends.append(jnp.concatenate([folded, folded], axis=1))
        whole = jnp.concatenate([fields[0], jnp.zeros(square, jnp.float32)], axis=1)
        whole = pltpu.roll(whole, half, 1)
        whole = jnp.where(wide < half, ends[0], whole)
        right = (wide >= half + tok_row) & (wide < 2 * half + tok_row)
        whole = jnp.where(right, ends[1], whole)
        whole = pltpu.roll(whole, span - tok_row + 1, 1, stride=1, stride_axis=0)
        taps[head : head + 1, :] = jnp.sum(whole, axis=0, keepdims=True)[:, :128]


def mixture_grad_kernel(grads, inverse, weighted, out):
    width = grads.shape[1]
    inner = []
    for head in range(width // LANDMARKS):
        cols = slice(head * LANDMARKS, (head + 1) * LANDMARKS)
        value = tn(inverse[head], grads[:, cols], HIGHEST).astype(LOW)
        out[:, cols] = value
        product = value.astype(jnp.float32) * weighted[:, cols]
        inner.append(jnp.sum(product, axis=1, keepdims=True))
    out[:, width:] = packed_parts(inner)


def inverse_back_kernel(
    grads, weighted, land, amats, inverses, products, seconds, thirds, out
):
    width = grads.shape[1]
    heads = width // LANDMARKS
    scale = LANDMARKS ** (-0.5)
    shape = (LANDMARKS, LANDMARKS)
    rows = lax.broadcasted_iota(jnp.int32, shape, 0)
    eye = (rows == lanes(shape)).astype(jnp.float32)
    every = range(heads)
    columns = [slice(head * LANDMARKS, (head + 1) * LANDMARKS) for head in every]
    grad = [nt(grads[:, c], weighted[:, c], HIGHEST) for c in columns]
    matrices = [amats[head] for head in every]
    total = [jnp.zeros(shape, jnp.float32) for _ in every]
    for step in reversed(range(NS_STEPS)):
        z = [inverses[step * heads + head] for head in every]
        p = [products[step * heads + head] for head in every]
        m2 = [seconds[step * heads + head] for head in every]
        m3 = [thirds[step * heads + head] for head in every]
        g3 = [-0.25 * tn(z[i], grad[i], HIGHEST) for i in every]
        gz = [0.25 * nt(grad[i], m3[i], HIGHEST) for i in every]
        g2 = [-tn(p[i], g3[i], HIGHEST) for i in every]
        gp = [nt(g3[i], m2[i], HIGHEST) for i in every]
        g1 = [tn(p[i], g2[i], HIGHEST) for i in every]
        gp = [gp[i] + nt(g2[i], 7.0 * eye - p[i], HIGHEST) - g1[i] for i in every]
        total = [total[i] + nt(gp[i], z[i], HIGHEST) for i in every]
        grad = [gz[i] + tn(matrices[i], gp[i], HIGHEST) for i in every]
    for head in every:
        matrix = matrices[head]
        sums = jnp.sum(matrix, axis=0, keepdims=True)
        square = sums * sums
        fourth = square * square
        bound = jnp.sum(fourth * fourth, axis=1, keepdims=True)
        bound = jnp.exp(jnp.log(bound) * 0.125)
        first = inverses[head]
        lost = jnp.sum(grad[head] * first, axis=1, keepdims=True)
        lost = -jnp.sum(lost, axis=0, keepdims=True) / bound
        ratio = sums / bound
        cube = ratio * ratio * ratio
        value = total[head] + grad[head].T / bound + lost * (cube * cube * ratio)
        inner = jnp.sum(value * matrix, axis=1, keepdims=True)
        scores = matrix * (value - inner) * scale
        keys = slice(width + head * LANDMARKS, width + (head + 1) * LANDMARKS)
        land_q = land[:LANDMARKS, columns[head]].astype(jnp.float32)
        land_k = land[:LANDMARKS, keys].astype(jnp.float32)
        out[:, columns[head]] = nn(scores, land_k, HIGHEST)
        out[:, keys] = tn(scores, land_q, HIGHEST)


def far_back_kernel(spot, qkv, land, conv, *refs):
    mixes, grads, near_keys = refs[:4], refs[4:8], refs[8:12]
    keys_out, values_out, parts = refs[12], refs[13], refs[14:18]
    width = qkv.shape[0] // 3
    tok_row = qkv.shape[1] // 4
    head_dim = LANDMARKS
    scale = head_dim ** (-0.5)
    for step in range(4):
        here = tokens_of(spot[0] ^ step, tok_row)
        land_rows = slice(step * LANDMARKS, (step + 1) * LANDMARKS)
        for head in range(width // head_dim):
            cols = slice(head * head_dim, (head + 1) * head_dim)
            keys = qkv[width + head * head_dim : width + (head + 1) * head_dim, here]
            values = qkv[2 * width + head * head_dim : 2 * width + (head + 1) * head_dim, here]
            land_q = land[land_rows, cols]
            log = unpacked_part(mixes[step][:, width:], head)
            inner = unpacked_part(grads[step][:, width:], head)
            probs = jnp.exp(nn(land_q, keys) * scale - log)
            grad = grads[step][:, cols]
            scores = (probs * (nn(grad, values) - inner) * scale).astype(LOW)
            parts[step][:, cols] = nt(scores, keys).astype(LOW)
            keys_out[cols, here] = tn(land_q, scores)
            values_out[cols, here] = (conv[cols, here] + tn(grad, probs.astype(LOW))).astype(LOW)
        parts[step][:, width:] = near_keys[step][...]


def token_grad_kernel(spot, near, far, values, pool, one, two, three, four, out):
    width = near.shape[0]
    tok_row = near.shape[1] // 4
    for step, grads in enumerate((one, two, three, four)):
        row = spot[0] ^ step
        here = tokens_of(row, tok_row)
        share = pool[row]
        out[:width, here] = (near[:, here] + tn(grads[:, :width], share)).astype(LOW)
        out[width : 2 * width, here] = (far[:, here] + tn(grads[:, width:], share)).astype(LOW)
    out[2 * width :, :] = values[...]


def send_rows(pieces):
    got = [exchange(piece, s, h) for piece, (s, h) in zip(pieces[1:], GROUP)]
    return [pieces[0]] + got


def spread_row(row):
    return [row] + [exchange(row, s, h) for s, h in GROUP]


def item_sum(pieces, layout, beside=None):
    return item_total(send_rows(pieces), layout, beside)


def item_total(pieces, layout, beside=None):
    span = layout["span"]
    dtype = pieces[0].dtype
    pieces = [piece.astype(jnp.float32) for piece in pieces]
    total = (pieces[0] + pieces[1]) + (pieces[2] + pieces[3])
    if beside is not None:
        beside, total = tied(beside, total)
        beside = exchange(beside, 0, 2)
    for low, bits in upper_levels():
        sent = total.astype(dtype)
        near = exchange(sent, 2 << low, 0).astype(jnp.float32)
        pair = total + jnp.where(span > 4 << low, near, 0.0)
        if bits == 2:
            far = exchange(sent, 4 << low, 0).astype(jnp.float32)
            cross = exchange(sent, 6 << low, 0).astype(jnp.float32)
            pair = pair + jnp.where(span > 8 << low, far + cross, 0.0)
        total = pair
    if beside is not None:
        beside, total = tied(beside, total)
        return total, beside
    return total


def land_mixture(pieces, inverse, layout):
    span = layout["span"]
    width = pieces[0].shape[1] - 128
    pieces = send_rows(pieces)
    flags = jnp.ones((3,), jnp.int32)
    for low, bits in upper_levels():
        call = functools.partial(merge_kernel, len(pieces))
        (row,) = on_core(call, [(pieces[0].shape, jnp.float32)], flags, *pieces)
        pieces = [row] + [exchange(row, m << (low + 1), 0) for m in range(1, 1 << bits)]
        wide = (span > 8 << low).astype(jnp.int32)
        flags = jnp.stack([(span > 4 << low).astype(jnp.int32), wide, wide])
    outs = [(pieces[0].shape, LOW), ((LANDMARKS, width), jnp.float32)]
    call = functools.partial(land_out_kernel, len(pieces))
    return on_core(call, outs, flags, *pieces, inverse)


def item_layout(item_lengths, tok_row, half):
    seq, across, core = place()
    rank = seq * 2 + across
    ends = jnp.cumsum(item_lengths, axis=1)
    starts = ends - item_lengths
    first_token = rank * tok_row
    chosen = (starts <= first_token) & (first_token < ends)
    length = jnp.sum(jnp.where(chosen, item_lengths, 0), axis=1)
    begin = jnp.sum(jnp.where(chosen, starts, 0), axis=1)
    segment = length // LANDMARKS
    first_rank = begin // tok_row
    spans = length // tok_row
    positions = first_token + jnp.arange(tok_row)
    marks = (positions[None, :] - begin[:, None]) // segment[:, None]
    hits = marks[:, None, :] == jnp.arange(LANDMARKS)[None, :, None]
    share = 1.0 / segment.astype(jnp.float32)
    pool = jnp.where(hits, share[:, None, None], 0.0).astype(LOW)
    left_open = rank > first_rank
    right_open = rank + 1 < first_rank + spans
    rims = jnp.repeat(jnp.stack([left_open, right_open]).astype(jnp.float32), half, axis=1)
    me = group_index()
    return dict(
        span=lax.dynamic_index_in_dim(spans, me, 0, keepdims=False),
        pool=pool,
        rims=jnp.pad(rims, ((0, 6), (0, 0))),
        spot=jnp.stack([me, core]).astype(jnp.int32),
    )


def dot(spec, one, two):
    return jnp.einsum(spec, one, two, preferred_element_type=jnp.float32)


def ordered(mine, other, axis):
    across = place()[1]
    low = jnp.where(across == 0, mine, other)
    high = jnp.where(across == 0, other, mine)
    return jnp.stack([low, high], axis=axis)


def fetch_small(query_bias, value_bias, conv_taps, up_bias):
    layers = query_bias.shape[0]
    flat = [a.reshape(layers, -1) for a in (query_bias, value_bias, conv_taps, up_bias)]
    sizes = [a.shape[1] for a in flat]
    packed = jnp.concatenate(flat, axis=1)
    other = exchange(jnp.pad(packed, ((0, 0), (0, -packed.shape[1] % 128))), 0, 2)
    rest, at = [], 0
    for size in sizes:
        rest.append(other[:, at : at + size])
        at += size
    heads = conv_taps.shape[1]
    q_bias = ordered(query_bias, rest[0], 1).reshape(layers, -1)
    v_bias = ordered(value_bias, rest[1], 1).reshape(layers, -1)
    taps = ordered(conv_taps, rest[2].reshape(conv_taps.shape), 1).reshape(layers, 2 * heads, -1)
    return q_bias, v_bias, taps, ordered(up_bias, rest[3], 1)


def across_gather(values):
    return lax.all_gather(values, "head", axis=0, axis_index_groups=[[0, 2], [1, 3]])


def fetch_weights(
    query_weight, key_weight, value_weight, out_weight, up_weight, down_weight, pooled
):
    model = up_weight.shape[1]
    packs = [
        jnp.concatenate([query_weight[i].T, key_weight[i].T, value_weight[i].T], 0)
        for i in range(2)
    ]
    pack, *pooled = tied(packs[0], *pooled)
    other = exchange(pack, 0, 2)
    own_out, other = tied(out_weight[0], other)
    other_out = exchange(own_out, 0, 2)
    held = jnp.concatenate([packs[1], out_weight[1]], 0)
    held, other_out = tied(held, other_out)
    first = ordered(pack.reshape(3, -1, model), other.reshape(3, -1, model), 1)
    layers = [
        dict(
            qkv=first.reshape(-1, model),
            out=ordered(own_out, other_out, 0).reshape(-1, model),
            up=up_weight[:1],
            down=down_weight[:1],
        ),
        dict(
            attn=jnp.swapaxes(across_gather(held).reshape(2, 4, -1, model), 0, 1),
            up=across_gather(up_weight[1]),
            down=across_gather(down_weight[1]),
        ),
    ]
    return layers, pooled


def tap_lines(taps):
    count = taps.shape[1]
    half = (count - 1) // 2
    gap = jnp.zeros((taps.shape[0], 256 - count), jnp.float32)
    flipped = taps[:, ::-1]
    lines = [jnp.concatenate([t[:, half:], gap, t[:, :half]], axis=1) for t in (flipped, taps)]
    pad = -taps.shape[0] % 8
    return [jnp.pad(line, ((0, pad), (0, 0))) for line in lines]


def token_sets(values, own_pair):
    own = pair_join(values, 1)
    flat = (own.shape[0] * own.shape[1], own.shape[2])
    if own_pair:
        return [own.reshape(flat)]
    return [own.reshape(flat), pair_join(exchange(values, 0, 2), 1).reshape(flat)]


def collect_sets(terms, rows):
    terms = [term.reshape(rows, -1, term.shape[-1]) for term in terms]
    total = pair_collect(terms[0])
    if len(terms) == 2:
        total = total + exchange(pair_collect(terms[1]).astype(LOW), 0, 2).astype(jnp.float32)
    return total


def join_pool(hidden, layout):
    batch_rows, piece, model = hidden.shape
    quarter = [((LANDMARKS, model // 2), LOW)] * 4
    x_low = hidden.astype(LOW)
    x_full, *pooled = on_core(
        join_pool_kernel,
        [((batch_rows * 2 * piece, model), LOW)] + quarter,
        layout["spot"],
        x_low,
        exchange(x_low, 0, 1),
        layout["pool"],
    )
    return x_full, send_rows(pooled)


def layer_forward(hidden, params, layout, joined, ahead=None):
    weights = params["weights"]
    if params["offload"]:
        attn = weights["attn"].reshape(-1, hidden.shape[2])
        weights["qkv"] = attn[: attn.shape[0] * 3 // 4]
        weights["out"] = attn[attn.shape[0] * 3 // 4 :]
    spot = layout["spot"]
    batch_rows, piece, model = hidden.shape
    tok_row = 2 * piece
    tokens = batch_rows * tok_row
    width = weights["out"].shape[0]
    half = params["half"]
    x_full, pooled = joined
    if params["offload"]:
        weights["up"], *pooled = tied(weights["up"], *pooled)
    pooled = jnp.concatenate(spread_row(item_total(pooled, layout).astype(LOW)), axis=0)
    pooled = pair_join(pooled, 1)
    bias_q, bias_v = params["q_bias"], params["v_bias"]
    no_bias = jnp.zeros_like(bias_q)
    column = jnp.concatenate([bias_q, no_bias, bias_v])[:, None]
    qkv = (nt(weights["qkv"], x_full) + column).astype(LOW)
    land = nt(pooled, weights["qkv"][: 2 * width]) + jnp.concatenate([bias_q, no_bias])
    land = land.astype(LOW)
    heads = width // LANDMARKS
    message = [((LANDMARKS, width + 128), jnp.float32)] * 4
    rim = [((width, batch_rows * half), LOW)] * 2
    *parts, low, high = on_core(
        functools.partial(far_kernel, half), message + rim, spot, qkv, land, us=4
    )
    low, high = rank_shift(high, 1), rank_shift(low, -1)
    square = (LANDMARKS, LANDMARKS)
    steps = ((NS_STEPS * heads,) + square, jnp.float32)
    own_land = land[:LANDMARKS]
    chain = on_core(
        inverse_kernel,
        [
            ((heads,) + square, jnp.float32),
            (((NS_STEPS + 1) * heads,) + square, jnp.float32),
            steps,
            steps,
            steps,
        ],
        None,
        own_land,
        us=5,
    )
    inverse = chain[1][NS_STEPS * heads :]
    own_out, weighted = land_mixture(parts, inverse, layout)
    if params["offload"]:
        own_out, weights["down"] = tied(own_out, weights["down"])
    mixes = spread_row(own_out)
    (att_low,) = on_core(
        functools.partial(near_kernel, half),
        [((width, tokens), LOW)],
        spot,
        qkv,
        low,
        high,
        layout["rims"],
        land,
        *mixes,
        params["lines"][0],
        us=3,
    )
    terms = tn(att_low, weights["out"]).reshape(batch_rows, tok_row, model)
    if ahead is not None:
        terms, ahead["attn"] = tied(terms, ahead["attn"])
    resid_one = hidden + (pair_collect(terms) + params["out_bias"])
    normed = layer_norm(resid_one, params["gain_one"], params["shift_one"])
    h_sets = token_sets(normed.astype(LOW), params["offload"])
    gelu_low, slopes, terms = [], [], []
    for h_full in h_sets:
        up_pre = dot("td,gdf->gtf", h_full, weights["up"]) + params["up_bias"][:, None, :]
        area = 0.5 * (1.0 + lax.erf(up_pre * 0.7071067811865476))
        bell = jnp.exp(-0.5 * up_pre * up_pre) * 0.3989422804014327
        gelu_low.append((up_pre * area).astype(LOW))
        slopes.append((area + up_pre * bell).astype(LOW))
        terms.append(dot("gtf,gfd->td", gelu_low[-1], weights["down"]))
    mlp_out = collect_sets(terms, batch_rows) + params["down_bias"]
    resid_two = normed + mlp_out
    result = layer_norm(resid_two, params["gain_two"], params["shift_two"])
    kept = dict(
        x_full=x_full,
        qkv=qkv,
        land=land,
        own_land=own_land,
        rims=(low, high),
        chain=chain,
        inverse=inverse,
        weighted=weighted,
        mixes=mixes,
        att_low=att_low,
        resid_one=resid_one,
        h_sets=h_sets,
        gelu_low=gelu_low,
        slopes=slopes,
        resid_two=resid_two,
    )
    return result, kept


def layer_backward(grad_out, kept, params, layout, pending):
    weights = params["weights"]
    spot = layout["spot"]
    batch_rows, piece, model = grad_out.shape
    tok_row = 2 * piece
    tokens = batch_rows * tok_row
    width = weights["out"].shape[0]
    half = params["half"]
    unused_two, pull_two = jax.vjp(
        layer_norm, kept["resid_two"], params["gain_two"], params["shift_two"]
    )
    grad_two, grad_gain_two, grad_shift_two = pull_two(grad_out)
    grad_mlp = grad_two.astype(LOW)
    grad_down_bias = jnp.sum(grad_mlp.astype(jnp.float32), axis=(0, 1))
    grad_sets = token_sets(grad_mlp, params["offload"])
    grad_ups, terms = [], []
    for grad_set, slope in zip(grad_sets, kept["slopes"]):
        grad_up = dot("td,gfd->gtf", grad_set, weights["down"])
        grad_ups.append((grad_up * slope.astype(jnp.float32)).astype(LOW))
        terms.append(dot("gtf,gdf->td", grad_ups[-1], weights["up"]))
    grad_normed = grad_two + collect_sets(terms, batch_rows)
    down_grad = sum(dot("gtf,td->gfd", g, d) for g, d in zip(kept["gelu_low"], grad_sets))
    up_grad = sum(dot("td,gtf->gdf", h, g) for h, g in zip(kept["h_sets"], grad_ups))
    ffn_grad = jnp.concatenate([up_grad, down_grad], axis=1).astype(LOW)
    grad_up_bias = sum(jnp.sum(g.astype(jnp.float32), axis=1) for g in grad_ups)
    if params["offload"]:
        ffn_grad = seq_scatter(ffn_grad)
        grad_up_bias = sides(grad_up_bias)
    else:
        ffn_one, attn_one = pending
        rows = attn_one.shape[1]
        packed = jnp.stack([attn_one[0], attn_one[1], ffn_grad[0, :rows], ffn_grad[0, rows:]])
        ffn_grad = (ffn_one, seq_scatter(packed))
        grad_up_bias = [grad_up_bias[0], jnp.zeros_like(grad_up_bias[0])]
    unused_one, pull_one = jax.vjp(
        layer_norm, kept["resid_one"], params["gain_one"], params["shift_one"]
    )
    grad_one, grad_gain_one, grad_shift_one = pull_one(grad_normed)
    grad_attn = grad_one.astype(LOW)
    grad_out_bias = jnp.sum(grad_attn.astype(jnp.float32), axis=(0, 1))
    grad_attn_full = pair_join(grad_attn, 1).reshape(tokens, model)
    grad_att = nt(weights["out"], grad_attn_full).astype(LOW)
    qkv, land, mixes = kept["qkv"], kept["land"], kept["mixes"]
    row = [((LANDMARKS, width), LOW)]
    rim = [((width, batch_rows * half), LOW)] * 2
    near_queries, *rest = on_core(
        functools.partial(near_back_kernel, half),
        [((width, tokens), jnp.float32)] + row * 8 + rim,
        spot,
        qkv,
        grad_att,
        land,
        *mixes,
        us=6,
    )
    near_outs, near_keys, (low, high) = rest[:4], rest[4:8], rest[8:]
    low, high = rank_shift(high, 1), rank_shift(low, -1)
    own_grad = item_sum(near_outs, layout)
    (own_mix_grad,) = on_core(
        mixture_grad_kernel,
        [((LANDMARKS, width + 128), LOW)],
        None,
        own_grad,
        kept["inverse"],
        kept["weighted"],
    )
    mix_grads = spread_row(own_mix_grad)
    if pending is not None:
        ffn_one, *mix_grads = tied(ffn_grad[0], *mix_grads)
        ffn_grad = (ffn_one, ffn_grad[1])
    grad_out_weight = nn(kept["att_low"], grad_attn_full)
    conv_grad, tap_grad = on_core(
        functools.partial(conv_back_kernel, half),
        [((width, tokens), jnp.float32), ((8, 128), jnp.float32)],
        None,
        qkv,
        grad_att,
        *kept["rims"],
        low,
        high,
        layout["rims"],
        params["lines"][1],
        us=6,
    )
    far_keys, values_low, *parts = on_core(
        far_back_kernel,
        [((width, tokens), jnp.float32), ((width, tokens), LOW)]
        + [((LANDMARKS, 2 * width), LOW)] * 4,
        spot,
        qkv,
        land,
        conv_grad,
        *mixes,
        *mix_grads,
        *near_keys,
        us=5,
    )
    (own_land_grad,) = on_core(
        inverse_back_kernel,
        [((LANDMARKS, 2 * width), jnp.float32)],
        None,
        own_grad,
        kept["weighted"],
        kept["own_land"],
        *kept["chain"],
        us=13,
    )
    if params["offload"]:
        own_land_grad = item_sum(parts, layout) + own_land_grad
    else:
        first_grad = jnp.stack([nn(values_low, kept["x_full"]), grad_out_weight])
        first_mine, first_theirs = split_across(first_grad)
        land_sum, first_got = item_sum(parts, layout, first_theirs.astype(LOW))
        own_land_grad = land_sum + own_land_grad
        first_grad = (first_mine + first_got.astype(jnp.float32)).astype(LOW)
    land_grads = spread_row(own_land_grad.astype(LOW))
    (grad_qkv,) = on_core(
        token_grad_kernel,
        [((3 * width, tokens), LOW)],
        spot,
        near_queries,
        far_keys,
        values_low,
        layout["pool"],
        *land_grads,
    )
    terms = tn(grad_qkv, weights["qkv"]).reshape(batch_rows, tok_row, model)
    grad_hidden = grad_one + pair_collect(terms)
    if params["offload"]:
        grad_weight = nn(grad_qkv, kept["x_full"])
        attn_grad = jnp.concatenate([grad_weight, grad_out_weight], axis=0)
        attn_grad = attn_grad.reshape(4, 2, width // 2, model).astype(LOW)
        attn_grad = jnp.swapaxes(attn_grad, 0, 1).reshape(2, 2 * width, model)
    else:
        grad_weight = nn(grad_qkv[: 2 * width], kept["x_full"]).reshape(2, width, model)
        attn_grad = across_sum(split_across(grad_weight))
        attn_grad, packed = tied(attn_grad, ffn_grad[1])
        ffn_grad = (ffn_grad[0], packed)
        attn_grad = jnp.concatenate([attn_grad, first_grad], axis=0)
    grad_bias = jnp.sum(grad_qkv.astype(jnp.float32), axis=1)
    heads = width // LANDMARKS
    mids = [
        split_flat(grad_bias[:width]),
        split_flat(grad_bias[2 * width :]),
        split_flat(tap_grad[:heads, : 2 * half + 1]),
        grad_up_bias,
    ]
    smalls = [
        grad_out_bias,
        grad_down_bias,
        grad_gain_one,
        grad_shift_one,
        grad_gain_two,
        grad_shift_two,
    ]
    return grad_hidden, (attn_grad, ffn_grad), mids, smalls


def sides(values):
    across = place()[1]
    return [jnp.where(across == 0, values[0], values[1]), jnp.where(across == 0, values[1], values[0])]


def seq_scatter(values):
    return lax.psum_scatter(values, "seq", scatter_dimension=values.ndim - 2, tiled=True)


def seq_gather(values):
    return lax.all_gather(values, "seq", axis=0, tiled=True)


def across_pick(values):
    mine, theirs = sides(values)
    return across_sum([mine.astype(jnp.float32), theirs])


def tied(values, *others):
    return lax.optimization_barrier((values,) + others)


def across_sum(pair):
    mine, theirs = pair
    got = exchange(theirs.astype(LOW), 0, 2).astype(jnp.float32)
    return (mine + got).astype(LOW)


def split_flat(values):
    across = place()[1]
    half = values.shape[0] // 2
    low, high = values[:half], values[half:]
    return [jnp.where(across == 0, low, high), jnp.where(across == 0, high, low)]


def split_across(values):
    across = place()[1]
    half = values.shape[1] // 2
    model = values.shape[2]
    low = values[:, :half].reshape(-1, model)
    high = values[:, half:].reshape(-1, model)
    return [jnp.where(across == 0, low, high), jnp.where(across == 0, high, low)]


def halve(values, mask):
    side = (lax.axis_index("seq") // mask) % 2
    half = values.shape[0] // 2
    low, high = values[:half], values[half:]
    keep = jnp.where(side == 0, low, high)
    sent = jnp.where(side == 0, high, low)
    return (keep.astype(jnp.float32) + exchange(sent, mask, 0).astype(jnp.float32)).astype(LOW)


def double(values, mask):
    side = (lax.axis_index("seq") // mask) % 2
    other = exchange(values, mask, 0)
    low = jnp.where(side == 0, values, other)
    high = jnp.where(side == 0, other, values)
    return jnp.concatenate([low, high], axis=0)


def reduce_big(total):
    masks = [1 << i for i in range(lax.axis_size("seq").bit_length() - 1)]
    rows = total.shape[0]
    extra = -rows % (2 * lax.axis_size("seq"))
    if extra:
        total = jnp.pad(total, ((0, extra), (0, 0)))
    middle = total.shape[0] // 2
    done = []
    for part, order in ((total[:middle], masks), (total[middle:], masks[1:] + masks[:1])):
        for mask in order:
            part = halve(part, mask)
        for mask in reversed(order):
            part = double(part, mask)
        done.append(part)
    return jnp.concatenate(done, axis=0)[:rows]


def seq_sum(values):
    mask = 1
    while mask < lax.axis_size("seq"):
        values = values + exchange(values, mask, 0)
        mask *= 2
    return values


def reduce_small(mid, small):
    mine = jnp.concatenate([m[0].reshape(-1) for m in mid])
    theirs = jnp.concatenate([m[1].reshape(-1) for m in mid])
    every = jnp.concatenate([s.reshape(-1) for s in small])
    count, extra = every.shape[0], mine.shape[0]
    pad = -(count + extra) % 1024
    got = exchange(jnp.pad(jnp.concatenate([every, theirs]), (0, pad)), 0, 2)
    total = jnp.pad(jnp.concatenate([every, mine]), (0, pad)) + got
    total = seq_sum(total)
    every = total[:count]
    every = every + exchange(every, 0, 1)
    mids, at = [], count
    for m in mid:
        mids.append(total[at : at + m[0].size].reshape(m[0].shape))
        at += m[0].size
    smalls, at = [], 0
    for s in small:
        smalls.append(every[at : at + s.size].reshape(s.shape))
        at += s.size
    return mids, smalls


def on_device(
    hidden_in,
    query_weight,
    key_weight,
    value_weight,
    query_bias,
    value_bias,
    out_weight,
    out_bias,
    conv_taps,
    up_weight,
    up_bias,
    down_weight,
    down_bias,
    gain_one,
    shift_one,
    gain_two,
    shift_two,
    out_grad,
    item_lengths,
):
    tok_row = hidden_in.shape[1] * 2
    half = (conv_taps.shape[2] - 1) // 2
    layout = item_layout(item_lengths, tok_row, half)
    q_bias, v_bias, taps, both_up = fetch_small(query_bias, value_bias, conv_taps, up_bias)
    hidden = hidden_in.astype(jnp.float32)
    x_full, pooled = join_pool(hidden, layout)
    weights, pooled = fetch_weights(
        query_weight, key_weight, value_weight, out_weight, up_weight, down_weight, pooled
    )
    params = []
    for i in range(2):
        params.append(
            dict(
                weights=weights[i],
                half=half,
                offload=i == 1,
                q_bias=q_bias[i],
                v_bias=v_bias[i],
                lines=tap_lines(taps[i]),
                up_bias=both_up[i] if i == 1 else up_bias[:1],
                out_bias=out_bias[i],
                down_bias=down_bias[i],
                gain_one=gain_one[i],
                shift_one=shift_one[i],
                gain_two=gain_two[i],
                shift_two=shift_two[i],
            )
        )
    kept = [None, None]
    for i in range(2):
        joined = (x_full, pooled) if i == 0 else join_pool(hidden, layout)
        ahead = weights[1] if i == 0 else None
        hidden, kept[i] = layer_forward(hidden, params[i], layout, joined, ahead)
    grad = out_grad
    big, mid, small = [None, None], [None, None], [None, None]
    pending = None
    for i in (1, 0):
        grad, grads, mid[i], small[i] = layer_backward(grad, kept[i], params[i], layout, pending)
        if i == 1:
            attn_grad, ffn_grad = grads
            grad, ffn_grad = tied(grad, ffn_grad)
            pending = [seq_gather(across_pick(ffn_grad)), attn_grad]
        else:
            attn_grad, (ffn_one, packed) = grads
            packed = jnp.concatenate([across_pick(packed[:2])[None], packed[2:]], axis=0)
            packed = lax.all_gather(packed, "seq", axis=1, tiled=True)
            big[0] = (reduce_big(attn_grad), packed[1:].reshape(-1, packed.shape[2]))
            big[1] = (packed[0], ffn_one)
    mids, smalls = reduce_small(
        [[jnp.stack(m) for m in zip(*pairs)] for pairs in zip(*mid)],
        [jnp.stack(pair) for pair in zip(*small)],
    )
    width = query_weight.shape[2]
    attn = jnp.stack([big[0][0], big[1][0]]).reshape(2, 4, width, -1)
    qkv = [jnp.swapaxes(attn[:, i], 1, 2).astype(jnp.float32) for i in range(3)]
    outs = attn[:, 3].astype(jnp.float32)
    both = [big[0][1], big[1][1]]
    rows = up_weight.shape[1]
    ups = jnp.stack([one[:rows] for one in both]).astype(jnp.float32)
    downs = jnp.stack([one[rows:] for one in both]).astype(jnp.float32)
    return (
        hidden.astype(LOW),
        grad,
        qkv[0],
        qkv[1],
        qkv[2],
        mids[0],
        mids[1],
        outs,
        smalls[0],
        mids[2].reshape(conv_taps.shape),
        ups,
        mids[3],
        downs,
        smalls[1],
        smalls[2],
        smalls[3],
        smalls[4],
        smalls[5],
    )


def solution(mesh):
    placed = (
        P(None, ("seq", "head"), None),
        P(None, None, "head"),
        P(None, None, "head"),
        P(None, None, "head"),
        P(None, "head"),
        P(None, "head"),
        P(None, "head", None),
        P(),
        P(None, "head", None),
        P(None, None, "head"),
        P(None, "head"),
        P(None, "head", None),
        P(),
        P(),
        P(),
        P(),
        P(),
        P(None, ("seq", "head"), None),
        P(),
    )
    return jax.shard_map(
        on_device,
        mesh=mesh,
        in_specs=placed,
        out_specs=(
            P(None, ("seq", "head"), None),
            P(None, ("seq", "head"), None),
            P(None, None, "head"),
            P(None, None, "head"),
            P(None, None, "head"),
            P(None, "head"),
            P(None, "head"),
            P(None, "head", None),
            P(),
            P(None, "head", None),
            P(None, None, "head"),
            P(None, "head"),
            P(None, "head", None),
            P(),
            P(),
            P(),
            P(),
            P(),
        ),
        check_vma=False,
    )
```

```python
import functools

import jax
import jax.numpy as jnp
from jax import lax
from jax.experimental import pallas as pl
from jax.experimental.pallas import tpu as pltpu
from jax.sharding import PartitionSpec as P

LANDMARKS = 64
NS_STEPS = 6


HIGHEST = lax.Precision.HIGHEST
EPSILON = 1e-05
FLOOR_TOP = -1e30
LOW = jnp.bfloat16
GROUP = ((0, 2), (1, 0), (1, 2))


def layer_norm(values, gain, offset):
    centred = values - jnp.mean(values, axis=-1, keepdims=True)
    variance = jnp.mean(centred * centred, axis=-1, keepdims=True)
    return centred * lax.rsqrt(variance + EPSILON) * gain + offset


def exchange(values, seq_mask, head_mask):
    if seq_mask == 0:
        count = lax.axis_size("head")
        return lax.ppermute(values, "head", [(i, i ^ head_mask) for i in range(count)])
    if head_mask == 0:
        count = lax.axis_size("seq")
        return lax.ppermute(values, "seq", [(i, i ^ seq_mask) for i in range(count)])
    heads = lax.axis_size("head")
    route = []
    for s in range(lax.axis_size("seq")):
        for h in range(heads):
            route.append((s * heads + h, (s ^ seq_mask) * heads + (h ^ head_mask)))
    return lax.ppermute(values, ("seq", "head"), route)


def rank_shift(values, step):
    heads = lax.axis_size("head")
    ranks = lax.axis_size("seq") * (heads // 2)
    route = []
    for rank in range(ranks):
        target = rank + step
        if 0 <= target < ranks:
            for core in range(2):
                source_dev = (rank // 2) * heads + (rank % 2) * 2 + core
                target_dev = (target // 2) * heads + (target % 2) * 2 + core
                route.append((source_dev, target_dev))
    return lax.ppermute(values, ("seq", "head"), route)


def place():
    seq = lax.axis_index("seq")
    head = lax.axis_index("head")
    return seq, head // 2, head % 2


def pair_join(values, axis):
    core = place()[2]
    other = exchange(values, 0, 1)
    low = jnp.where(core == 0, values, other)
    high = jnp.where(core == 0, other, values)
    return jnp.concatenate([low, high], axis=axis)


def pair_collect(terms):
    core = place()[2]
    half = terms.shape[1] // 2
    low, high = terms[:, :half], terms[:, half:]
    mine = jnp.where(core == 0, low, high)
    theirs = jnp.where(core == 0, high, low).astype(jnp.bfloat16)
    return mine + exchange(theirs, 0, 1).astype(jnp.float32)


def group_index():
    seq, across, core = place()
    return across + 2 * (seq % 2)


def upper_levels():
    levels = (lax.axis_size("seq") // 2).bit_length() - 1
    return [(low, min(2, levels - low)) for low in range(0, levels, 2)]


def nn(one, two, precision=None):
    return lax.dot_general(
        one, two, (((1,), (0,)), ((), ())), precision, preferred_element_type=jnp.float32
    )


def nt(one, two, precision=None):
    return lax.dot_general(
        one, two, (((1,), (1,)), ((), ())), precision, preferred_element_type=jnp.float32
    )


def tn(one, two, precision=None):
    return lax.dot_general(
        one, two, (((0,), (0,)), ((), ())), precision, preferred_element_type=jnp.float32
    )


def on_core(kernel, outs, scalars, *arrays, us=1):
    shapes = tuple(jax.ShapeDtypeStruct(shape, dtype) for shape, dtype in outs)
    specs = [pl.BlockSpec(memory_space=pltpu.SMEM)] if scalars is not None else []
    specs += [pl.BlockSpec(memory_space=pltpu.VMEM)] * len(arrays)
    given = ((scalars,) if scalars is not None else ()) + arrays
    return pl.pallas_call(
        kernel,
        out_shape=shapes,
        in_specs=specs,
        out_specs=tuple(pl.BlockSpec(memory_space=pltpu.VMEM) for _ in outs),
        compiler_params=pltpu.CompilerParams(vmem_limit_bytes=48 * 1024 * 1024),
        cost_estimate=pl.CostEstimate(
            flops=us * 10**9, bytes_accessed=us * 3 * 10**6, transcendentals=0
        ),
    )(*given)


def tokens_of(row, tok_row):
    return pl.ds(pl.multiple_of(row * tok_row, tok_row), tok_row)


def lanes(shape):
    return lax.broadcasted_iota(jnp.int32, shape, len(shape) - 1)


def join_pool_kernel(spot, own, other, pool, full, one, two, three, four):
    rows, piece, model = own.shape
    tok_row = 2 * piece
    core = spot[1]
    half = model // 2
    for row in range(rows):
        mine = pl.multiple_of(row * tok_row + core * piece, piece)
        theirs = pl.multiple_of(row * tok_row + (1 - core) * piece, piece)
        full[pl.ds(mine, piece), :] = own[row]
        full[pl.ds(theirs, piece), :] = other[row]
    side = pl.ds(pl.multiple_of(core * half, half), half)
    for step, out in enumerate((one, two, three, four)):
        row = spot[0] ^ step
        block = full[tokens_of(row, tok_row), side]
        out[...] = nn(pool[row], block).astype(LOW)


def rim_blocks(block_of, rows, tok_row, half):
    low, high = None, None
    for row in range(rows):
        block = block_of(row).astype(jnp.float32)
        lane = lanes(block.shape)
        first = block if row == 0 else pltpu.roll(block, row * half, 1)
        shift = (row * half + half) % tok_row
        last = block if shift == 0 else pltpu.roll(block, shift, 1)
        inside = lane // half == row
        low = jnp.where(inside, first, 0.0 if low is None else low)
        high = jnp.where(inside, last, 0.0 if high is None else high)
    return low.astype(LOW), high.astype(LOW)


def far_kernel(half, spot, qkv, land, one, two, three, four, low, high):
    width = qkv.shape[0] // 3
    head_dim = LANDMARKS
    heads = width // head_dim
    tok_row = qkv.shape[1] // 4
    scale = head_dim ** (-0.5)
    for step, out in enumerate((one, two, three, four)):
        here = tokens_of(spot[0] ^ step, tok_row)
        logs = jnp.zeros((LANDMARKS, out.shape[1] - width), jnp.float32)
        lane = lanes(logs.shape)
        for head in range(heads):
            cols = slice(head * head_dim, (head + 1) * head_dim)
            keys = qkv[width + head * head_dim : width + (head + 1) * head_dim, here]
            values = qkv[2 * width + head * head_dim : 2 * width + (head + 1) * head_dim, here]
            land_q = land[step * LANDMARKS : (step + 1) * LANDMARKS, cols]
            scores = nn(land_q, keys) * scale
            top = jnp.max(scores, axis=1, keepdims=True)
            grown = jnp.exp(scores - top)
            total = jnp.sum(grown, axis=1, keepdims=True)
            out[:, cols] = nt(grown.astype(LOW), values) / total
            logs = jnp.where(lane == head, top + jnp.log(total), logs)
        out[:, width:] = logs
    low[...], high[...] = rim_blocks(
        lambda row: qkv[2 * width :, row * tok_row : (row + 1) * tok_row], 4, tok_row, half
    )


def merged(flags, pieces, width):
    head_dim = LANDMARKS
    mixes, logs = [], []
    for head in range(width // head_dim):
        cols = slice(head * head_dim, (head + 1) * head_dim)
        column = slice(width + head, width + head + 1)
        log = [pieces[0][:, column]]
        for index, piece in enumerate(pieces[1:]):
            log.append(jnp.where(flags[index] > 0, piece[:, column], FLOOR_TOP))
        top = functools.reduce(jnp.maximum, log)
        shares = [jnp.exp(value - top) for value in log]
        total = functools.reduce(jnp.add, shares)
        mix = sum(share * piece[:, cols] for share, piece in zip(shares, pieces))
        mixes.append(mix / total)
        logs.append(top + jnp.log(total))
    return mixes, logs


def merge_kernel(count, flags, *refs):
    out = refs[count]
    width = out.shape[1] - 128
    mixes, logs = merged(flags, refs[:count], width)
    packed = jnp.zeros((LANDMARKS, 128), jnp.float32)
    lane = lanes(packed.shape)
    for head, (mix, log) in enumerate(zip(mixes, logs)):
        out[:, head * LANDMARKS : (head + 1) * LANDMARKS] = mix
        packed = jnp.where(lane == head, log, packed)
    out[:, width:] = packed


def packed_parts(columns):
    packed = jnp.zeros((LANDMARKS, 128), jnp.float32)
    lane = lanes(packed.shape)
    for head, column in enumerate(columns):
        for part in range(3):
            rounded = column.astype(LOW).astype(jnp.float32)
            packed = jnp.where(lane == head + 8 * part, rounded, packed)
            column = column - rounded
    return packed.astype(LOW)


def unpacked_part(packed, head):
    packed = packed.astype(jnp.float32)
    return (
        packed[:, head : head + 1]
        + packed[:, head + 8 : head + 9]
        + packed[:, head + 16 : head + 17]
    )


def land_out_kernel(count, flags, *refs):
    inverse, out, weighted = refs[count:]
    width = weighted.shape[1]
    mixes, logs = merged(flags, refs[:count], width)
    for head, mix in enumerate(mixes):
        cols = slice(head * LANDMARKS, (head + 1) * LANDMARKS)
        weighted[:, cols] = mix
        out[:, cols] = nn(inverse[head], mix, HIGHEST).astype(LOW)
    out[:, width:] = packed_parts(logs)


def inverse_kernel(land, amats, inverses, products, seconds, thirds):
    width = land.shape[1] // 2
    heads = width // LANDMARKS
    scale = LANDMARKS ** (-0.5)
    shape = (LANDMARKS, LANDMARKS)
    rows = lax.broadcasted_iota(jnp.int32, shape, 0)
    eye = (rows == lanes(shape)).astype(jnp.float32)
    matrices, iterates = [], []
    for head in range(heads):
        cols = slice(head * LANDMARKS, (head + 1) * LANDMARKS)
        keys = slice(width + head * LANDMARKS, width + (head + 1) * LANDMARKS)
        scores = nt(land[:LANDMARKS, cols], land[:LANDMARKS, keys]) * scale
        grown = jnp.exp(scores - jnp.max(scores, axis=1, keepdims=True))
        matrix = grown / jnp.sum(grown, axis=1, keepdims=True)
        columns = jnp.sum(matrix, axis=0, keepdims=True)
        square = columns * columns
        fourth = square * square
        bound = jnp.sum(fourth * fourth, axis=1, keepdims=True)
        bound = jnp.exp(jnp.log(bound) * 0.125)
        amats[head] = matrix
        matrices.append(matrix)
        iterates.append(matrix.T / bound)
    for step in range(NS_STEPS):
        product = [nn(a, z, HIGHEST) for a, z in zip(matrices, iterates)]
        inner = [nn(p, 7.0 * eye - p, HIGHEST) for p in product]
        second = [15.0 * eye - value for value in inner]
        third = [13.0 * eye - nn(p, m, HIGHEST) for p, m in zip(product, second)]
        for head in range(heads):
            inverses[step * heads + head] = iterates[head]
            products[step * heads + head] = product[head]
            seconds[step * heads + head] = second[head]
            thirds[step * heads + head] = third[head]
        iterates = [0.25 * nn(z, m, HIGHEST) for z, m in zip(iterates, third)]
    for head in range(heads):
        inverses[NS_STEPS * heads + head] = iterates[head]


def band_blocks(line, tok_row, half):
    span = line.shape[1]
    wide = jnp.broadcast_to(line, (tok_row, span))
    middle = pltpu.roll(wide, 0, 1, stride=1, stride_axis=0)[:, :tok_row]
    short = jnp.broadcast_to(line, (half, span))
    low = pltpu.roll(short, span - half, 1, stride=1, stride_axis=0)[:, :tok_row]
    high = pltpu.roll(short, tok_row, 1, stride=1, stride_axis=0)[:, :tok_row]
    reps = tok_row // half
    return [
        part.astype(LOW)
        for part in (middle, jnp.concatenate([low] * reps, 0), jnp.concatenate([high] * reps, 0))
    ]


def near_kernel(half, spot, qkv, low, high, rims, land, one, two, three, four, line, out):
    width = qkv.shape[0] // 3
    tok_row = qkv.shape[1] // 4
    head_dim = LANDMARKS
    scale = head_dim ** (-0.5)
    low_all = low[...].astype(jnp.float32) * rims[0:1, :]
    high_all = high[...].astype(jnp.float32) * rims[1:2, :]
    lane = lanes((head_dim, tok_row)) // half
    bands = [band_blocks(line[h : h + 1, :], tok_row, half) for h in range(width // head_dim)]
    for step, mixed in enumerate((one, two, three, four)):
        row = spot[0] ^ step
        here = tokens_of(row, tok_row)
        land_rows = slice(step * LANDMARKS, (step + 1) * LANDMARKS)
        for head in range(width // head_dim):
            cols = slice(head * head_dim, (head + 1) * head_dim)
            keys = slice(width + head * head_dim, width + (head + 1) * head_dim)
            queries = qkv[cols, here]
            scores = nn(land[land_rows, keys], queries) * scale
            grown = jnp.exp(scores - jnp.max(scores, axis=0, keepdims=True))
            probs = grown / jnp.sum(grown, axis=0, keepdims=True)
            total = tn(mixed[:, cols], probs.astype(LOW))
            values = qkv[2 * width + head * head_dim : 2 * width + (head + 1) * head_dim, here]
            total = total + nn(values, bands[head][0])
            mine = lane == row
            total = total + nn(jnp.where(mine, low_all[cols, :], 0.0).astype(LOW), bands[head][1])
            total = total + nn(jnp.where(mine, high_all[cols, :], 0.0).astype(LOW), bands[head][2])
            out[cols, here] = total.astype(LOW)


def near_back_kernel(half, spot, qkv, grads, land, *refs):
    mixes, queries_out = refs[:4], refs[4]
    land_outs, land_keys, low, high = refs[5:9], refs[9:13], refs[13], refs[14]
    width = qkv.shape[0] // 3
    tok_row = qkv.shape[1] // 4
    head_dim = LANDMARKS
    scale = head_dim ** (-0.5)
    for step in range(4):
        here = tokens_of(spot[0] ^ step, tok_row)
        land_rows = slice(step * LANDMARKS, (step + 1) * LANDMARKS)
        for head in range(width // head_dim):
            cols = slice(head * head_dim, (head + 1) * head_dim)
            keys = slice(width + head * head_dim, width + (head + 1) * head_dim)
            queries = qkv[cols, here]
            land_k = land[land_rows, keys]
            scores = nn(land_k, queries) * scale
            grown = jnp.exp(scores - jnp.max(scores, axis=0, keepdims=True))
            probs = grown / jnp.sum(grown, axis=0, keepdims=True)
            grad = grads[cols, here]
            grad_probs = nn(mixes[step][:, cols], grad)
            inner = jnp.sum(grad_probs * probs, axis=0, keepdims=True)
            grad_scores = (probs * (grad_probs - inner) * scale).astype(LOW)
            queries_out[cols, here] = tn(land_k, grad_scores)
            land_keys[step][:, cols] = nt(grad_scores, queries).astype(LOW)
            land_outs[step][:, cols] = nt(probs.astype(LOW), grad).astype(LOW)
    low[...], high[...] = rim_blocks(
        lambda row: grads[:, row * tok_row : (row + 1) * tok_row], 4, tok_row, half
    )


def conv_back_kernel(half, qkv, grads, low, high, grad_low, grad_high, rims, line, out, taps):
    width = qkv.shape[0] // 3
    tok_row = qkv.shape[1] // 4
    head_dim = LANDMARKS
    span = line.shape[1]
    low_all = low[...].astype(jnp.float32) * rims[0:1, :]
    high_all = high[...].astype(jnp.float32) * rims[1:2, :]
    grad_low_all = grad_low[...].astype(jnp.float32) * rims[0:1, :]
    grad_high_all = grad_high[...].astype(jnp.float32) * rims[1:2, :]
    lane = lanes((head_dim, tok_row)) // half
    square = (tok_row, tok_row)
    turned = (lax.broadcasted_iota(jnp.int32, square, 0) + lanes(square) == tok_row - 1).astype(LOW)
    wide = lanes((tok_row, span))
    for head in range(width // head_dim):
        cols = slice(head * head_dim, (head + 1) * head_dim)
        bands = band_blocks(line[head : head + 1, :], tok_row, half)
        fields = [jnp.zeros(square, jnp.float32) for _ in range(3)]
        for row in range(4):
            here = slice(row * tok_row, (row + 1) * tok_row)
            mine = lane == row

            def rim(block):
                return jnp.where(mine, block[cols, :], 0.0).astype(LOW)

            grad = grads[cols, here]
            values = qkv[2 * width + head * head_dim : 2 * width + (head + 1) * head_dim, here]
            total = nn(grad, bands[0]) + nn(rim(grad_low_all), bands[1])
            out[cols, here] = total + nn(rim(grad_high_all), bands[2])
            backward = nn(grad, turned).astype(LOW)
            for index, block in enumerate((values, rim(low_all), rim(high_all))):
                fields[index] = fields[index] + tn(backward, block)
        ends = []
        for field in fields[1:]:
            folded = field + pltpu.roll(field, 2 * half, 1)
            folded = folded + pltpu.roll(folded, half, 1)
            ends.append(jnp.concatenate([folded, folded], axis=1))
        whole = jnp.concatenate([fields[0], jnp.zeros(square, jnp.float32)], axis=1)
        whole = pltpu.roll(whole, half, 1)
        whole = jnp.where(wide < half, ends[0], whole)
        right = (wide >= half + tok_row) & (wide < 2 * half + tok_row)
        whole = jnp.where(right, ends[1], whole)
        whole = pltpu.roll(whole, span - tok_row + 1, 1, stride=1, stride_axis=0)
        taps[head : head + 1, :] = jnp.sum(whole, axis=0, keepdims=True)[:, :128]


def mixture_grad_kernel(grads, inverse, weighted, out):
    width = grads.shape[1]
    inner = []
    for head in range(width // LANDMARKS):
        cols = slice(head * LANDMARKS, (head + 1) * LANDMARKS)
        value = tn(inverse[head], grads[:, cols], HIGHEST).astype(LOW)
        out[:, cols] = value
        product = value.astype(jnp.float32) * weighted[:, cols]
        inner.append(jnp.sum(product, axis=1, keepdims=True))
    out[:, width:] = packed_parts(inner)


def inverse_back_kernel(
    grads, weighted, land, amats, inverses, products, seconds, thirds, out
):
    width = grads.shape[1]
    heads = width // LANDMARKS
    scale = LANDMARKS ** (-0.5)
    shape = (LANDMARKS, LANDMARKS)
    rows = lax.broadcasted_iota(jnp.int32, shape, 0)
    eye = (rows == lanes(shape)).astype(jnp.float32)
    every = range(heads)
    columns = [slice(head * LANDMARKS, (head + 1) * LANDMARKS) for head in every]
    grad = [nt(grads[:, c], weighted[:, c], HIGHEST) for c in columns]
    matrices = [amats[head] for head in every]
    total = [jnp.zeros(shape, jnp.float32) for _ in every]
    for step in reversed(range(NS_STEPS)):
        z = [inverses[step * heads + head] for head in every]
        p = [products[step * heads + head] for head in every]
        m2 = [seconds[step * heads + head] for head in every]
        m3 = [thirds[step * heads + head] for head in every]
        g3 = [-0.25 * tn(z[i], grad[i], HIGHEST) for i in every]
        gz = [0.25 * nt(grad[i], m3[i], HIGHEST) for i in every]
        g2 = [-tn(p[i], g3[i], HIGHEST) for i in every]
        gp = [nt(g3[i], m2[i], HIGHEST) for i in every]
        g1 = [tn(p[i], g2[i], HIGHEST) for i in every]
        gp = [gp[i] + nt(g2[i], 7.0 * eye - p[i], HIGHEST) - g1[i] for i in every]
        total = [total[i] + nt(gp[i], z[i], HIGHEST) for i in every]
        grad = [gz[i] + tn(matrices[i], gp[i], HIGHEST) for i in every]
    for head in every:
        matrix = matrices[head]
        sums = jnp.sum(matrix, axis=0, keepdims=True)
        square = sums * sums
        fourth = square * square
        bound = jnp.sum(fourth * fourth, axis=1, keepdims=True)
        bound = jnp.exp(jnp.log(bound) * 0.125)
        first = inverses[head]
        lost = jnp.sum(grad[head] * first, axis=1, keepdims=True)
        lost = -jnp.sum(lost, axis=0, keepdims=True) / bound
        ratio = sums / bound
        cube = ratio * ratio * ratio
        value = total[head] + grad[head].T / bound + lost * (cube * cube * ratio)
        inner = jnp.sum(value * matrix, axis=1, keepdims=True)
        scores = matrix * (value - inner) * scale
        keys = slice(width + head * LANDMARKS, width + (head + 1) * LANDMARKS)
        land_q = land[:LANDMARKS, columns[head]].astype(jnp.float32)
        land_k = land[:LANDMARKS, keys].astype(jnp.float32)
        out[:, columns[head]] = nn(scores, land_k, HIGHEST)
        out[:, keys] = tn(scores, land_q, HIGHEST)


def far_back_kernel(spot, qkv, land, conv, *refs):
    mixes, grads, near_keys = refs[:4], refs[4:8], refs[8:12]
    keys_out, values_out, parts = refs[12], refs[13], refs[14:18]
    width = qkv.shape[0] // 3
    tok_row = qkv.shape[1] // 4
    head_dim = LANDMARKS
    scale = head_dim ** (-0.5)
    for step in range(4):
        here = tokens_of(spot[0] ^ step, tok_row)
        land_rows = slice(step * LANDMARKS, (step + 1) * LANDMARKS)
        for head in range(width // head_dim):
            cols = slice(head * head_dim, (head + 1) * head_dim)
            keys = qkv[width + head * head_dim : width + (head + 1) * head_dim, here]
            values = qkv[2 * width + head * head_dim : 2 * width + (head + 1) * head_dim, here]
            land_q = land[land_rows, cols]
            log = unpacked_part(mixes[step][:, width:], head)
            inner = unpacked_part(grads[step][:, width:], head)
            probs = jnp.exp(nn(land_q, keys) * scale - log)
            grad = grads[step][:, cols]
            scores = (probs * (nn(grad, values) - inner) * scale).astype(LOW)
            parts[step][:, cols] = nt(scores, keys).astype(LOW)
            keys_out[cols, here] = tn(land_q, scores)
            values_out[cols, here] = (conv[cols, here] + tn(grad, probs.astype(LOW))).astype(LOW)
        parts[step][:, width:] = near_keys[step][...]


def token_grad_kernel(spot, near, far, values, pool, one, two, three, four, out):
    width = near.shape[0]
    tok_row = near.shape[1] // 4
    for step, grads in enumerate((one, two, three, four)):
        row = spot[0] ^ step
        here = tokens_of(row, tok_row)
        share = pool[row]
        out[:width, here] = (near[:, here] + tn(grads[:, :width], share)).astype(LOW)
        out[width : 2 * width, here] = (far[:, here] + tn(grads[:, width:], share)).astype(LOW)
    out[2 * width :, :] = values[...]


def send_rows(pieces):
    got = [exchange(piece, s, h) for piece, (s, h) in zip(pieces[1:], GROUP)]
    return [pieces[0]] + got


def spread_row(row):
    return [row] + [exchange(row, s, h) for s, h in GROUP]


def item_sum(pieces, layout, beside=None):
    return item_total(send_rows(pieces), layout, beside)


def item_total(pieces, layout, beside=None):
    span = layout["span"]
    dtype = pieces[0].dtype
    pieces = [piece.astype(jnp.float32) for piece in pieces]
    total = (pieces[0] + pieces[1]) + (pieces[2] + pieces[3])
    if beside is not None:
        beside, total = tied(beside, total)
        beside = exchange(beside, 0, 2)
    for low, bits in upper_levels():
        sent = total.astype(dtype)
        near = exchange(sent, 2 << low, 0).astype(jnp.float32)
        pair = total + jnp.where(span > 4 << low, near, 0.0)
        if bits == 2:
            far = exchange(sent, 4 << low, 0).astype(jnp.float32)
            cross = exchange(sent, 6 << low, 0).astype(jnp.float32)
            pair = pair + jnp.where(span > 8 << low, far + cross, 0.0)
        total = pair
    if beside is not None:
        beside, total = tied(beside, total)
        return total, beside
    return total


def land_mixture(pieces, inverse, layout):
    span = layout["span"]
    width = pieces[0].shape[1] - 128
    pieces = send_rows(pieces)
    flags = jnp.ones((3,), jnp.int32)
    for low, bits in upper_levels():
        call = functools.partial(merge_kernel, len(pieces))
        (row,) = on_core(call, [(pieces[0].shape, jnp.float32)], flags, *pieces)
        pieces = [row] + [exchange(row, m << (low + 1), 0) for m in range(1, 1 << bits)]
        wide = (span > 8 << low).astype(jnp.int32)
        flags = jnp.stack([(span > 4 << low).astype(jnp.int32), wide, wide])
    outs = [(pieces[0].shape, LOW), ((LANDMARKS, width), jnp.float32)]
    call = functools.partial(land_out_kernel, len(pieces))
    return on_core(call, outs, flags, *pieces, inverse)


def item_layout(item_lengths, tok_row, half):
    seq, across, core = place()
    rank = seq * 2 + across
    ends = jnp.cumsum(item_lengths, axis=1)
    starts = ends - item_lengths
    first_token = rank * tok_row
    chosen = (starts <= first_token) & (first_token < ends)
    length = jnp.sum(jnp.where(chosen, item_lengths, 0), axis=1)
    begin = jnp.sum(jnp.where(chosen, starts, 0), axis=1)
    segment = length // LANDMARKS
    first_rank = begin // tok_row
    spans = length // tok_row
    positions = first_token + jnp.arange(tok_row)
    marks = (positions[None, :] - begin[:, None]) // segment[:, None]
    hits = marks[:, None, :] == jnp.arange(LANDMARKS)[None, :, None]
    share = 1.0 / segment.astype(jnp.float32)
    pool = jnp.where(hits, share[:, None, None], 0.0).astype(LOW)
    left_open = rank > first_rank
    right_open = rank + 1 < first_rank + spans
    rims = jnp.repeat(jnp.stack([left_open, right_open]).astype(jnp.float32), half, axis=1)
    me = group_index()
    return dict(
        span=lax.dynamic_index_in_dim(spans, me, 0, keepdims=False),
        pool=pool,
        rims=jnp.pad(rims, ((0, 6), (0, 0))),
        spot=jnp.stack([me, core]).astype(jnp.int32),
    )


def dot(spec, one, two):
    return jnp.einsum(spec, one, two, preferred_element_type=jnp.float32)


def ordered(mine, other, axis):
    across = place()[1]
    low = jnp.where(across == 0, mine, other)
    high = jnp.where(across == 0, other, mine)
    return jnp.stack([low, high], axis=axis)


def fetch_small(query_bias, value_bias, conv_taps, up_bias):
    layers = query_bias.shape[0]
    flat = [a.reshape(layers, -1) for a in (query_bias, value_bias, conv_taps, up_bias)]
    sizes = [a.shape[1] for a in flat]
    packed = jnp.concatenate(flat, axis=1)
    other = exchange(jnp.pad(packed, ((0, 0), (0, -packed.shape[1] % 128))), 0, 2)
    rest, at = [], 0
    for size in sizes:
        rest.append(other[:, at : at + size])
        at += size
    heads = conv_taps.shape[1]
    q_bias = ordered(query_bias, rest[0], 1).reshape(layers, -1)
    v_bias = ordered(value_bias, rest[1], 1).reshape(layers, -1)
    taps = ordered(conv_taps, rest[2].reshape(conv_taps.shape), 1).reshape(layers, 2 * heads, -1)
    return q_bias, v_bias, taps, ordered(up_bias, rest[3], 1)


def across_gather(values):
    return lax.all_gather(values, "head", axis=0, axis_index_groups=[[0, 2], [1, 3]])


def fetch_weights(
    query_weight, key_weight, value_weight, out_weight, up_weight, down_weight, pooled
):
    model = up_weight.shape[1]
    packs = [
        jnp.concatenate([query_weight[i].T, key_weight[i].T, value_weight[i].T], 0)
        for i in range(2)
    ]
    pack, *pooled = tied(packs[0], *pooled)
    other = exchange(pack, 0, 2)
    own_out, other = tied(out_weight[0], other)
    other_out = exchange(own_out, 0, 2)
    held = jnp.concatenate([packs[1], out_weight[1]], 0)
    held, other = tied(held, other)
    first = ordered(pack.reshape(3, -1, model), other.reshape(3, -1, model), 1)
    layers = [
        dict(
            qkv=first.reshape(-1, model),
            out=ordered(own_out, other_out, 0).reshape(-1, model),
            up=up_weight[:1],
            down=down_weight[:1],
        ),
        dict(
            attn=jnp.swapaxes(across_gather(held).reshape(2, 4, -1, model), 0, 1),
            up=across_gather(up_weight[1]),
            down=across_gather(down_weight[1]),
        ),
    ]
    return layers, pooled


def tap_lines(taps):
    count = taps.shape[1]
    half = (count - 1) // 2
    gap = jnp.zeros((taps.shape[0], 256 - count), jnp.float32)
    flipped = taps[:, ::-1]
    lines = [jnp.concatenate([t[:, half:], gap, t[:, :half]], axis=1) for t in (flipped, taps)]
    pad = -taps.shape[0] % 8
    return [jnp.pad(line, ((0, pad), (0, 0))) for line in lines]


def token_sets(values, own_pair):
    own = pair_join(values, 1)
    flat = (own.shape[0] * own.shape[1], own.shape[2])
    if own_pair:
        return [own.reshape(flat)]
    return [own.reshape(flat), pair_join(exchange(values, 0, 2), 1).reshape(flat)]


def collect_sets(terms, rows):
    terms = [term.reshape(rows, -1, term.shape[-1]) for term in terms]
    total = pair_collect(terms[0])
    if len(terms) == 2:
        total = total + exchange(pair_collect(terms[1]).astype(LOW), 0, 2).astype(jnp.float32)
    return total


def join_pool(hidden, layout):
    batch_rows, piece, model = hidden.shape
    quarter = [((LANDMARKS, model // 2), LOW)] * 4
    x_low = hidden.astype(LOW)
    x_full, *pooled = on_core(
        join_pool_kernel,
        [((batch_rows * 2 * piece, model), LOW)] + quarter,
        layout["spot"],
        x_low,
        exchange(x_low, 0, 1),
        layout["pool"],
    )
    return x_full, send_rows(pooled)


def layer_forward(hidden, params, layout, joined, ahead=None):
    weights = params["weights"]
    if params["offload"]:
        attn = weights["attn"].reshape(-1, hidden.shape[2])
        weights["qkv"] = attn[: attn.shape[0] * 3 // 4]
        weights["out"] = attn[attn.shape[0] * 3 // 4 :]
    spot = layout["spot"]
    batch_rows, piece, model = hidden.shape
    tok_row = 2 * piece
    tokens = batch_rows * tok_row
    width = weights["out"].shape[0]
    half = params["half"]
    x_full, pooled = joined
    if params["offload"]:
        weights["up"], *pooled = tied(weights["up"], *pooled)
    pooled = jnp.concatenate(spread_row(item_total(pooled, layout).astype(LOW)), axis=0)
    pooled = pair_join(pooled, 1)
    bias_q, bias_v = params["q_bias"], params["v_bias"]
    no_bias = jnp.zeros_like(bias_q)
    column = jnp.concatenate([bias_q, no_bias, bias_v])[:, None]
    qkv = (nt(weights["qkv"], x_full) + column).astype(LOW)
    land = nt(pooled, weights["qkv"][: 2 * width]) + jnp.concatenate([bias_q, no_bias])
    land = land.astype(LOW)
    heads = width // LANDMARKS
    message = [((LANDMARKS, width + 128), jnp.float32)] * 4
    rim = [((width, batch_rows * half), LOW)] * 2
    *parts, low, high = on_core(
        functools.partial(far_kernel, half), message + rim, spot, qkv, land, us=4
    )
    low, high = rank_shift(high, 1), rank_shift(low, -1)
    square = (LANDMARKS, LANDMARKS)
    steps = ((NS_STEPS * heads,) + square, jnp.float32)
    own_land = land[:LANDMARKS]
    chain = on_core(
        inverse_kernel,
        [
            ((heads,) + square, jnp.float32),
            (((NS_STEPS + 1) * heads,) + square, jnp.float32),
            steps,
            steps,
            steps,
        ],
        None,
        own_land,
        us=5,
    )
    inverse = chain[1][NS_STEPS * heads :]
    own_out, weighted = land_mixture(parts, inverse, layout)
    if params["offload"]:
        own_out, weights["down"] = tied(own_out, weights["down"])
    mixes = spread_row(own_out)
    (att_low,) = on_core(
        functools.partial(near_kernel, half),
        [((width, tokens), LOW)],
        spot,
        qkv,
        low,
        high,
        layout["rims"],
        land,
        *mixes,
        params["lines"][0],
        us=3,
    )
    terms = tn(att_low, weights["out"]).reshape(batch_rows, tok_row, model)
    if ahead is not None:
        terms, ahead["attn"] = tied(terms, ahead["attn"])
    resid_one = hidden + (pair_collect(terms) + params["out_bias"])
    normed = layer_norm(resid_one, params["gain_one"], params["shift_one"])
    h_sets = token_sets(normed.astype(LOW), params["offload"])
    gelu_low, slopes, terms = [], [], []
    for h_full in h_sets:
        up_pre = dot("td,gdf->gtf", h_full, weights["up"]) + params["up_bias"][:, None, :]
        area = 0.5 * (1.0 + lax.erf(up_pre * 0.7071067811865476))
        bell = jnp.exp(-0.5 * up_pre * up_pre) * 0.3989422804014327
        gelu_low.append((up_pre * area).astype(LOW))
        slopes.append((area + up_pre * bell).astype(LOW))
        terms.append(dot("gtf,gfd->td", gelu_low[-1], weights["down"]))
    mlp_out = collect_sets(terms, batch_rows) + params["down_bias"]
    resid_two = normed + mlp_out
    result = layer_norm(resid_two, params["gain_two"], params["shift_two"])
    kept = dict(
        x_full=x_full,
        qkv=qkv,
        land=land,
        own_land=own_land,
        rims=(low, high),
        chain=chain,
        inverse=inverse,
        weighted=weighted,
        mixes=mixes,
        att_low=att_low,
        resid_one=resid_one,
        h_sets=h_sets,
        gelu_low=gelu_low,
        slopes=slopes,
        resid_two=resid_two,
    )
    return result, kept


def layer_backward(grad_out, kept, params, layout, pending):
    weights = params["weights"]
    spot = layout["spot"]
    batch_rows, piece, model = grad_out.shape
    tok_row = 2 * piece
    tokens = batch_rows * tok_row
    width = weights["out"].shape[0]
    half = params["half"]
    unused_two, pull_two = jax.vjp(
        layer_norm, kept["resid_two"], params["gain_two"], params["shift_two"]
    )
    grad_two, grad_gain_two, grad_shift_two = pull_two(grad_out)
    grad_mlp = grad_two.astype(LOW)
    grad_down_bias = jnp.sum(grad_mlp.astype(jnp.float32), axis=(0, 1))
    grad_sets = token_sets(grad_mlp, params["offload"])
    grad_ups, terms = [], []
    for grad_set, slope in zip(grad_sets, kept["slopes"]):
        grad_up = dot("td,gfd->gtf", grad_set, weights["down"])
        grad_ups.append((grad_up * slope.astype(jnp.float32)).astype(LOW))
        terms.append(dot("gtf,gdf->td", grad_ups[-1], weights["up"]))
    grad_normed = grad_two + collect_sets(terms, batch_rows)
    down_grad = sum(dot("gtf,td->gfd", g, d) for g, d in zip(kept["gelu_low"], grad_sets))
    up_grad = sum(dot("td,gtf->gdf", h, g) for h, g in zip(kept["h_sets"], grad_ups))
    ffn_grad = jnp.concatenate([up_grad, down_grad], axis=1).astype(LOW)
    grad_up_bias = sum(jnp.sum(g.astype(jnp.float32), axis=1) for g in grad_ups)
    if params["offload"]:
        ffn_grad = seq_scatter(ffn_grad)
        grad_up_bias = sides(grad_up_bias)
    else:
        ffn_one, attn_one = pending
        rows = attn_one.shape[1]
        packed = jnp.stack([attn_one[0], attn_one[1], ffn_grad[0, :rows], ffn_grad[0, rows:]])
        ffn_grad = (ffn_one, seq_scatter(packed))
        grad_up_bias = [grad_up_bias[0], jnp.zeros_like(grad_up_bias[0])]
    unused_one, pull_one = jax.vjp(
        layer_norm, kept["resid_one"], params["gain_one"], params["shift_one"]
    )
    grad_one, grad_gain_one, grad_shift_one = pull_one(grad_normed)
    grad_attn = grad_one.astype(LOW)
    grad_out_bias = jnp.sum(grad_attn.astype(jnp.float32), axis=(0, 1))
    grad_attn_full = pair_join(grad_attn, 1).reshape(tokens, model)
    grad_att = nt(weights["out"], grad_attn_full).astype(LOW)
    qkv, land, mixes = kept["qkv"], kept["land"], kept["mixes"]
    row = [((LANDMARKS, width), LOW)]
    rim = [((width, batch_rows * half), LOW)] * 2
    near_queries, *rest = on_core(
        functools.partial(near_back_kernel, half),
        [((width, tokens), jnp.float32)] + row * 8 + rim,
        spot,
        qkv,
        grad_att,
        land,
        *mixes,
        us=6,
    )
    near_outs, near_keys, (low, high) = rest[:4], rest[4:8], rest[8:]
    low, high = rank_shift(high, 1), rank_shift(low, -1)
    own_grad = item_sum(near_outs, layout)
    (own_mix_grad,) = on_core(
        mixture_grad_kernel,
        [((LANDMARKS, width + 128), LOW)],
        None,
        own_grad,
        kept["inverse"],
        kept["weighted"],
    )
    mix_grads = spread_row(own_mix_grad)
    if pending is not None:
        ffn_one, *mix_grads = tied(ffn_grad[0], *mix_grads)
        ffn_grad = (ffn_one, ffn_grad[1])
    grad_out_weight = nn(kept["att_low"], grad_attn_full)
    conv_grad, tap_grad = on_core(
        functools.partial(conv_back_kernel, half),
        [((width, tokens), jnp.float32), ((8, 128), jnp.float32)],
        None,
        qkv,
        grad_att,
        *kept["rims"],
        low,
        high,
        layout["rims"],
        params["lines"][1],
        us=6,
    )
    far_keys, values_low, *parts = on_core(
        far_back_kernel,
        [((width, tokens), jnp.float32), ((width, tokens), LOW)]
        + [((LANDMARKS, 2 * width), LOW)] * 4,
        spot,
        qkv,
        land,
        conv_grad,
        *mixes,
        *mix_grads,
        *near_keys,
        us=5,
    )
    own_grad, *parts = tied(own_grad, *parts)
    (own_land_grad,) = on_core(
        inverse_back_kernel,
        [((LANDMARKS, 2 * width), jnp.float32)],
        None,
        own_grad,
        kept["weighted"],
        kept["own_land"],
        *kept["chain"],
        us=13,
    )
    if params["offload"]:
        own_land_grad = item_sum(parts, layout) + own_land_grad
    else:
        first_grad = jnp.stack([nn(values_low, kept["x_full"]), grad_out_weight])
        first_mine, first_theirs = split_across(first_grad)
        land_sum, first_got = item_sum(parts, layout, first_theirs.astype(LOW))
        own_land_grad = land_sum + own_land_grad
        first_grad = (first_mine + first_got.astype(jnp.float32)).astype(LOW)
    land_grads = spread_row(own_land_grad.astype(LOW))
    (grad_qkv,) = on_core(
        token_grad_kernel,
        [((3 * width, tokens), LOW)],
        spot,
        near_queries,
        far_keys,
        values_low,
        layout["pool"],
        *land_grads,
    )
    terms = tn(grad_qkv, weights["qkv"]).reshape(batch_rows, tok_row, model)
    grad_hidden = grad_one + pair_collect(terms)
    if params["offload"]:
        grad_weight = nn(grad_qkv, kept["x_full"])
        attn_grad = jnp.concatenate([grad_weight, grad_out_weight], axis=0)
        attn_grad = attn_grad.reshape(4, 2, width // 2, model).astype(LOW)
        attn_grad = jnp.swapaxes(attn_grad, 0, 1).reshape(2, 2 * width, model)
    else:
        grad_weight = nn(grad_qkv[: 2 * width], kept["x_full"]).reshape(2, width, model)
        attn_grad = across_sum(split_across(grad_weight))
        attn_grad, packed = tied(attn_grad, ffn_grad[1])
        ffn_grad = (ffn_grad[0], packed)
        attn_grad = jnp.concatenate([attn_grad, first_grad], axis=0)
    grad_bias = jnp.sum(grad_qkv.astype(jnp.float32), axis=1)
    heads = width // LANDMARKS
    mids = [
        split_flat(grad_bias[:width]),
        split_flat(grad_bias[2 * width :]),
        split_flat(tap_grad[:heads, : 2 * half + 1]),
        grad_up_bias,
    ]
    smalls = [
        grad_out_bias,
        grad_down_bias,
        grad_gain_one,
        grad_shift_one,
        grad_gain_two,
        grad_shift_two,
    ]
    return grad_hidden, (attn_grad, ffn_grad), mids, smalls


def sides(values):
    across = place()[1]
    return [jnp.where(across == 0, values[0], values[1]), jnp.where(across == 0, values[1], values[0])]


def seq_scatter(values):
    return lax.psum_scatter(values, "seq", scatter_dimension=values.ndim - 2, tiled=True)


def seq_gather(values):
    return lax.all_gather(values, "seq", axis=0, tiled=True)


def across_pick(values):
    mine, theirs = sides(values)
    return across_sum([mine.astype(jnp.float32), theirs])


def tied(values, *others):
    return lax.optimization_barrier((values,) + others)


def across_sum(pair):
    mine, theirs = pair
    got = exchange(theirs.astype(LOW), 0, 2).astype(jnp.float32)
    return (mine + got).astype(LOW)


def split_flat(values):
    across = place()[1]
    half = values.shape[0] // 2
    low, high = values[:half], values[half:]
    return [jnp.where(across == 0, low, high), jnp.where(across == 0, high, low)]


def split_across(values):
    across = place()[1]
    half = values.shape[1] // 2
    model = values.shape[2]
    low = values[:, :half].reshape(-1, model)
    high = values[:, half:].reshape(-1, model)
    return [jnp.where(across == 0, low, high), jnp.where(across == 0, high, low)]


def halve(values, mask):
    side = (lax.axis_index("seq") // mask) % 2
    half = values.shape[0] // 2
    low, high = values[:half], values[half:]
    keep = jnp.where(side == 0, low, high)
    sent = jnp.where(side == 0, high, low)
    return (keep.astype(jnp.float32) + exchange(sent, mask, 0).astype(jnp.float32)).astype(LOW)


def double(values, mask):
    side = (lax.axis_index("seq") // mask) % 2
    other = exchange(values, mask, 0)
    low = jnp.where(side == 0, values, other)
    high = jnp.where(side == 0, other, values)
    return jnp.concatenate([low, high], axis=0)


def reduce_big(total):
    masks = [1 << i for i in range(lax.axis_size("seq").bit_length() - 1)]
    rows = total.shape[0]
    extra = -rows % (2 * lax.axis_size("seq"))
    if extra:
        total = jnp.pad(total, ((0, extra), (0, 0)))
    middle = total.shape[0] // 2
    done = []
    for part, order in ((total[:middle], masks), (total[middle:], masks[1:] + masks[:1])):
        for mask in order:
            part = halve(part, mask)
        for mask in reversed(order):
            part = double(part, mask)
        done.append(part)
    return jnp.concatenate(done, axis=0)[:rows]


def seq_sum(values):
    mask = 1
    while mask < lax.axis_size("seq"):
        values = values + exchange(values, mask, 0)
        mask *= 2
    return values


def reduce_small(mid, small):
    mine = jnp.concatenate([m[0].reshape(-1) for m in mid])
    theirs = jnp.concatenate([m[1].reshape(-1) for m in mid])
    every = jnp.concatenate([s.reshape(-1) for s in small])
    count, extra = every.shape[0], mine.shape[0]
    pad = -(count + extra) % 1024
    got = exchange(jnp.pad(jnp.concatenate([every, theirs]), (0, pad)), 0, 2)
    total = jnp.pad(jnp.concatenate([every, mine]), (0, pad)) + got
    total = seq_sum(total)
    every = total[:count]
    every = every + exchange(every, 0, 1)
    mids, at = [], count
    for m in mid:
        mids.append(total[at : at + m[0].size].reshape(m[0].shape))
        at += m[0].size
    smalls, at = [], 0
    for s in small:
        smalls.append(every[at : at + s.size].reshape(s.shape))
        at += s.size
    return mids, smalls


def on_device(
    hidden_in,
    query_weight,
    key_weight,
    value_weight,
    query_bias,
    value_bias,
    out_weight,
    out_bias,
    conv_taps,
    up_weight,
    up_bias,
    down_weight,
    down_bias,
    gain_one,
    shift_one,
    gain_two,
    shift_two,
    out_grad,
    item_lengths,
):
    tok_row = hidden_in.shape[1] * 2
    half = (conv_taps.shape[2] - 1) // 2
    layout = item_layout(item_lengths, tok_row, half)
    q_bias, v_bias, taps, both_up = fetch_small(query_bias, value_bias, conv_taps, up_bias)
    hidden = hidden_in.astype(jnp.float32)
    x_full, pooled = join_pool(hidden, layout)
    weights, pooled = fetch_weights(
        query_weight, key_weight, value_weight, out_weight, up_weight, down_weight, pooled
    )
    params = []
    for i in range(2):
        params.append(
            dict(
                weights=weights[i],
                half=half,
                offload=i == 1,
                q_bias=q_bias[i],
                v_bias=v_bias[i],
                lines=tap_lines(taps[i]),
                up_bias=both_up[i] if i == 1 else up_bias[:1],
                out_bias=out_bias[i],
                down_bias=down_bias[i],
                gain_one=gain_one[i],
                shift_one=shift_one[i],
                gain_two=gain_two[i],
                shift_two=shift_two[i],
            )
        )
    kept = [None, None]
    for i in range(2):
        joined = (x_full, pooled) if i == 0 else join_pool(hidden, layout)
        ahead = weights[1] if i == 0 else None
        hidden, kept[i] = layer_forward(hidden, params[i], layout, joined, ahead)
    grad = out_grad
    big, mid, small = [None, None], [None, None], [None, None]
    pending = None
    for i in (1, 0):
        grad, grads, mid[i], small[i] = layer_backward(grad, kept[i], params[i], layout, pending)
        if i == 1:
            attn_grad, ffn_grad = grads
            grad, ffn_grad = tied(grad, ffn_grad)
            pending = [seq_gather(across_pick(ffn_grad)), attn_grad]
        else:
            attn_grad, (ffn_one, packed) = grads
            packed = jnp.concatenate([across_pick(packed[:2])[None], packed[2:]], axis=0)
            packed = lax.all_gather(packed, "seq", axis=1, tiled=True)
            big[0] = (reduce_big(attn_grad), packed[1:].reshape(-1, packed.shape[2]))
            big[1] = (packed[0], ffn_one)
    mids, smalls = reduce_small(
        [[jnp.stack(m) for m in zip(*pairs)] for pairs in zip(*mid)],
        [jnp.stack(pair) for pair in zip(*small)],
    )
    width = query_weight.shape[2]
    attn = jnp.stack([big[0][0], big[1][0]]).reshape(2, 4, width, -1)
    qkv = [jnp.swapaxes(attn[:, i], 1, 2).astype(jnp.float32) for i in range(3)]
    outs = attn[:, 3].astype(jnp.float32)
    both = [big[0][1], big[1][1]]
    rows = up_weight.shape[1]
    ups = jnp.stack([one[:rows] for one in both]).astype(jnp.float32)
    downs = jnp.stack([one[rows:] for one in both]).astype(jnp.float32)
    return (
        hidden.astype(LOW),
        grad,
        qkv[0],
        qkv[1],
        qkv[2],
        mids[0],
        mids[1],
        outs,
        smalls[0],
        mids[2].reshape(conv_taps.shape),
        ups,
        mids[3],
        downs,
        smalls[1],
        smalls[2],
        smalls[3],
        smalls[4],
        smalls[5],
    )


def solution(mesh):
    placed = (
        P(None, ("seq", "head"), None),
        P(None, None, "head"),
        P(None, None, "head"),
        P(None, None, "head"),
        P(None, "head"),
        P(None, "head"),
        P(None, "head", None),
        P(),
        P(None, "head", None),
        P(None, None, "head"),
        P(None, "head"),
        P(None, "head", None),
        P(),
        P(),
        P(),
        P(),
        P(),
        P(None, ("seq", "head"), None),
        P(),
    )
    return jax.shard_map(
        on_device,
        mesh=mesh,
        in_specs=placed,
        out_specs=(
            P(None, ("seq", "head"), None),
            P(None, ("seq", "head"), None),
            P(None, None, "head"),
            P(None, None, "head"),
            P(None, None, "head"),
            P(None, "head"),
            P(None, "head"),
            P(None, "head", None),
            P(),
            P(None, "head", None),
            P(None, None, "head"),
            P(None, "head"),
            P(None, "head", None),
            P(),
            P(),
            P(),
            P(),
            P(),
        ),
        check_vma=False,
    )
```

```python
import functools

import jax
import jax.numpy as jnp
from jax import lax
from jax.experimental import pallas as pl
from jax.experimental.pallas import tpu as pltpu
from jax.sharding import PartitionSpec as P

LANDMARKS = 64
NS_STEPS = 6


HIGHEST = lax.Precision.HIGHEST
EPSILON = 1e-05
FLOOR_TOP = -1e30
LOW = jnp.bfloat16
GROUP = ((0, 2), (1, 0), (1, 2))


def layer_norm(values, gain, offset):
    centred = values - jnp.mean(values, axis=-1, keepdims=True)
    variance = jnp.mean(centred * centred, axis=-1, keepdims=True)
    return centred * lax.rsqrt(variance + EPSILON) * gain + offset


def exchange(values, seq_mask, head_mask):
    if seq_mask == 0:
        count = lax.axis_size("head")
        return lax.ppermute(values, "head", [(i, i ^ head_mask) for i in range(count)])
    if head_mask == 0:
        count = lax.axis_size("seq")
        return lax.ppermute(values, "seq", [(i, i ^ seq_mask) for i in range(count)])
    heads = lax.axis_size("head")
    route = []
    for s in range(lax.axis_size("seq")):
        for h in range(heads):
            route.append((s * heads + h, (s ^ seq_mask) * heads + (h ^ head_mask)))
    return lax.ppermute(values, ("seq", "head"), route)


def rank_shift(values, step):
    heads = lax.axis_size("head")
    ranks = lax.axis_size("seq") * (heads // 2)
    route = []
    for rank in range(ranks):
        target = rank + step
        if 0 <= target < ranks:
            for core in range(2):
                source_dev = (rank // 2) * heads + (rank % 2) * 2 + core
                target_dev = (target // 2) * heads + (target % 2) * 2 + core
                route.append((source_dev, target_dev))
    return lax.ppermute(values, ("seq", "head"), route)


def place():
    seq = lax.axis_index("seq")
    head = lax.axis_index("head")
    return seq, head // 2, head % 2


def pair_join(values, axis):
    core = place()[2]
    other = exchange(values, 0, 1)
    low = jnp.where(core == 0, values, other)
    high = jnp.where(core == 0, other, values)
    return jnp.concatenate([low, high], axis=axis)


def pair_collect(terms):
    core = place()[2]
    half = terms.shape[1] // 2
    low, high = terms[:, :half], terms[:, half:]
    mine = jnp.where(core == 0, low, high)
    theirs = jnp.where(core == 0, high, low).astype(jnp.bfloat16)
    return mine + exchange(theirs, 0, 1).astype(jnp.float32)


def group_index():
    seq, across, core = place()
    return across + 2 * (seq % 2)


def upper_levels():
    levels = (lax.axis_size("seq") // 2).bit_length() - 1
    return [(low, min(2, levels - low)) for low in range(0, levels, 2)]


def nn(one, two, precision=None):
    return lax.dot_general(
        one, two, (((1,), (0,)), ((), ())), precision, preferred_element_type=jnp.float32
    )


def nt(one, two, precision=None):
    return lax.dot_general(
        one, two, (((1,), (1,)), ((), ())), precision, preferred_element_type=jnp.float32
    )


def tn(one, two, precision=None):
    return lax.dot_general(
        one, two, (((0,), (0,)), ((), ())), precision, preferred_element_type=jnp.float32
    )


def on_core(kernel, outs, scalars, *arrays, us=1):
    shapes = tuple(jax.ShapeDtypeStruct(shape, dtype) for shape, dtype in outs)
    specs = [pl.BlockSpec(memory_space=pltpu.SMEM)] if scalars is not None else []
    specs += [pl.BlockSpec(memory_space=pltpu.VMEM)] * len(arrays)
    given = ((scalars,) if scalars is not None else ()) + arrays
    return pl.pallas_call(
        kernel,
        out_shape=shapes,
        in_specs=specs,
        out_specs=tuple(pl.BlockSpec(memory_space=pltpu.VMEM) for _ in outs),
        compiler_params=pltpu.CompilerParams(vmem_limit_bytes=48 * 1024 * 1024),
        cost_estimate=pl.CostEstimate(
            flops=us * 10**9, bytes_accessed=us * 3 * 10**6, transcendentals=0
        ),
    )(*given)


def tokens_of(row, tok_row):
    return pl.ds(pl.multiple_of(row * tok_row, tok_row), tok_row)


def lanes(shape):
    return lax.broadcasted_iota(jnp.int32, shape, len(shape) - 1)


def join_pool_kernel(spot, own, other, pool, full, one, two, three, four):
    rows, piece, model = own.shape
    tok_row = 2 * piece
    core = spot[1]
    half = model // 2
    for row in range(rows):
        mine = pl.multiple_of(row * tok_row + core * piece, piece)
        theirs = pl.multiple_of(row * tok_row + (1 - core) * piece, piece)
        full[pl.ds(mine, piece), :] = own[row]
        full[pl.ds(theirs, piece), :] = other[row]
    side = pl.ds(pl.multiple_of(core * half, half), half)
    for step, out in enumerate((one, two, three, four)):
        row = spot[0] ^ step
        block = full[tokens_of(row, tok_row), side]
        out[...] = nn(pool[row], block).astype(LOW)


def rim_blocks(block_of, rows, tok_row, half):
    low, high = None, None
    for row in range(rows):
        block = block_of(row).astype(jnp.float32)
        lane = lanes(block.shape)
        first = block if row == 0 else pltpu.roll(block, row * half, 1)
        shift = (row * half + half) % tok_row
        last = block if shift == 0 else pltpu.roll(block, shift, 1)
        inside = lane // half == row
        low = jnp.where(inside, first, 0.0 if low is None else low)
        high = jnp.where(inside, last, 0.0 if high is None else high)
    return low.astype(LOW), high.astype(LOW)


def far_kernel(half, spot, qkv, land, base, one, two, three, four, low, high):
    width = qkv.shape[0] // 3
    head_dim = LANDMARKS
    heads = width // head_dim
    tok_row = qkv.shape[1] // 4
    scale = head_dim ** (-0.5)
    for step, out in enumerate((one, two, three, four)):
        here = tokens_of(spot[0] ^ step, tok_row)
        logs = []
        for head in range(heads):
            cols = slice(head * head_dim, (head + 1) * head_dim)
            keys = qkv[width + head * head_dim : width + (head + 1) * head_dim, here]
            values = qkv[2 * width + head * head_dim : 2 * width + (head + 1) * head_dim, here]
            land_q = land[step * LANDMARKS : (step + 1) * LANDMARKS, cols]
            scores = nn(land_q, keys) * scale
            top = jnp.max(scores, axis=1, keepdims=True)
            grown = jnp.exp(scores - top)
            total = jnp.sum(grown, axis=1, keepdims=True)
            mix = nt(grown.astype(LOW), values) / total
            out[:, cols] = (mix - base[step : step + 1, cols]).astype(LOW)
            logs.append(top + jnp.log(total))
        out[:, width:] = packed_parts(logs)
    low[...], high[...] = rim_blocks(
        lambda row: qkv[2 * width :, row * tok_row : (row + 1) * tok_row], 4, tok_row, half
    )


def merged(flags, pieces, width):
    head_dim = LANDMARKS
    mixes, logs = [], []
    for head in range(width // head_dim):
        cols = slice(head * head_dim, (head + 1) * head_dim)
        log = [unpacked_part(piece[:, width:], head) for piece in pieces]
        for index in range(1, len(pieces)):
            log[index] = jnp.where(flags[index - 1] > 0, log[index], FLOOR_TOP)
        top = functools.reduce(jnp.maximum, log)
        shares = [jnp.exp(value - top) for value in log]
        total = functools.reduce(jnp.add, shares)
        mix = sum(s * piece[:, cols].astype(jnp.float32) for s, piece in zip(shares, pieces))
        mixes.append(mix / total)
        logs.append(top + jnp.log(total))
    return mixes, logs


def merge_kernel(count, flags, *refs):
    out = refs[count]
    width = out.shape[1] - 128
    mixes, logs = merged(flags, refs[:count], width)
    for head, mix in enumerate(mixes):
        out[:, head * LANDMARKS : (head + 1) * LANDMARKS] = mix.astype(LOW)
    out[:, width:] = packed_parts(logs)


def packed_parts(columns):
    packed = jnp.zeros((LANDMARKS, 128), jnp.float32)
    lane = lanes(packed.shape)
    for head, column in enumerate(columns):
        for part in range(3):
            rounded = column.astype(LOW).astype(jnp.float32)
            packed = jnp.where(lane == head + 8 * part, rounded, packed)
            column = column - rounded
    return packed.astype(LOW)


def unpacked_part(packed, head):
    packed = packed.astype(jnp.float32)
    return (
        packed[:, head : head + 1]
        + packed[:, head + 8 : head + 9]
        + packed[:, head + 16 : head + 17]
    )


def land_out_kernel(count, flags, *refs):
    inverse, base, out, weighted = refs[count:]
    width = weighted.shape[1]
    mixes, logs = merged(flags, refs[:count], width)
    for head, mix in enumerate(mixes):
        cols = slice(head * LANDMARKS, (head + 1) * LANDMARKS)
        mix = mix + base[0:1, cols]
        weighted[:, cols] = mix
        out[:, cols] = nn(inverse[head], mix, HIGHEST).astype(LOW)
    out[:, width:] = packed_parts(logs)


def inverse_kernel(land, amats, inverses, products, seconds, thirds):
    width = land.shape[1] // 2
    heads = width // LANDMARKS
    scale = LANDMARKS ** (-0.5)
    shape = (LANDMARKS, LANDMARKS)
    rows = lax.broadcasted_iota(jnp.int32, shape, 0)
    eye = (rows == lanes(shape)).astype(jnp.float32)
    matrices, iterates = [], []
    for head in range(heads):
        cols = slice(head * LANDMARKS, (head + 1) * LANDMARKS)
        keys = slice(width + head * LANDMARKS, width + (head + 1) * LANDMARKS)
        scores = nt(land[:LANDMARKS, cols], land[:LANDMARKS, keys]) * scale
        grown = jnp.exp(scores - jnp.max(scores, axis=1, keepdims=True))
        matrix = grown / jnp.sum(grown, axis=1, keepdims=True)
        columns = jnp.sum(matrix, axis=0, keepdims=True)
        square = columns * columns
        fourth = square * square
        bound = jnp.sum(fourth * fourth, axis=1, keepdims=True)
        bound = jnp.exp(jnp.log(bound) * 0.125)
        amats[head] = matrix
        matrices.append(matrix)
        iterates.append(matrix.T / bound)
    for step in range(NS_STEPS):
        product = [nn(a, z, HIGHEST) for a, z in zip(matrices, iterates)]
        inner = [nn(p, 7.0 * eye - p, HIGHEST) for p in product]
        second = [15.0 * eye - value for value in inner]
        third = [13.0 * eye - nn(p, m, HIGHEST) for p, m in zip(product, second)]
        for head in range(heads):
            inverses[step * heads + head] = iterates[head]
            products[step * heads + head] = product[head]
            seconds[step * heads + head] = second[head]
            thirds[step * heads + head] = third[head]
        iterates = [0.25 * nn(z, m, HIGHEST) for z, m in zip(iterates, third)]
    for head in range(heads):
        inverses[NS_STEPS * heads + head] = iterates[head]


def band_blocks(line, tok_row, half):
    span = line.shape[1]
    wide = jnp.broadcast_to(line, (tok_row, span))
    middle = pltpu.roll(wide, 0, 1, stride=1, stride_axis=0)[:, :tok_row]
    short = jnp.broadcast_to(line, (half, span))
    low = pltpu.roll(short, span - half, 1, stride=1, stride_axis=0)[:, :tok_row]
    high = pltpu.roll(short, tok_row, 1, stride=1, stride_axis=0)[:, :tok_row]
    reps = tok_row // half
    return [
        part.astype(LOW)
        for part in (middle, jnp.concatenate([low] * reps, 0), jnp.concatenate([high] * reps, 0))
    ]


def near_kernel(half, spot, qkv, low, high, rims, land, one, two, three, four, line, out):
    width = qkv.shape[0] // 3
    tok_row = qkv.shape[1] // 4
    head_dim = LANDMARKS
    scale = head_dim ** (-0.5)
    low_all = low[...].astype(jnp.float32) * rims[0:1, :]
    high_all = high[...].astype(jnp.float32) * rims[1:2, :]
    lane = lanes((head_dim, tok_row)) // half
    bands = [band_blocks(line[h : h + 1, :], tok_row, half) for h in range(width // head_dim)]
    for step, mixed in enumerate((one, two, three, four)):
        row = spot[0] ^ step
        here = tokens_of(row, tok_row)
        land_rows = slice(step * LANDMARKS, (step + 1) * LANDMARKS)
        for head in range(width // head_dim):
            cols = slice(head * head_dim, (head + 1) * head_dim)
            keys = slice(width + head * head_dim, width + (head + 1) * head_dim)
            queries = qkv[cols, here]
            scores = nn(land[land_rows, keys], queries) * scale
            grown = jnp.exp(scores - jnp.max(scores, axis=0, keepdims=True))
            probs = grown / jnp.sum(grown, axis=0, keepdims=True)
            total = tn(mixed[:, cols], probs.astype(LOW))
            values = qkv[2 * width + head * head_dim : 2 * width + (head + 1) * head_dim, here]
            total = total + nn(values, bands[head][0])
            mine = lane == row
            total = total + nn(jnp.where(mine, low_all[cols, :], 0.0).astype(LOW), bands[head][1])
            total = total + nn(jnp.where(mine, high_all[cols, :], 0.0).astype(LOW), bands[head][2])
            out[cols, here] = total.astype(LOW)


def near_back_kernel(half, spot, qkv, grads, land, *refs):
    mixes, queries_out = refs[:4], refs[4]
    land_outs, land_keys, low, high = refs[5:9], refs[9:13], refs[13], refs[14]
    width = qkv.shape[0] // 3
    tok_row = qkv.shape[1] // 4
    head_dim = LANDMARKS
    scale = head_dim ** (-0.5)
    for step in range(4):
        here = tokens_of(spot[0] ^ step, tok_row)
        land_rows = slice(step * LANDMARKS, (step + 1) * LANDMARKS)
        for head in range(width // head_dim):
            cols = slice(head * head_dim, (head + 1) * head_dim)
            keys = slice(width + head * head_dim, width + (head + 1) * head_dim)
            queries = qkv[cols, here]
            land_k = land[land_rows, keys]
            scores = nn(land_k, queries) * scale
            grown = jnp.exp(scores - jnp.max(scores, axis=0, keepdims=True))
            probs = grown / jnp.sum(grown, axis=0, keepdims=True)
            grad = grads[cols, here]
            grad_probs = nn(mixes[step][:, cols], grad)
            inner = jnp.sum(grad_probs * probs, axis=0, keepdims=True)
            grad_scores = (probs * (grad_probs - inner) * scale).astype(LOW)
            queries_out[cols, here] = tn(land_k, grad_scores)
            land_keys[step][:, cols] = nt(grad_scores, queries).astype(LOW)
            land_outs[step][:, cols] = nt(probs.astype(LOW), grad).astype(LOW)
    low[...], high[...] = rim_blocks(
        lambda row: grads[:, row * tok_row : (row + 1) * tok_row], 4, tok_row, half
    )


def conv_back_kernel(half, qkv, grads, low, high, grad_low, grad_high, rims, line, out, taps):
    width = qkv.shape[0] // 3
    tok_row = qkv.shape[1] // 4
    head_dim = LANDMARKS
    span = line.shape[1]
    low_all = low[...].astype(jnp.float32) * rims[0:1, :]
    high_all = high[...].astype(jnp.float32) * rims[1:2, :]
    grad_low_all = grad_low[...].astype(jnp.float32) * rims[0:1, :]
    grad_high_all = grad_high[...].astype(jnp.float32) * rims[1:2, :]
    lane = lanes((head_dim, tok_row)) // half
    square = (tok_row, tok_row)
    turned = (lax.broadcasted_iota(jnp.int32, square, 0) + lanes(square) == tok_row - 1).astype(LOW)
    wide = lanes((tok_row, span))
    for head in range(width // head_dim):
        cols = slice(head * head_dim, (head + 1) * head_dim)
        bands = band_blocks(line[head : head + 1, :], tok_row, half)
        fields = [jnp.zeros(square, jnp.float32) for _ in range(3)]
        for row in range(4):
            here = slice(row * tok_row, (row + 1) * tok_row)
            mine = lane == row

            def rim(block):
                return jnp.where(mine, block[cols, :], 0.0).astype(LOW)

            grad = grads[cols, here]
            values = qkv[2 * width + head * head_dim : 2 * width + (head + 1) * head_dim, here]
            total = nn(grad, bands[0]) + nn(rim(grad_low_all), bands[1])
            out[cols, here] = total + nn(rim(grad_high_all), bands[2])
            backward = nn(grad, turned).astype(LOW)
            for index, block in enumerate((values, rim(low_all), rim(high_all))):
                fields[index] = fields[index] + tn(backward, block)
        ends = []
        for field in fields[1:]:
            folded = field + pltpu.roll(field, 2 * half, 1)
            folded = folded + pltpu.roll(folded, half, 1)
            ends.append(jnp.concatenate([folded, folded], axis=1))
        whole = jnp.concatenate([fields[0], jnp.zeros(square, jnp.float32)], axis=1)
        whole = pltpu.roll(whole, half, 1)
        whole = jnp.where(wide < half, ends[0], whole)
        right = (wide >= half + tok_row) & (wide < 2 * half + tok_row)
        whole = jnp.where(right, ends[1], whole)
        whole = pltpu.roll(whole, span - tok_row + 1, 1, stride=1, stride_axis=0)
        taps[head : head + 1, :] = jnp.sum(whole, axis=0, keepdims=True)[:, :128]


def mixture_grad_kernel(grads, inverse, weighted, out):
    width = grads.shape[1]
    inner = []
    for head in range(width // LANDMARKS):
        cols = slice(head * LANDMARKS, (head + 1) * LANDMARKS)
        value = tn(inverse[head], grads[:, cols], HIGHEST).astype(LOW)
        out[:, cols] = value
        product = value.astype(jnp.float32) * weighted[:, cols]
        inner.append(jnp.sum(product, axis=1, keepdims=True))
    out[:, width:] = packed_parts(inner)


def inverse_back_kernel(
    grads, weighted, land, amats, inverses, products, seconds, thirds, out
):
    width = grads.shape[1]
    heads = width // LANDMARKS
    scale = LANDMARKS ** (-0.5)
    shape = (LANDMARKS, LANDMARKS)
    rows = lax.broadcasted_iota(jnp.int32, shape, 0)
    eye = (rows == lanes(shape)).astype(jnp.float32)
    every = range(heads)
    columns = [slice(head * LANDMARKS, (head + 1) * LANDMARKS) for head in every]
    grad = [nt(grads[:, c], weighted[:, c], HIGHEST) for c in columns]
    matrices = [amats[head] for head in every]
    total = [jnp.zeros(shape, jnp.float32) for _ in every]
    for step in reversed(range(NS_STEPS)):
        z = [inverses[step * heads + head] for head in every]
        p = [products[step * heads + head] for head in every]
        m2 = [seconds[step * heads + head] for head in every]
        m3 = [thirds[step * heads + head] for head in every]
        g3 = [-0.25 * tn(z[i], grad[i], HIGHEST) for i in every]
        gz = [0.25 * nt(grad[i], m3[i], HIGHEST) for i in every]
        g2 = [-tn(p[i], g3[i], HIGHEST) for i in every]
        gp = [nt(g3[i], m2[i], HIGHEST) for i in every]
        g1 = [tn(p[i], g2[i], HIGHEST) for i in every]
        gp = [gp[i] + nt(g2[i], 7.0 * eye - p[i], HIGHEST) - g1[i] for i in every]
        total = [total[i] + nt(gp[i], z[i], HIGHEST) for i in every]
        grad = [gz[i] + tn(matrices[i], gp[i], HIGHEST) for i in every]
    for head in every:
        matrix = matrices[head]
        sums = jnp.sum(matrix, axis=0, keepdims=True)
        square = sums * sums
        fourth = square * square
        bound = jnp.sum(fourth * fourth, axis=1, keepdims=True)
        bound = jnp.exp(jnp.log(bound) * 0.125)
        first = inverses[head]
        lost = jnp.sum(grad[head] * first, axis=1, keepdims=True)
        lost = -jnp.sum(lost, axis=0, keepdims=True) / bound
        ratio = sums / bound
        cube = ratio * ratio * ratio
        value = total[head] + grad[head].T / bound + lost * (cube * cube * ratio)
        inner = jnp.sum(value * matrix, axis=1, keepdims=True)
        scores = matrix * (value - inner) * scale
        keys = slice(width + head * LANDMARKS, width + (head + 1) * LANDMARKS)
        land_q = land[:LANDMARKS, columns[head]].astype(jnp.float32)
        land_k = land[:LANDMARKS, keys].astype(jnp.float32)
        out[:, columns[head]] = nn(scores, land_k, HIGHEST)
        out[:, keys] = tn(scores, land_q, HIGHEST)


def far_back_kernel(spot, qkv, land, conv, *refs):
    mixes, grads, near_keys = refs[:4], refs[4:8], refs[8:12]
    keys_out, values_out, parts = refs[12], refs[13], refs[14:18]
    width = qkv.shape[0] // 3
    tok_row = qkv.shape[1] // 4
    head_dim = LANDMARKS
    scale = head_dim ** (-0.5)
    for step in range(4):
        here = tokens_of(spot[0] ^ step, tok_row)
        land_rows = slice(step * LANDMARKS, (step + 1) * LANDMARKS)
        for head in range(width // head_dim):
            cols = slice(head * head_dim, (head + 1) * head_dim)
            keys = qkv[width + head * head_dim : width + (head + 1) * head_dim, here]
            values = qkv[2 * width + head * head_dim : 2 * width + (head + 1) * head_dim, here]
            land_q = land[land_rows, cols]
            log = unpacked_part(mixes[step][:, width:], head)
            inner = unpacked_part(grads[step][:, width:], head)
            probs = jnp.exp(nn(land_q, keys) * scale - log)
            grad = grads[step][:, cols]
            scores = (probs * (nn(grad, values) - inner) * scale).astype(LOW)
            parts[step][:, cols] = nt(scores, keys).astype(LOW)
            keys_out[cols, here] = tn(land_q, scores)
            values_out[cols, here] = (conv[cols, here] + tn(grad, probs.astype(LOW))).astype(LOW)
        parts[step][:, width:] = near_keys[step][...]


def token_grad_kernel(spot, near, far, values, pool, one, two, three, four, out):
    width = near.shape[0]
    tok_row = near.shape[1] // 4
    for step, grads in enumerate((one, two, three, four)):
        row = spot[0] ^ step
        here = tokens_of(row, tok_row)
        share = pool[row]
        out[:width, here] = (near[:, here] + tn(grads[:, :width], share)).astype(LOW)
        out[width : 2 * width, here] = (far[:, here] + tn(grads[:, width:], share)).astype(LOW)
    out[2 * width :, :] = values[...]


def send_rows(pieces):
    got = [exchange(piece, s, h) for piece, (s, h) in zip(pieces[1:], GROUP)]
    return [pieces[0]] + got


def spread_row(row):
    return [row] + [exchange(row, s, h) for s, h in GROUP]


def item_sum(pieces, layout, beside=None):
    return item_total(send_rows(pieces), layout, beside)


def item_total(pieces, layout, beside=None):
    span = layout["span"]
    dtype = pieces[0].dtype
    pieces = [piece.astype(jnp.float32) for piece in pieces]
    total = (pieces[0] + pieces[1]) + (pieces[2] + pieces[3])
    if beside is not None:
        beside, total = tied(beside, total)
        beside = exchange(beside, 0, 2)
    for low, bits in upper_levels():
        sent = total.astype(dtype)
        near = exchange(sent, 2 << low, 0).astype(jnp.float32)
        pair = total + jnp.where(span > 4 << low, near, 0.0)
        if bits == 2:
            far = exchange(sent, 4 << low, 0).astype(jnp.float32)
            cross = exchange(sent, 6 << low, 0).astype(jnp.float32)
            pair = pair + jnp.where(span > 8 << low, far + cross, 0.0)
        total = pair
    if beside is not None:
        beside, total = tied(beside, total)
        return total, beside
    return total


def land_mixture(pieces, inverse, base, layout):
    span = layout["span"]
    width = pieces[0].shape[1] - 128
    pieces = send_rows(pieces)
    flags = jnp.ones((3,), jnp.int32)
    for low, bits in upper_levels():
        call = functools.partial(merge_kernel, len(pieces))
        (row,) = on_core(call, [(pieces[0].shape, LOW)], flags, *pieces)
        pieces = [row] + [exchange(row, m << (low + 1), 0) for m in range(1, 1 << bits)]
        wide = (span > 8 << low).astype(jnp.int32)
        flags = jnp.stack([(span > 4 << low).astype(jnp.int32), wide, wide])
    outs = [(pieces[0].shape, LOW), ((LANDMARKS, width), jnp.float32)]
    call = functools.partial(land_out_kernel, len(pieces))
    return on_core(call, outs, flags, *pieces, inverse, base)


def item_layout(item_lengths, tok_row, half):
    seq, across, core = place()
    rank = seq * 2 + across
    ends = jnp.cumsum(item_lengths, axis=1)
    starts = ends - item_lengths
    first_token = rank * tok_row
    chosen = (starts <= first_token) & (first_token < ends)
    length = jnp.sum(jnp.where(chosen, item_lengths, 0), axis=1)
    begin = jnp.sum(jnp.where(chosen, starts, 0), axis=1)
    segment = length // LANDMARKS
    first_rank = begin // tok_row
    spans = length // tok_row
    positions = first_token + jnp.arange(tok_row)
    marks = (positions[None, :] - begin[:, None]) // segment[:, None]
    hits = marks[:, None, :] == jnp.arange(LANDMARKS)[None, :, None]
    share = 1.0 / segment.astype(jnp.float32)
    pool = jnp.where(hits, share[:, None, None], 0.0).astype(LOW)
    left_open = rank > first_rank
    right_open = rank + 1 < first_rank + spans
    rims = jnp.repeat(jnp.stack([left_open, right_open]).astype(jnp.float32), half, axis=1)
    me = group_index()
    return dict(
        span=lax.dynamic_index_in_dim(spans, me, 0, keepdims=False),
        pool=pool,
        rims=jnp.pad(rims, ((0, 6), (0, 0))),
        spot=jnp.stack([me, core]).astype(jnp.int32),
    )


def dot(spec, one, two):
    return jnp.einsum(spec, one, two, preferred_element_type=jnp.float32)


def ordered(mine, other, axis):
    across = place()[1]
    low = jnp.where(across == 0, mine, other)
    high = jnp.where(across == 0, other, mine)
    return jnp.stack([low, high], axis=axis)


def fetch_small(query_bias, value_bias, conv_taps, up_bias):
    layers = query_bias.shape[0]
    flat = [a.reshape(layers, -1) for a in (query_bias, value_bias, conv_taps, up_bias)]
    sizes = [a.shape[1] for a in flat]
    packed = jnp.concatenate(flat, axis=1)
    other = exchange(jnp.pad(packed, ((0, 0), (0, -packed.shape[1] % 128))), 0, 2)
    rest, at = [], 0
    for size in sizes:
        rest.append(other[:, at : at + size])
        at += size
    heads = conv_taps.shape[1]
    q_bias = ordered(query_bias, rest[0], 1).reshape(layers, -1)
    v_bias = ordered(value_bias, rest[1], 1).reshape(layers, -1)
    taps = ordered(conv_taps, rest[2].reshape(conv_taps.shape), 1).reshape(layers, 2 * heads, -1)
    return q_bias, v_bias, taps, ordered(up_bias, rest[3], 1)


def across_gather(values):
    return lax.all_gather(values, "head", axis=0, axis_index_groups=[[0, 2], [1, 3]])


def fetch_weights(
    query_weight, key_weight, value_weight, out_weight, up_weight, down_weight, pooled
):
    model = up_weight.shape[1]
    packs = [
        jnp.concatenate([query_weight[i].T, key_weight[i].T, value_weight[i].T], 0)
        for i in range(2)
    ]
    pack, *pooled = tied(packs[0], *pooled)
    other = exchange(pack, 0, 2)
    own_out, other = tied(out_weight[0], other)
    other_out = exchange(own_out, 0, 2)
    held = jnp.concatenate([packs[1], out_weight[1]], 0)
    held, other = tied(held, other)
    first = ordered(pack.reshape(3, -1, model), other.reshape(3, -1, model), 1)
    layers = [
        dict(
            qkv=first.reshape(-1, model),
            out=ordered(own_out, other_out, 0).reshape(-1, model),
            up=up_weight[:1],
            down=down_weight[:1],
        ),
        dict(
            attn=jnp.swapaxes(across_gather(held).reshape(2, 4, -1, model), 0, 1),
            up=across_gather(up_weight[1]),
            down=across_gather(down_weight[1]),
        ),
    ]
    return layers, pooled


def tap_lines(taps):
    count = taps.shape[1]
    half = (count - 1) // 2
    gap = jnp.zeros((taps.shape[0], 256 - count), jnp.float32)
    flipped = taps[:, ::-1]
    lines = [jnp.concatenate([t[:, half:], gap, t[:, :half]], axis=1) for t in (flipped, taps)]
    pad = -taps.shape[0] % 8
    return [jnp.pad(line, ((0, pad), (0, 0))) for line in lines]


def token_sets(values, own_pair):
    own = pair_join(values, 1)
    flat = (own.shape[0] * own.shape[1], own.shape[2])
    if own_pair:
        return [own.reshape(flat)]
    return [own.reshape(flat), pair_join(exchange(values, 0, 2), 1).reshape(flat)]


def collect_sets(terms, rows):
    terms = [term.reshape(rows, -1, term.shape[-1]) for term in terms]
    total = pair_collect(terms[0])
    if len(terms) == 2:
        total = total + exchange(pair_collect(terms[1]).astype(LOW), 0, 2).astype(jnp.float32)
    return total


def join_pool(hidden, layout):
    batch_rows, piece, model = hidden.shape
    quarter = [((LANDMARKS, model // 2), LOW)] * 4
    x_low = hidden.astype(LOW)
    x_full, *pooled = on_core(
        join_pool_kernel,
        [((batch_rows * 2 * piece, model), LOW)] + quarter,
        layout["spot"],
        x_low,
        exchange(x_low, 0, 1),
        layout["pool"],
    )
    return x_full, send_rows(pooled)


def layer_forward(hidden, params, layout, joined, ahead=None):
    weights = params["weights"]
    if params["offload"]:
        attn = weights["attn"].reshape(-1, hidden.shape[2])
        weights["qkv"] = attn[: attn.shape[0] * 3 // 4]
        weights["out"] = attn[attn.shape[0] * 3 // 4 :]
    spot = layout["spot"]
    batch_rows, piece, model = hidden.shape
    tok_row = 2 * piece
    tokens = batch_rows * tok_row
    width = weights["out"].shape[0]
    half = params["half"]
    x_full, pooled = joined
    if params["offload"]:
        weights["up"], *pooled = tied(weights["up"], *pooled)
    pooled = jnp.concatenate(spread_row(item_total(pooled, layout).astype(LOW)), axis=0)
    pooled = pair_join(pooled, 1)
    bias_q, bias_v = params["q_bias"], params["v_bias"]
    no_bias = jnp.zeros_like(bias_q)
    column = jnp.concatenate([bias_q, no_bias, bias_v])[:, None]
    qkv = (nt(weights["qkv"], x_full) + column).astype(LOW)
    land = nt(pooled, weights["qkv"][: 2 * width]) + jnp.concatenate([bias_q, no_bias])
    land = land.astype(LOW)
    heads = width // LANDMARKS
    message = [((LANDMARKS, width + 128), LOW)] * 4
    means = jnp.mean(pooled.reshape(4, LANDMARKS, -1).astype(jnp.float32), axis=1)
    base = nt(means.astype(LOW), weights["qkv"][2 * width :]) + bias_v
    base = jnp.pad(base, ((0, 4), (0, 0)))
    rim = [((width, batch_rows * half), LOW)] * 2
    *parts, low, high = on_core(
        functools.partial(far_kernel, half), message + rim, spot, qkv, land, base, us=4
    )
    low, high = rank_shift(high, 1), rank_shift(low, -1)
    square = (LANDMARKS, LANDMARKS)
    steps = ((NS_STEPS * heads,) + square, jnp.float32)
    own_land = land[:LANDMARKS]
    chain = on_core(
        inverse_kernel,
        [
            ((heads,) + square, jnp.float32),
            (((NS_STEPS + 1) * heads,) + square, jnp.float32),
            steps,
            steps,
            steps,
        ],
        None,
        own_land,
        us=5,
    )
    inverse = chain[1][NS_STEPS * heads :]
    own_out, weighted = land_mixture(parts, inverse, base, layout)
    if params["offload"]:
        own_out, weights["down"] = tied(own_out, weights["down"])
    mixes = spread_row(own_out)
    (att_low,) = on_core(
        functools.partial(near_kernel, half),
        [((width, tokens), LOW)],
        spot,
        qkv,
        low,
        high,
        layout["rims"],
        land,
        *mixes,
        params["lines"][0],
        us=3,
    )
    terms = tn(att_low, weights["out"]).reshape(batch_rows, tok_row, model)
    if ahead is not None:
        terms, ahead["attn"] = tied(terms, ahead["attn"])
    resid_one = hidden + (pair_collect(terms) + params["out_bias"])
    normed = layer_norm(resid_one, params["gain_one"], params["shift_one"])
    h_sets = token_sets(normed.astype(LOW), params["offload"])
    gelu_low, slopes, terms = [], [], []
    for h_full in h_sets:
        up_pre = dot("td,gdf->gtf", h_full, weights["up"]) + params["up_bias"][:, None, :]
        area = 0.5 * (1.0 + lax.erf(up_pre * 0.7071067811865476))
        bell = jnp.exp(-0.5 * up_pre * up_pre) * 0.3989422804014327
        gelu_low.append((up_pre * area).astype(LOW))
        slopes.append((area + up_pre * bell).astype(LOW))
        terms.append(dot("gtf,gfd->td", gelu_low[-1], weights["down"]))
    mlp_out = collect_sets(terms, batch_rows) + params["down_bias"]
    resid_two = normed + mlp_out
    result = layer_norm(resid_two, params["gain_two"], params["shift_two"])
    kept = dict(
        x_full=x_full,
        qkv=qkv,
        land=land,
        own_land=own_land,
        rims=(low, high),
        chain=chain,
        inverse=inverse,
        weighted=weighted,
        mixes=mixes,
        att_low=att_low,
        resid_one=resid_one,
        h_sets=h_sets,
        gelu_low=gelu_low,
        slopes=slopes,
        resid_two=resid_two,
    )
    return result, kept


def layer_backward(grad_out, kept, params, layout, pending):
    weights = params["weights"]
    spot = layout["spot"]
    batch_rows, piece, model = grad_out.shape
    tok_row = 2 * piece
    tokens = batch_rows * tok_row
    width = weights["out"].shape[0]
    half = params["half"]
    unused_two, pull_two = jax.vjp(
        layer_norm, kept["resid_two"], params["gain_two"], params["shift_two"]
    )
    grad_two, grad_gain_two, grad_shift_two = pull_two(grad_out)
    grad_mlp = grad_two.astype(LOW)
    grad_down_bias = jnp.sum(grad_mlp.astype(jnp.float32), axis=(0, 1))
    grad_sets = token_sets(grad_mlp, params["offload"])
    grad_ups, terms = [], []
    for grad_set, slope in zip(grad_sets, kept["slopes"]):
        grad_up = dot("td,gfd->gtf", grad_set, weights["down"])
        grad_ups.append((grad_up * slope.astype(jnp.float32)).astype(LOW))
        terms.append(dot("gtf,gdf->td", grad_ups[-1], weights["up"]))
    grad_normed = grad_two + collect_sets(terms, batch_rows)
    down_grad = sum(dot("gtf,td->gfd", g, d) for g, d in zip(kept["gelu_low"], grad_sets))
    up_grad = sum(dot("td,gtf->gdf", h, g) for h, g in zip(kept["h_sets"], grad_ups))
    ffn_grad = jnp.concatenate([up_grad, down_grad], axis=1).astype(LOW)
    grad_up_bias = sum(jnp.sum(g.astype(jnp.float32), axis=1) for g in grad_ups)
    if params["offload"]:
        ffn_grad = seq_scatter(ffn_grad)
        grad_up_bias = sides(grad_up_bias)
    else:
        ffn_one, attn_one = pending
        rows = attn_one.shape[1]
        packed = jnp.stack([attn_one[0], attn_one[1], ffn_grad[0, :rows], ffn_grad[0, rows:]])
        ffn_grad = (ffn_one, seq_scatter(packed))
        grad_up_bias = [grad_up_bias[0], jnp.zeros_like(grad_up_bias[0])]
    unused_one, pull_one = jax.vjp(
        layer_norm, kept["resid_one"], params["gain_one"], params["shift_one"]
    )
    grad_one, grad_gain_one, grad_shift_one = pull_one(grad_normed)
    grad_attn = grad_one.astype(LOW)
    grad_out_bias = jnp.sum(grad_attn.astype(jnp.float32), axis=(0, 1))
    grad_attn_full = pair_join(grad_attn, 1).reshape(tokens, model)
    grad_att = nt(weights["out"], grad_attn_full).astype(LOW)
    qkv, land, mixes = kept["qkv"], kept["land"], kept["mixes"]
    row = [((LANDMARKS, width), LOW)]
    rim = [((width, batch_rows * half), LOW)] * 2
    near_queries, *rest = on_core(
        functools.partial(near_back_kernel, half),
        [((width, tokens), jnp.float32)] + row * 8 + rim,
        spot,
        qkv,
        grad_att,
        land,
        *mixes,
        us=6,
    )
    near_outs, near_keys, (low, high) = rest[:4], rest[4:8], rest[8:]
    low, high = rank_shift(high, 1), rank_shift(low, -1)
    own_grad = item_sum(near_outs, layout)
    (own_mix_grad,) = on_core(
        mixture_grad_kernel,
        [((LANDMARKS, width + 128), LOW)],
        None,
        own_grad,
        kept["inverse"],
        kept["weighted"],
    )
    mix_grads = spread_row(own_mix_grad)
    if pending is not None:
        ffn_one, *mix_grads = tied(ffn_grad[0], *mix_grads)
        ffn_grad = (ffn_one, ffn_grad[1])
    grad_out_weight = nn(kept["att_low"], grad_attn_full)
    conv_grad, tap_grad = on_core(
        functools.partial(conv_back_kernel, half),
        [((width, tokens), jnp.float32), ((8, 128), jnp.float32)],
        None,
        qkv,
        grad_att,
        *kept["rims"],
        low,
        high,
        layout["rims"],
        params["lines"][1],
        us=6,
    )
    far_keys, values_low, *parts = on_core(
        far_back_kernel,
        [((width, tokens), jnp.float32), ((width, tokens), LOW)]
        + [((LANDMARKS, 2 * width), LOW)] * 4,
        spot,
        qkv,
        land,
        conv_grad,
        *mixes,
        *mix_grads,
        *near_keys,
        us=5,
    )
    own_grad, *parts = tied(own_grad, *parts)
    (own_land_grad,) = on_core(
        inverse_back_kernel,
        [((LANDMARKS, 2 * width), jnp.float32)],
        None,
        own_grad,
        kept["weighted"],
        kept["own_land"],
        *kept["chain"],
        us=13,
    )
    if params["offload"]:
        own_land_grad = item_sum(parts, layout) + own_land_grad
    else:
        first_grad = jnp.stack([nn(values_low, kept["x_full"]), grad_out_weight])
        first_mine, first_theirs = split_across(first_grad)
        land_sum, first_got = item_sum(parts, layout, first_theirs.astype(LOW))
        own_land_grad = land_sum + own_land_grad
        first_grad = (first_mine + first_got.astype(jnp.float32)).astype(LOW)
    land_grads = spread_row(own_land_grad.astype(LOW))
    (grad_qkv,) = on_core(
        token_grad_kernel,
        [((3 * width, tokens), LOW)],
        spot,
        near_queries,
        far_keys,
        values_low,
        layout["pool"],
        *land_grads,
    )
    terms = tn(grad_qkv, weights["qkv"]).reshape(batch_rows, tok_row, model)
    grad_hidden = grad_one + pair_collect(terms)
    if params["offload"]:
        grad_weight = nn(grad_qkv, kept["x_full"])
        attn_grad = jnp.concatenate([grad_weight, grad_out_weight], axis=0)
        attn_grad = attn_grad.reshape(4, 2, width // 2, model).astype(LOW)
        attn_grad = jnp.swapaxes(attn_grad, 0, 1).reshape(2, 2 * width, model)
    else:
        grad_weight = nn(grad_qkv[: 2 * width], kept["x_full"]).reshape(2, width, model)
        attn_grad = across_sum(split_across(grad_weight))
        unused, packed = tied(attn_grad, ffn_grad[1])
        ffn_grad = (ffn_grad[0], packed)
        attn_grad = jnp.concatenate([attn_grad, first_grad], axis=0)
    grad_bias = jnp.sum(grad_qkv.astype(jnp.float32), axis=1)
    heads = width // LANDMARKS
    mids = [
        split_flat(grad_bias[:width]),
        split_flat(grad_bias[2 * width :]),
        split_flat(tap_grad[:heads, : 2 * half + 1]),
        grad_up_bias,
    ]
    smalls = [
        grad_out_bias,
        grad_down_bias,
        grad_gain_one,
        grad_shift_one,
        grad_gain_two,
        grad_shift_two,
    ]
    return grad_hidden, (attn_grad, ffn_grad), mids, smalls


def sides(values):
    across = place()[1]
    return [jnp.where(across == 0, values[0], values[1]), jnp.where(across == 0, values[1], values[0])]


def seq_scatter(values):
    return lax.psum_scatter(values, "seq", scatter_dimension=values.ndim - 2, tiled=True)


def seq_gather(values):
    return lax.all_gather(values, "seq", axis=0, tiled=True)


def across_pick(values):
    mine, theirs = sides(values)
    return across_sum([mine.astype(jnp.float32), theirs])


def tied(values, *others):
    return lax.optimization_barrier((values,) + others)


def across_sum(pair):
    mine, theirs = pair
    got = exchange(theirs.astype(LOW), 0, 2).astype(jnp.float32)
    return (mine + got).astype(LOW)


def split_flat(values):
    across = place()[1]
    half = values.shape[0] // 2
    low, high = values[:half], values[half:]
    return [jnp.where(across == 0, low, high), jnp.where(across == 0, high, low)]


def split_across(values):
    across = place()[1]
    half = values.shape[1] // 2
    model = values.shape[2]
    low = values[:, :half].reshape(-1, model)
    high = values[:, half:].reshape(-1, model)
    return [jnp.where(across == 0, low, high), jnp.where(across == 0, high, low)]


def halve(values, mask):
    side = (lax.axis_index("seq") // mask) % 2
    half = values.shape[0] // 2
    low, high = values[:half], values[half:]
    keep = jnp.where(side == 0, low, high)
    sent = jnp.where(side == 0, high, low)
    return (keep.astype(jnp.float32) + exchange(sent, mask, 0).astype(jnp.float32)).astype(LOW)


def double(values, mask):
    side = (lax.axis_index("seq") // mask) % 2
    other = exchange(values, mask, 0)
    low = jnp.where(side == 0, values, other)
    high = jnp.where(side == 0, other, values)
    return jnp.concatenate([low, high], axis=0)


def reduce_big(total):
    masks = [1 << i for i in range(lax.axis_size("seq").bit_length() - 1)]
    rows = total.shape[0]
    extra = -rows % (2 * lax.axis_size("seq"))
    if extra:
        total = jnp.pad(total, ((0, extra), (0, 0)))
    middle = total.shape[0] // 2
    done = []
    for part, order in ((total[:middle], masks), (total[middle:], masks[1:] + masks[:1])):
        for mask in order:
            part = halve(part, mask)
        for mask in reversed(order):
            part = double(part, mask)
        done.append(part)
    return jnp.concatenate(done, axis=0)[:rows]


def seq_sum(values):
    mask = 1
    while mask < lax.axis_size("seq"):
        values = values + exchange(values, mask, 0)
        mask *= 2
    return values


def reduce_small(mid, small):
    mine = jnp.concatenate([m[0].reshape(-1) for m in mid])
    theirs = jnp.concatenate([m[1].reshape(-1) for m in mid])
    every = jnp.concatenate([s.reshape(-1) for s in small])
    count, extra = every.shape[0], mine.shape[0]
    pad = -(count + extra) % 1024
    got = exchange(jnp.pad(jnp.concatenate([every, theirs]), (0, pad)), 0, 2)
    total = jnp.pad(jnp.concatenate([every, mine]), (0, pad)) + got
    total = seq_sum(total)
    every = total[:count]
    every = every + exchange(every, 0, 1)
    mids, at = [], count
    for m in mid:
        mids.append(total[at : at + m[0].size].reshape(m[0].shape))
        at += m[0].size
    smalls, at = [], 0
    for s in small:
        smalls.append(every[at : at + s.size].reshape(s.shape))
        at += s.size
    return mids, smalls


def on_device(
    hidden_in,
    query_weight,
    key_weight,
    value_weight,
    query_bias,
    value_bias,
    out_weight,
    out_bias,
    conv_taps,
    up_weight,
    up_bias,
    down_weight,
    down_bias,
    gain_one,
    shift_one,
    gain_two,
    shift_two,
    out_grad,
    item_lengths,
):
    tok_row = hidden_in.shape[1] * 2
    half = (conv_taps.shape[2] - 1) // 2
    layout = item_layout(item_lengths, tok_row, half)
    q_bias, v_bias, taps, both_up = fetch_small(query_bias, value_bias, conv_taps, up_bias)
    hidden = hidden_in.astype(jnp.float32)
    x_full, pooled = join_pool(hidden, layout)
    weights, pooled = fetch_weights(
        query_weight, key_weight, value_weight, out_weight, up_weight, down_weight, pooled
    )
    params = []
    for i in range(2):
        params.append(
            dict(
                weights=weights[i],
                half=half,
                offload=i == 1,
                q_bias=q_bias[i],
                v_bias=v_bias[i],
                lines=tap_lines(taps[i]),
                up_bias=both_up[i] if i == 1 else up_bias[:1],
                out_bias=out_bias[i],
                down_bias=down_bias[i],
                gain_one=gain_one[i],
                shift_one=shift_one[i],
                gain_two=gain_two[i],
                shift_two=shift_two[i],
            )
        )
    kept = [None, None]
    for i in range(2):
        joined = (x_full, pooled) if i == 0 else join_pool(hidden, layout)
        ahead = weights[1] if i == 0 else None
        hidden, kept[i] = layer_forward(hidden, params[i], layout, joined, ahead)
    grad = out_grad
    big, mid, small = [None, None], [None, None], [None, None]
    pending = None
    for i in (1, 0):
        grad, grads, mid[i], small[i] = layer_backward(grad, kept[i], params[i], layout, pending)
        if i == 1:
            attn_grad, ffn_grad = grads
            grad, ffn_grad = tied(grad, ffn_grad)
            pending = [seq_gather(across_pick(ffn_grad)), attn_grad]
        else:
            attn_grad, (ffn_one, packed) = grads
            packed = jnp.concatenate([across_pick(packed[:2])[None], packed[2:]], axis=0)
            packed = lax.all_gather(packed, "seq", axis=1, tiled=True)
            big[0] = (reduce_big(attn_grad), packed[1:].reshape(-1, packed.shape[2]))
            big[1] = (packed[0], ffn_one)
    mids, smalls = reduce_small(
        [[jnp.stack(m) for m in zip(*pairs)] for pairs in zip(*mid)],
        [jnp.stack(pair) for pair in zip(*small)],
    )
    width = query_weight.shape[2]
    attn = jnp.stack([big[0][0], big[1][0]]).reshape(2, 4, width, -1)
    qkv = [jnp.swapaxes(attn[:, i], 1, 2).astype(jnp.float32) for i in range(3)]
    outs = attn[:, 3].astype(jnp.float32)
    both = [big[0][1], big[1][1]]
    rows = up_weight.shape[1]
    ups = jnp.stack([one[:rows] for one in both]).astype(jnp.float32)
    downs = jnp.stack([one[rows:] for one in both]).astype(jnp.float32)
    return (
        hidden.astype(LOW),
        grad,
        qkv[0],
        qkv[1],
        qkv[2],
        mids[0],
        mids[1],
        outs,
        smalls[0],
        mids[2].reshape(conv_taps.shape),
        ups,
        mids[3],
        downs,
        smalls[1],
        smalls[2],
        smalls[3],
        smalls[4],
        smalls[5],
    )


def solution(mesh):
    placed = (
        P(None, ("seq", "head"), None),
        P(None, None, "head"),
        P(None, None, "head"),
        P(None, None, "head"),
        P(None, "head"),
        P(None, "head"),
        P(None, "head", None),
        P(),
        P(None, "head", None),
        P(None, None, "head"),
        P(None, "head"),
        P(None, "head", None),
        P(),
        P(),
        P(),
        P(),
        P(),
        P(None, ("seq", "head"), None),
        P(),
    )
    return jax.shard_map(
        on_device,
        mesh=mesh,
        in_specs=placed,
        out_specs=(
            P(None, ("seq", "head"), None),
            P(None, ("seq", "head"), None),
            P(None, None, "head"),
            P(None, None, "head"),
            P(None, None, "head"),
            P(None, "head"),
            P(None, "head"),
            P(None, "head", None),
            P(),
            P(None, "head", None),
            P(None, None, "head"),
            P(None, "head"),
            P(None, "head", None),
            P(),
            P(),
            P(),
            P(),
            P(),
        ),
        check_vma=False,
    )
```

```python
import functools

import jax
import jax.numpy as jnp
from jax import lax
from jax.experimental import pallas as pl
from jax.experimental.pallas import tpu as pltpu
from jax.sharding import PartitionSpec as P

LANDMARKS = 64
NS_STEPS = 6


HIGHEST = lax.Precision.HIGHEST
EPSILON = 1e-05
FLOOR_TOP = -1e30
LOW = jnp.bfloat16
GROUP = ((0, 2), (1, 0), (1, 2))


def layer_norm(values, gain, offset):
    centred = values - jnp.mean(values, axis=-1, keepdims=True)
    variance = jnp.mean(centred * centred, axis=-1, keepdims=True)
    return centred * lax.rsqrt(variance + EPSILON) * gain + offset


def exchange(values, seq_mask, head_mask):
    if seq_mask == 0:
        count = lax.axis_size("head")
        return lax.ppermute(values, "head", [(i, i ^ head_mask) for i in range(count)])
    if head_mask == 0:
        count = lax.axis_size("seq")
        return lax.ppermute(values, "seq", [(i, i ^ seq_mask) for i in range(count)])
    heads = lax.axis_size("head")
    route = []
    for s in range(lax.axis_size("seq")):
        for h in range(heads):
            route.append((s * heads + h, (s ^ seq_mask) * heads + (h ^ head_mask)))
    return lax.ppermute(values, ("seq", "head"), route)


def rank_shift(values, step):
    heads = lax.axis_size("head")
    ranks = lax.axis_size("seq") * (heads // 2)
    route = []
    for rank in range(ranks):
        target = rank + step
        if 0 <= target < ranks:
            for core in range(2):
                source_dev = (rank // 2) * heads + (rank % 2) * 2 + core
                target_dev = (target // 2) * heads + (target % 2) * 2 + core
                route.append((source_dev, target_dev))
    return lax.ppermute(values, ("seq", "head"), route)


def place():
    seq = lax.axis_index("seq")
    head = lax.axis_index("head")
    return seq, head // 2, head % 2


def pair_join(values, axis):
    core = place()[2]
    other = exchange(values, 0, 1)
    low = jnp.where(core == 0, values, other)
    high = jnp.where(core == 0, other, values)
    return jnp.concatenate([low, high], axis=axis)


def pair_collect(terms):
    core = place()[2]
    half = terms.shape[1] // 2
    low, high = terms[:, :half], terms[:, half:]
    mine = jnp.where(core == 0, low, high)
    theirs = jnp.where(core == 0, high, low).astype(jnp.bfloat16)
    return mine + exchange(theirs, 0, 1).astype(jnp.float32)


def group_index():
    seq, across, core = place()
    return across + 2 * (seq % 2)


def upper_levels():
    levels = (lax.axis_size("seq") // 2).bit_length() - 1
    return [(low, min(2, levels - low)) for low in range(0, levels, 2)]


def nn(one, two, precision=None):
    return lax.dot_general(
        one, two, (((1,), (0,)), ((), ())), precision, preferred_element_type=jnp.float32
    )


def nt(one, two, precision=None):
    return lax.dot_general(
        one, two, (((1,), (1,)), ((), ())), precision, preferred_element_type=jnp.float32
    )


def tn(one, two, precision=None):
    return lax.dot_general(
        one, two, (((0,), (0,)), ((), ())), precision, preferred_element_type=jnp.float32
    )


def on_core(kernel, outs, scalars, *arrays, us=1):
    shapes = tuple(jax.ShapeDtypeStruct(shape, dtype) for shape, dtype in outs)
    specs = [pl.BlockSpec(memory_space=pltpu.SMEM)] if scalars is not None else []
    specs += [pl.BlockSpec(memory_space=pltpu.VMEM)] * len(arrays)
    given = ((scalars,) if scalars is not None else ()) + arrays
    return pl.pallas_call(
        kernel,
        out_shape=shapes,
        in_specs=specs,
        out_specs=tuple(pl.BlockSpec(memory_space=pltpu.VMEM) for _ in outs),
        compiler_params=pltpu.CompilerParams(vmem_limit_bytes=48 * 1024 * 1024),
        cost_estimate=pl.CostEstimate(
            flops=us * 10**9, bytes_accessed=us * 3 * 10**6, transcendentals=0
        ),
    )(*given)


def tokens_of(row, tok_row):
    return pl.ds(pl.multiple_of(row * tok_row, tok_row), tok_row)


def lanes(shape):
    return lax.broadcasted_iota(jnp.int32, shape, len(shape) - 1)


def join_pool_kernel(spot, own, other, pool, full, one, two, three, four):
    rows, piece, model = own.shape
    tok_row = 2 * piece
    core = spot[1]
    half = model // 2
    for row in range(rows):
        mine = pl.multiple_of(row * tok_row + core * piece, piece)
        theirs = pl.multiple_of(row * tok_row + (1 - core) * piece, piece)
        full[pl.ds(mine, piece), :] = own[row]
        full[pl.ds(theirs, piece), :] = other[row]
    side = pl.ds(pl.multiple_of(core * half, half), half)
    for step, out in enumerate((one, two, three, four)):
        row = spot[0] ^ step
        block = full[tokens_of(row, tok_row), side]
        out[...] = nn(pool[row], block).astype(LOW)


def rim_blocks(block_of, rows, tok_row, half):
    low, high = None, None
    for row in range(rows):
        block = block_of(row).astype(jnp.float32)
        lane = lanes(block.shape)
        first = block if row == 0 else pltpu.roll(block, row * half, 1)
        shift = (row * half + half) % tok_row
        last = block if shift == 0 else pltpu.roll(block, shift, 1)
        inside = lane // half == row
        low = jnp.where(inside, first, 0.0 if low is None else low)
        high = jnp.where(inside, last, 0.0 if high is None else high)
    return low.astype(LOW), high.astype(LOW)


def far_kernel(half, spot, qkv, land, base, one, two, three, four, low, high):
    width = qkv.shape[0] // 3
    head_dim = LANDMARKS
    heads = width // head_dim
    tok_row = qkv.shape[1] // 4
    scale = head_dim ** (-0.5)
    for step, out in enumerate((one, two, three, four)):
        here = tokens_of(spot[0] ^ step, tok_row)
        logs = []
        for head in range(heads):
            cols = slice(head * head_dim, (head + 1) * head_dim)
            keys = qkv[width + head * head_dim : width + (head + 1) * head_dim, here]
            values = qkv[2 * width + head * head_dim : 2 * width + (head + 1) * head_dim, here]
            land_q = land[step * LANDMARKS : (step + 1) * LANDMARKS, cols]
            scores = nn(land_q, keys) * scale
            top = jnp.max(scores, axis=1, keepdims=True)
            grown = jnp.exp(scores - top)
            total = jnp.sum(grown, axis=1, keepdims=True)
            mix = nt(grown.astype(LOW), values) / total
            out[:, cols] = (mix - base[step : step + 1, cols]).astype(LOW)
            logs.append(top + jnp.log(total))
        out[:, width:] = packed_parts(logs)
    low[...], high[...] = rim_blocks(
        lambda row: qkv[2 * width :, row * tok_row : (row + 1) * tok_row], 4, tok_row, half
    )


def merged(flags, pieces, width):
    head_dim = LANDMARKS
    mixes, logs = [], []
    for head in range(width // head_dim):
        cols = slice(head * head_dim, (head + 1) * head_dim)
        log = [unpacked_part(piece[:, width:], head) for piece in pieces]
        for index in range(1, len(pieces)):
            log[index] = jnp.where(flags[index - 1] > 0, log[index], FLOOR_TOP)
        top = functools.reduce(jnp.maximum, log)
        shares = [jnp.exp(value - top) for value in log]
        total = functools.reduce(jnp.add, shares)
        mix = sum(s * piece[:, cols].astype(jnp.float32) for s, piece in zip(shares, pieces))
        mixes.append(mix / total)
        logs.append(top + jnp.log(total))
    return mixes, logs


def merge_kernel(count, flags, *refs):
    out = refs[count]
    width = out.shape[1] - 128
    mixes, logs = merged(flags, refs[:count], width)
    for head, mix in enumerate(mixes):
        out[:, head * LANDMARKS : (head + 1) * LANDMARKS] = mix.astype(LOW)
    out[:, width:] = packed_parts(logs)


def packed_parts(columns):
    packed = jnp.zeros((LANDMARKS, 128), jnp.float32)
    lane = lanes(packed.shape)
    for head, column in enumerate(columns):
        for part in range(3):
            rounded = column.astype(LOW).astype(jnp.float32)
            packed = jnp.where(lane == head + 8 * part, rounded, packed)
            column = column - rounded
    return packed.astype(LOW)


def unpacked_part(packed, head):
    packed = packed.astype(jnp.float32)
    return (
        packed[:, head : head + 1]
        + packed[:, head + 8 : head + 9]
        + packed[:, head + 16 : head + 17]
    )


def land_out_kernel(count, flags, *refs):
    inverse, base, out, weighted = refs[count:]
    width = weighted.shape[1]
    mixes, logs = merged(flags, refs[:count], width)
    for head, mix in enumerate(mixes):
        cols = slice(head * LANDMARKS, (head + 1) * LANDMARKS)
        mix = mix + base[0:1, cols]
        weighted[:, cols] = mix
        out[:, cols] = nn(inverse[head], mix, HIGHEST).astype(LOW)
    out[:, width:] = packed_parts(logs)


def inverse_kernel(land, amats, inverses, products, seconds, thirds):
    width = land.shape[1] // 2
    heads = width // LANDMARKS
    scale = LANDMARKS ** (-0.5)
    shape = (LANDMARKS, LANDMARKS)
    rows = lax.broadcasted_iota(jnp.int32, shape, 0)
    eye = (rows == lanes(shape)).astype(jnp.float32)
    matrices, iterates = [], []
    for head in range(heads):
        cols = slice(head * LANDMARKS, (head + 1) * LANDMARKS)
        keys = slice(width + head * LANDMARKS, width + (head + 1) * LANDMARKS)
        scores = nt(land[:LANDMARKS, cols], land[:LANDMARKS, keys]) * scale
        grown = jnp.exp(scores - jnp.max(scores, axis=1, keepdims=True))
        matrix = grown / jnp.sum(grown, axis=1, keepdims=True)
        columns = jnp.sum(matrix, axis=0, keepdims=True)
        square = columns * columns
        fourth = square * square
        bound = jnp.sum(fourth * fourth, axis=1, keepdims=True)
        bound = jnp.exp(jnp.log(bound) * 0.125)
        amats[head] = matrix
        matrices.append(matrix)
        iterates.append(matrix.T / bound)
    for step in range(NS_STEPS):
        product = [nn(a, z, HIGHEST) for a, z in zip(matrices, iterates)]
        inner = [nn(p, 7.0 * eye - p, HIGHEST) for p in product]
        second = [15.0 * eye - value for value in inner]
        third = [13.0 * eye - nn(p, m, HIGHEST) for p, m in zip(product, second)]
        for head in range(heads):
            inverses[step * heads + head] = iterates[head]
            products[step * heads + head] = product[head]
            seconds[step * heads + head] = second[head]
            thirds[step * heads + head] = third[head]
        iterates = [0.25 * nn(z, m, HIGHEST) for z, m in zip(iterates, third)]
    for head in range(heads):
        inverses[NS_STEPS * heads + head] = iterates[head]


def band_blocks(line, tok_row, half):
    span = line.shape[1]
    wide = jnp.broadcast_to(line, (tok_row, span))
    middle = pltpu.roll(wide, 0, 1, stride=1, stride_axis=0)[:, :tok_row]
    short = jnp.broadcast_to(line, (half, span))
    low = pltpu.roll(short, span - half, 1, stride=1, stride_axis=0)[:, :tok_row]
    high = pltpu.roll(short, tok_row, 1, stride=1, stride_axis=0)[:, :tok_row]
    reps = tok_row // half
    return [
        part.astype(LOW)
        for part in (middle, jnp.concatenate([low] * reps, 0), jnp.concatenate([high] * reps, 0))
    ]


def near_kernel(half, spot, qkv, low, high, rims, land, one, two, three, four, line, out):
    width = qkv.shape[0] // 3
    tok_row = qkv.shape[1] // 4
    head_dim = LANDMARKS
    scale = head_dim ** (-0.5)
    low_all = low[...].astype(jnp.float32) * rims[0:1, :]
    high_all = high[...].astype(jnp.float32) * rims[1:2, :]
    lane = lanes((head_dim, tok_row)) // half
    bands = [band_blocks(line[h : h + 1, :], tok_row, half) for h in range(width // head_dim)]
    for step, mixed in enumerate((one, two, three, four)):
        row = spot[0] ^ step
        here = tokens_of(row, tok_row)
        land_rows = slice(step * LANDMARKS, (step + 1) * LANDMARKS)
        for head in range(width // head_dim):
            cols = slice(head * head_dim, (head + 1) * head_dim)
            keys = slice(width + head * head_dim, width + (head + 1) * head_dim)
            queries = qkv[cols, here]
            scores = nn(land[land_rows, keys], queries) * scale
            grown = jnp.exp(scores - jnp.max(scores, axis=0, keepdims=True))
            probs = grown / jnp.sum(grown, axis=0, keepdims=True)
            total = tn(mixed[:, cols], probs.astype(LOW))
            values = qkv[2 * width + head * head_dim : 2 * width + (head + 1) * head_dim, here]
            total = total + nn(values, bands[head][0])
            mine = lane == row
            total = total + nn(jnp.where(mine, low_all[cols, :], 0.0).astype(LOW), bands[head][1])
            total = total + nn(jnp.where(mine, high_all[cols, :], 0.0).astype(LOW), bands[head][2])
            out[cols, here] = total.astype(LOW)


def near_back_kernel(half, spot, qkv, grads, land, *refs):
    mixes, queries_out = refs[:4], refs[4]
    land_outs, land_keys, low, high = refs[5:9], refs[9:13], refs[13], refs[14]
    width = qkv.shape[0] // 3
    tok_row = qkv.shape[1] // 4
    head_dim = LANDMARKS
    scale = head_dim ** (-0.5)
    for step in range(4):
        here = tokens_of(spot[0] ^ step, tok_row)
        land_rows = slice(step * LANDMARKS, (step + 1) * LANDMARKS)
        for head in range(width // head_dim):
            cols = slice(head * head_dim, (head + 1) * head_dim)
            keys = slice(width + head * head_dim, width + (head + 1) * head_dim)
            queries = qkv[cols, here]
            land_k = land[land_rows, keys]
            scores = nn(land_k, queries) * scale
            grown = jnp.exp(scores - jnp.max(scores, axis=0, keepdims=True))
            probs = grown / jnp.sum(grown, axis=0, keepdims=True)
            grad = grads[cols, here]
            grad_probs = nn(mixes[step][:, cols], grad)
            inner = jnp.sum(grad_probs * probs, axis=0, keepdims=True)
            grad_scores = (probs * (grad_probs - inner) * scale).astype(LOW)
            queries_out[cols, here] = tn(land_k, grad_scores)
            land_keys[step][:, cols] = nt(grad_scores, queries).astype(LOW)
            land_outs[step][:, cols] = nt(probs.astype(LOW), grad).astype(LOW)
    low[...], high[...] = rim_blocks(
        lambda row: grads[:, row * tok_row : (row + 1) * tok_row], 4, tok_row, half
    )


def conv_back_kernel(half, qkv, grads, low, high, grad_low, grad_high, rims, line, out, taps):
    width = qkv.shape[0] // 3
    tok_row = qkv.shape[1] // 4
    head_dim = LANDMARKS
    span = line.shape[1]
    low_all = low[...].astype(jnp.float32) * rims[0:1, :]
    high_all = high[...].astype(jnp.float32) * rims[1:2, :]
    grad_low_all = grad_low[...].astype(jnp.float32) * rims[0:1, :]
    grad_high_all = grad_high[...].astype(jnp.float32) * rims[1:2, :]
    lane = lanes((head_dim, tok_row)) // half
    square = (tok_row, tok_row)
    turned = (lax.broadcasted_iota(jnp.int32, square, 0) + lanes(square) == tok_row - 1).astype(LOW)
    wide = lanes((tok_row, span))
    for head in range(width // head_dim):
        cols = slice(head * head_dim, (head + 1) * head_dim)
        bands = band_blocks(line[head : head + 1, :], tok_row, half)
        fields = [jnp.zeros(square, jnp.float32) for _ in range(3)]
        for row in range(4):
            here = slice(row * tok_row, (row + 1) * tok_row)
            mine = lane == row

            def rim(block):
                return jnp.where(mine, block[cols, :], 0.0).astype(LOW)

            grad = grads[cols, here]
            values = qkv[2 * width + head * head_dim : 2 * width + (head + 1) * head_dim, here]
            total = nn(grad, bands[0]) + nn(rim(grad_low_all), bands[1])
            out[cols, here] = total + nn(rim(grad_high_all), bands[2])
            backward = nn(grad, turned).astype(LOW)
            for index, block in enumerate((values, rim(low_all), rim(high_all))):
                fields[index] = fields[index] + tn(backward, block)
        ends = []
        for field in fields[1:]:
            folded = field + pltpu.roll(field, 2 * half, 1)
            folded = folded + pltpu.roll(folded, half, 1)
            ends.append(jnp.concatenate([folded, folded], axis=1))
        whole = jnp.concatenate([fields[0], jnp.zeros(square, jnp.float32)], axis=1)
        whole = pltpu.roll(whole, half, 1)
        whole = jnp.where(wide < half, ends[0], whole)
        right = (wide >= half + tok_row) & (wide < 2 * half + tok_row)
        whole = jnp.where(right, ends[1], whole)
        whole = pltpu.roll(whole, span - tok_row + 1, 1, stride=1, stride_axis=0)
        taps[head : head + 1, :] = jnp.sum(whole, axis=0, keepdims=True)[:, :128]


def mixture_grad_kernel(grads, inverse, weighted, out):
    width = grads.shape[1]
    inner = []
    for head in range(width // LANDMARKS):
        cols = slice(head * LANDMARKS, (head + 1) * LANDMARKS)
        value = tn(inverse[head], grads[:, cols], HIGHEST).astype(LOW)
        out[:, cols] = value
        product = value.astype(jnp.float32) * weighted[:, cols]
        inner.append(jnp.sum(product, axis=1, keepdims=True))
    out[:, width:] = packed_parts(inner)


def inverse_back_kernel(
    grads, weighted, land, amats, inverses, products, seconds, thirds, out
):
    width = grads.shape[1]
    heads = width // LANDMARKS
    scale = LANDMARKS ** (-0.5)
    shape = (LANDMARKS, LANDMARKS)
    rows = lax.broadcasted_iota(jnp.int32, shape, 0)
    eye = (rows == lanes(shape)).astype(jnp.float32)
    every = range(heads)
    columns = [slice(head * LANDMARKS, (head + 1) * LANDMARKS) for head in every]
    grad = [nt(grads[:, c], weighted[:, c], HIGHEST) for c in columns]
    matrices = [amats[head] for head in every]
    total = [jnp.zeros(shape, jnp.float32) for _ in every]
    for step in reversed(range(NS_STEPS)):
        z = [inverses[step * heads + head] for head in every]
        p = [products[step * heads + head] for head in every]
        m2 = [seconds[step * heads + head] for head in every]
        m3 = [thirds[step * heads + head] for head in every]
        g3 = [-0.25 * tn(z[i], grad[i], HIGHEST) for i in every]
        gz = [0.25 * nt(grad[i], m3[i], HIGHEST) for i in every]
        g2 = [-tn(p[i], g3[i], HIGHEST) for i in every]
        gp = [nt(g3[i], m2[i], HIGHEST) for i in every]
        g1 = [tn(p[i], g2[i], HIGHEST) for i in every]
        gp = [gp[i] + nt(g2[i], 7.0 * eye - p[i], HIGHEST) - g1[i] for i in every]
        total = [total[i] + nt(gp[i], z[i], HIGHEST) for i in every]
        grad = [gz[i] + tn(matrices[i], gp[i], HIGHEST) for i in every]
    for head in every:
        matrix = matrices[head]
        sums = jnp.sum(matrix, axis=0, keepdims=True)
        square = sums * sums
        fourth = square * square
        bound = jnp.sum(fourth * fourth, axis=1, keepdims=True)
        bound = jnp.exp(jnp.log(bound) * 0.125)
        first = inverses[head]
        lost = jnp.sum(grad[head] * first, axis=1, keepdims=True)
        lost = -jnp.sum(lost, axis=0, keepdims=True) / bound
        ratio = sums / bound
        cube = ratio * ratio * ratio
        value = total[head] + grad[head].T / bound + lost * (cube * cube * ratio)
        inner = jnp.sum(value * matrix, axis=1, keepdims=True)
        scores = matrix * (value - inner) * scale
        keys = slice(width + head * LANDMARKS, width + (head + 1) * LANDMARKS)
        land_q = land[:LANDMARKS, columns[head]].astype(jnp.float32)
        land_k = land[:LANDMARKS, keys].astype(jnp.float32)
        out[:, columns[head]] = nn(scores, land_k, HIGHEST)
        out[:, keys] = tn(scores, land_q, HIGHEST)


def far_back_kernel(spot, qkv, land, conv, *refs):
    mixes, grads, near_keys = refs[:4], refs[4:8], refs[8:12]
    keys_out, values_out, parts = refs[12], refs[13], refs[14:18]
    width = qkv.shape[0] // 3
    tok_row = qkv.shape[1] // 4
    head_dim = LANDMARKS
    scale = head_dim ** (-0.5)
    for step in range(4):
        here = tokens_of(spot[0] ^ step, tok_row)
        land_rows = slice(step * LANDMARKS, (step + 1) * LANDMARKS)
        for head in range(width // head_dim):
            cols = slice(head * head_dim, (head + 1) * head_dim)
            keys = qkv[width + head * head_dim : width + (head + 1) * head_dim, here]
            values = qkv[2 * width + head * head_dim : 2 * width + (head + 1) * head_dim, here]
            land_q = land[land_rows, cols]
            log = unpacked_part(mixes[step][:, width:], head)
            inner = unpacked_part(grads[step][:, width:], head)
            probs = jnp.exp(nn(land_q, keys) * scale - log)
            grad = grads[step][:, cols]
            scores = (probs * (nn(grad, values) - inner) * scale).astype(LOW)
            parts[step][:, cols] = nt(scores, keys).astype(LOW)
            keys_out[cols, here] = tn(land_q, scores)
            values_out[cols, here] = (conv[cols, here] + tn(grad, probs.astype(LOW))).astype(LOW)
        parts[step][:, width:] = near_keys[step][...]


def token_grad_kernel(spot, near, far, values, pool, one, two, three, four, out):
    width = near.shape[0]
    tok_row = near.shape[1] // 4
    for step, grads in enumerate((one, two, three, four)):
        row = spot[0] ^ step
        here = tokens_of(row, tok_row)
        share = pool[row]
        out[:width, here] = (near[:, here] + tn(grads[:, :width], share)).astype(LOW)
        out[width : 2 * width, here] = (far[:, here] + tn(grads[:, width:], share)).astype(LOW)
    out[2 * width :, :] = values[...]


def send_rows(pieces):
    got = [exchange(piece, s, h) for piece, (s, h) in zip(pieces[1:], GROUP)]
    return [pieces[0]] + got


def spread_row(row):
    return [row] + [exchange(row, s, h) for s, h in GROUP]


def item_sum(pieces, layout, beside=None):
    return item_total(send_rows(pieces), layout, beside)


def item_total(pieces, layout, beside=None):
    span = layout["span"]
    dtype = pieces[0].dtype
    pieces = [piece.astype(jnp.float32) for piece in pieces]
    total = (pieces[0] + pieces[1]) + (pieces[2] + pieces[3])
    if beside is not None:
        beside, total = tied(beside, total)
        beside = exchange(beside, 0, 2)
    for low, bits in upper_levels():
        sent = total.astype(dtype)
        near = exchange(sent, 2 << low, 0).astype(jnp.float32)
        pair = total + jnp.where(span > 4 << low, near, 0.0)
        if bits == 2:
            far = exchange(sent, 4 << low, 0).astype(jnp.float32)
            cross = exchange(sent, 6 << low, 0).astype(jnp.float32)
            pair = pair + jnp.where(span > 8 << low, far + cross, 0.0)
        total = pair
    if beside is not None:
        beside, total = tied(beside, total)
        return total, beside
    return total


def land_mixture(pieces, inverse, base, layout):
    span = layout["span"]
    width = pieces[0].shape[1] - 128
    pieces = send_rows(pieces)
    flags = jnp.ones((3,), jnp.int32)
    for low, bits in upper_levels():
        call = functools.partial(merge_kernel, len(pieces))
        (row,) = on_core(call, [(pieces[0].shape, LOW)], flags, *pieces)
        pieces = [row] + [exchange(row, m << (low + 1), 0) for m in range(1, 1 << bits)]
        wide = (span > 8 << low).astype(jnp.int32)
        flags = jnp.stack([(span > 4 << low).astype(jnp.int32), wide, wide])
    outs = [(pieces[0].shape, LOW), ((LANDMARKS, width), jnp.float32)]
    call = functools.partial(land_out_kernel, len(pieces))
    return on_core(call, outs, flags, *pieces, inverse, base)


def item_layout(item_lengths, tok_row, half):
    seq, across, core = place()
    rank = seq * 2 + across
    ends = jnp.cumsum(item_lengths, axis=1)
    starts = ends - item_lengths
    first_token = rank * tok_row
    chosen = (starts <= first_token) & (first_token < ends)
    length = jnp.sum(jnp.where(chosen, item_lengths, 0), axis=1)
    begin = jnp.sum(jnp.where(chosen, starts, 0), axis=1)
    segment = length // LANDMARKS
    first_rank = begin // tok_row
    spans = length // tok_row
    positions = first_token + jnp.arange(tok_row)
    marks = (positions[None, :] - begin[:, None]) // segment[:, None]
    hits = marks[:, None, :] == jnp.arange(LANDMARKS)[None, :, None]
    share = 1.0 / segment.astype(jnp.float32)
    pool = jnp.where(hits, share[:, None, None], 0.0).astype(LOW)
    left_open = rank > first_rank
    right_open = rank + 1 < first_rank + spans
    rims = jnp.repeat(jnp.stack([left_open, right_open]).astype(jnp.float32), half, axis=1)
    me = group_index()
    return dict(
        span=lax.dynamic_index_in_dim(spans, me, 0, keepdims=False),
        pool=pool,
        rims=jnp.pad(rims, ((0, 6), (0, 0))),
        spot=jnp.stack([me, core]).astype(jnp.int32),
    )


def dot(spec, one, two):
    return jnp.einsum(spec, one, two, preferred_element_type=jnp.float32)


def ordered(mine, other, axis):
    across = place()[1]
    low = jnp.where(across == 0, mine, other)
    high = jnp.where(across == 0, other, mine)
    return jnp.stack([low, high], axis=axis)


def fetch_small(query_bias, value_bias, conv_taps, up_bias):
    layers = query_bias.shape[0]
    flat = [a.reshape(layers, -1) for a in (query_bias, value_bias, conv_taps, up_bias)]
    sizes = [a.shape[1] for a in flat]
    packed = jnp.concatenate(flat, axis=1)
    other = exchange(jnp.pad(packed, ((0, 0), (0, -packed.shape[1] % 128))), 0, 2)
    rest, at = [], 0
    for size in sizes:
        rest.append(other[:, at : at + size])
        at += size
    heads = conv_taps.shape[1]
    q_bias = ordered(query_bias, rest[0], 1).reshape(layers, -1)
    v_bias = ordered(value_bias, rest[1], 1).reshape(layers, -1)
    taps = ordered(conv_taps, rest[2].reshape(conv_taps.shape), 1).reshape(layers, 2 * heads, -1)
    return q_bias, v_bias, taps, ordered(up_bias, rest[3], 1)


def across_gather(values):
    return lax.all_gather(values, "head", axis=0, axis_index_groups=[[0, 2], [1, 3]])


def fetch_weights(
    query_weight, key_weight, value_weight, out_weight, up_weight, down_weight, pooled
):
    model = up_weight.shape[1]
    packs = [
        jnp.concatenate([query_weight[i].T, key_weight[i].T, value_weight[i].T], 0)
        for i in range(2)
    ]
    cut = packs[0].shape[0] * 2 // 3
    pack, *pooled = tied(packs[0][:cut], *pooled)
    other = exchange(pack, 0, 2)
    own_out, other = tied(out_weight[0], other)
    other_out = exchange(own_out, 0, 2)
    held = jnp.concatenate([packs[1], out_weight[1]], 0)
    held, other = tied(held, other)
    first = ordered(pack.reshape(2, -1, model), other.reshape(2, -1, model), 1)
    layers = [
        dict(
            front=first.reshape(-1, model),
            back=packs[0][cut:],
            out=ordered(own_out, other_out, 0).reshape(-1, model),
            up=up_weight[:1],
            down=down_weight[:1],
        ),
        dict(
            attn=jnp.swapaxes(across_gather(held).reshape(2, 4, -1, model), 0, 1),
            up=across_gather(up_weight[1]),
            down=across_gather(down_weight[1]),
        ),
    ]
    return layers, pooled


def tap_lines(taps):
    count = taps.shape[1]
    half = (count - 1) // 2
    gap = jnp.zeros((taps.shape[0], 256 - count), jnp.float32)
    flipped = taps[:, ::-1]
    lines = [jnp.concatenate([t[:, half:], gap, t[:, :half]], axis=1) for t in (flipped, taps)]
    pad = -taps.shape[0] % 8
    return [jnp.pad(line, ((0, pad), (0, 0))) for line in lines]


def token_sets(values, own_pair):
    own = pair_join(values, 1)
    flat = (own.shape[0] * own.shape[1], own.shape[2])
    if own_pair:
        return [own.reshape(flat)]
    return [own.reshape(flat), pair_join(exchange(values, 0, 2), 1).reshape(flat)]


def collect_sets(terms, rows):
    terms = [term.reshape(rows, -1, term.shape[-1]) for term in terms]
    total = pair_collect(terms[0])
    if len(terms) == 2:
        total = total + exchange(pair_collect(terms[1]).astype(LOW), 0, 2).astype(jnp.float32)
    return total


def join_pool(hidden, layout):
    batch_rows, piece, model = hidden.shape
    quarter = [((LANDMARKS, model // 2), LOW)] * 4
    x_low = hidden.astype(LOW)
    x_full, *pooled = on_core(
        join_pool_kernel,
        [((batch_rows * 2 * piece, model), LOW)] + quarter,
        layout["spot"],
        x_low,
        exchange(x_low, 0, 1),
        layout["pool"],
    )
    return x_full, send_rows(pooled)


def layer_forward(hidden, params, layout, joined, ahead=None):
    weights = params["weights"]
    if params["offload"]:
        attn = weights["attn"].reshape(-1, hidden.shape[2])
        weights["qkv"] = attn[: attn.shape[0] * 3 // 4]
        weights["out"] = attn[attn.shape[0] * 3 // 4 :]
    spot = layout["spot"]
    batch_rows, piece, model = hidden.shape
    tok_row = 2 * piece
    tokens = batch_rows * tok_row
    width = weights["out"].shape[0]
    half = params["half"]
    x_full, pooled = joined
    if params["offload"]:
        weights["up"], *pooled = tied(weights["up"], *pooled)
    own_pooled = item_total(pooled, layout).astype(LOW)
    if not params["offload"]:
        back, own_pooled = tied(weights["back"], own_pooled)
        back = ordered(back, exchange(back, 0, 2), 0).reshape(-1, model)
        weights["qkv"] = jnp.concatenate([weights["front"], back], axis=0)
    pooled = jnp.concatenate(spread_row(own_pooled), axis=0)
    pooled = pair_join(pooled, 1)
    bias_q, bias_v = params["q_bias"], params["v_bias"]
    no_bias = jnp.zeros_like(bias_q)
    column = jnp.concatenate([bias_q, no_bias, bias_v])[:, None]
    qkv = (nt(weights["qkv"], x_full) + column).astype(LOW)
    land = nt(pooled, weights["qkv"][: 2 * width]) + jnp.concatenate([bias_q, no_bias])
    land = land.astype(LOW)
    heads = width // LANDMARKS
    message = [((LANDMARKS, width + 128), LOW)] * 4
    means = jnp.mean(pooled.reshape(4, LANDMARKS, -1).astype(jnp.float32), axis=1)
    base = nt(means.astype(LOW), weights["qkv"][2 * width :]) + bias_v
    base = jnp.pad(base, ((0, 4), (0, 0)))
    rim = [((width, batch_rows * half), LOW)] * 2
    *parts, low, high = on_core(
        functools.partial(far_kernel, half), message + rim, spot, qkv, land, base, us=4
    )
    low, high = rank_shift(high, 1), rank_shift(low, -1)
    square = (LANDMARKS, LANDMARKS)
    steps = ((NS_STEPS * heads,) + square, jnp.float32)
    own_land = land[:LANDMARKS]
    chain = on_core(
        inverse_kernel,
        [
            ((heads,) + square, jnp.float32),
            (((NS_STEPS + 1) * heads,) + square, jnp.float32),
            steps,
            steps,
            steps,
        ],
        None,
        own_land,
        us=5,
    )
    inverse = chain[1][NS_STEPS * heads :]
    own_out, weighted = land_mixture(parts, inverse, base, layout)
    if params["offload"]:
        own_out, weights["down"] = tied(own_out, weights["down"])
    mixes = spread_row(own_out)
    (att_low,) = on_core(
        functools.partial(near_kernel, half),
        [((width, tokens), LOW)],
        spot,
        qkv,
        low,
        high,
        layout["rims"],
        land,
        *mixes,
        params["lines"][0],
        us=3,
    )
    terms = tn(att_low, weights["out"]).reshape(batch_rows, tok_row, model)
    if ahead is not None:
        terms, ahead["attn"] = tied(terms, ahead["attn"])
    resid_one = hidden + (pair_collect(terms) + params["out_bias"])
    normed = layer_norm(resid_one, params["gain_one"], params["shift_one"])
    h_sets = token_sets(normed.astype(LOW), params["offload"])
    gelu_low, slopes, terms = [], [], []
    for h_full in h_sets:
        up_pre = dot("td,gdf->gtf", h_full, weights["up"]) + params["up_bias"][:, None, :]
        area = 0.5 * (1.0 + lax.erf(up_pre * 0.7071067811865476))
        bell = jnp.exp(-0.5 * up_pre * up_pre) * 0.3989422804014327
        gelu_low.append((up_pre * area).astype(LOW))
        slopes.append((area + up_pre * bell).astype(LOW))
        terms.append(dot("gtf,gfd->td", gelu_low[-1], weights["down"]))
    mlp_out = collect_sets(terms, batch_rows) + params["down_bias"]
    resid_two = normed + mlp_out
    result = layer_norm(resid_two, params["gain_two"], params["shift_two"])
    kept = dict(
        x_full=x_full,
        qkv=qkv,
        land=land,
        own_land=own_land,
        rims=(low, high),
        chain=chain,
        inverse=inverse,
        weighted=weighted,
        mixes=mixes,
        att_low=att_low,
        resid_one=resid_one,
        h_sets=h_sets,
        gelu_low=gelu_low,
        slopes=slopes,
        resid_two=resid_two,
    )
    return result, kept


def layer_backward(grad_out, kept, params, layout, pending):
    weights = params["weights"]
    spot = layout["spot"]
    batch_rows, piece, model = grad_out.shape
    tok_row = 2 * piece
    tokens = batch_rows * tok_row
    width = weights["out"].shape[0]
    half = params["half"]
    unused_two, pull_two = jax.vjp(
        layer_norm, kept["resid_two"], params["gain_two"], params["shift_two"]
    )
    grad_two, grad_gain_two, grad_shift_two = pull_two(grad_out)
    grad_mlp = grad_two.astype(LOW)
    grad_down_bias = jnp.sum(grad_mlp.astype(jnp.float32), axis=(0, 1))
    grad_sets = token_sets(grad_mlp, params["offload"])
    grad_ups, terms = [], []
    for grad_set, slope in zip(grad_sets, kept["slopes"]):
        grad_up = dot("td,gfd->gtf", grad_set, weights["down"])
        grad_ups.append((grad_up * slope.astype(jnp.float32)).astype(LOW))
        terms.append(dot("gtf,gdf->td", grad_ups[-1], weights["up"]))
    grad_normed = grad_two + collect_sets(terms, batch_rows)
    down_grad = sum(dot("gtf,td->gfd", g, d) for g, d in zip(kept["gelu_low"], grad_sets))
    up_grad = sum(dot("td,gtf->gdf", h, g) for h, g in zip(kept["h_sets"], grad_ups))
    ffn_grad = jnp.concatenate([up_grad, down_grad], axis=1).astype(LOW)
    grad_up_bias = sum(jnp.sum(g.astype(jnp.float32), axis=1) for g in grad_ups)
    if params["offload"]:
        ffn_grad = seq_scatter(ffn_grad)
        grad_up_bias = sides(grad_up_bias)
    else:
        ffn_one, attn_one = pending
        rows = attn_one.shape[1]
        packed = jnp.stack([attn_one[0], attn_one[1], ffn_grad[0, :rows], ffn_grad[0, rows:]])
        ffn_grad = (ffn_one, seq_scatter(packed))
        grad_up_bias = [grad_up_bias[0], jnp.zeros_like(grad_up_bias[0])]
    unused_one, pull_one = jax.vjp(
        layer_norm, kept["resid_one"], params["gain_one"], params["shift_one"]
    )
    grad_one, grad_gain_one, grad_shift_one = pull_one(grad_normed)
    grad_attn = grad_one.astype(LOW)
    grad_out_bias = jnp.sum(grad_attn.astype(jnp.float32), axis=(0, 1))
    grad_attn_full = pair_join(grad_attn, 1).reshape(tokens, model)
    grad_att = nt(weights["out"], grad_attn_full).astype(LOW)
    qkv, land, mixes = kept["qkv"], kept["land"], kept["mixes"]
    row = [((LANDMARKS, width), LOW)]
    rim = [((width, batch_rows * half), LOW)] * 2
    near_queries, *rest = on_core(
        functools.partial(near_back_kernel, half),
        [((width, tokens), jnp.float32)] + row * 8 + rim,
        spot,
        qkv,
        grad_att,
        land,
        *mixes,
        us=6,
    )
    near_outs, near_keys, (low, high) = rest[:4], rest[4:8], rest[8:]
    low, high = rank_shift(high, 1), rank_shift(low, -1)
    own_grad = item_sum(near_outs, layout)
    (own_mix_grad,) = on_core(
        mixture_grad_kernel,
        [((LANDMARKS, width + 128), LOW)],
        None,
        own_grad,
        kept["inverse"],
        kept["weighted"],
    )
    mix_grads = spread_row(own_mix_grad)
    if pending is not None:
        ffn_one, *mix_grads = tied(ffn_grad[0], *mix_grads)
        ffn_grad = (ffn_one, ffn_grad[1])
    grad_out_weight = nn(kept["att_low"], grad_attn_full)
    conv_grad, tap_grad = on_core(
        functools.partial(conv_back_kernel, half),
        [((width, tokens), jnp.float32), ((8, 128), jnp.float32)],
        None,
        qkv,
        grad_att,
        *kept["rims"],
        low,
        high,
        layout["rims"],
        params["lines"][1],
        us=6,
    )
    far_keys, values_low, *parts = on_core(
        far_back_kernel,
        [((width, tokens), jnp.float32), ((width, tokens), LOW)]
        + [((LANDMARKS, 2 * width), LOW)] * 4,
        spot,
        qkv,
        land,
        conv_grad,
        *mixes,
        *mix_grads,
        *near_keys,
        us=5,
    )
    own_grad, *parts = tied(own_grad, *parts)
    (own_land_grad,) = on_core(
        inverse_back_kernel,
        [((LANDMARKS, 2 * width), jnp.float32)],
        None,
        own_grad,
        kept["weighted"],
        kept["own_land"],
        *kept["chain"],
        us=13,
    )
    if params["offload"]:
        own_land_grad = item_sum(parts, layout) + own_land_grad
    else:
        first_grad = jnp.stack([nn(values_low, kept["x_full"]), grad_out_weight])
        first_mine, first_theirs = split_across(first_grad)
        land_sum, first_got = item_sum(parts, layout, first_theirs.astype(LOW))
        own_land_grad = land_sum + own_land_grad
        first_grad = (first_mine + first_got.astype(jnp.float32)).astype(LOW)
    land_grads = spread_row(own_land_grad.astype(LOW))
    (grad_qkv,) = on_core(
        token_grad_kernel,
        [((3 * width, tokens), LOW)],
        spot,
        near_queries,
        far_keys,
        values_low,
        layout["pool"],
        *land_grads,
    )
    terms = tn(grad_qkv, weights["qkv"]).reshape(batch_rows, tok_row, model)
    grad_hidden = grad_one + pair_collect(terms)
    if params["offload"]:
        grad_weight = nn(grad_qkv, kept["x_full"])
        attn_grad = jnp.concatenate([grad_weight, grad_out_weight], axis=0)
        attn_grad = attn_grad.reshape(4, 2, width // 2, model).astype(LOW)
        attn_grad = jnp.swapaxes(attn_grad, 0, 1).reshape(2, 2 * width, model)
    else:
        grad_weight = nn(grad_qkv[: 2 * width], kept["x_full"]).reshape(2, width, model)
        attn_grad = across_sum(split_across(grad_weight))
        unused, packed = tied(attn_grad, ffn_grad[1])
        ffn_grad = (ffn_grad[0], packed)
        attn_grad = jnp.concatenate([attn_grad, first_grad], axis=0)
    grad_bias = jnp.sum(grad_qkv.astype(jnp.float32), axis=1)
    heads = width // LANDMARKS
    mids = [
        split_flat(grad_bias[:width]),
        split_flat(grad_bias[2 * width :]),
        split_flat(tap_grad[:heads, : 2 * half + 1]),
        grad_up_bias,
    ]
    smalls = [
        grad_out_bias,
        grad_down_bias,
        grad_gain_one,
        grad_shift_one,
        grad_gain_two,
        grad_shift_two,
    ]
    return grad_hidden, (attn_grad, ffn_grad), mids, smalls


def sides(values):
    across = place()[1]
    return [jnp.where(across == 0, values[0], values[1]), jnp.where(across == 0, values[1], values[0])]


def seq_scatter(values):
    return lax.psum_scatter(values, "seq", scatter_dimension=values.ndim - 2, tiled=True)


def seq_gather(values):
    return lax.all_gather(values, "seq", axis=0, tiled=True)


def across_pick(values):
    mine, theirs = sides(values)
    return across_sum([mine.astype(jnp.float32), theirs])


def tied(values, *others):
    return lax.optimization_barrier((values,) + others)


def across_sum(pair):
    mine, theirs = pair
    got = exchange(theirs.astype(LOW), 0, 2).astype(jnp.float32)
    return (mine + got).astype(LOW)


def split_flat(values):
    across = place()[1]
    half = values.shape[0] // 2
    low, high = values[:half], values[half:]
    return [jnp.where(across == 0, low, high), jnp.where(across == 0, high, low)]


def split_across(values):
    across = place()[1]
    half = values.shape[1] // 2
    model = values.shape[2]
    low = values[:, :half].reshape(-1, model)
    high = values[:, half:].reshape(-1, model)
    return [jnp.where(across == 0, low, high), jnp.where(across == 0, high, low)]


def halve(values, mask):
    side = (lax.axis_index("seq") // mask) % 2
    half = values.shape[0] // 2
    low, high = values[:half], values[half:]
    keep = jnp.where(side == 0, low, high)
    sent = jnp.where(side == 0, high, low)
    return (keep.astype(jnp.float32) + exchange(sent, mask, 0).astype(jnp.float32)).astype(LOW)


def double(values, mask):
    side = (lax.axis_index("seq") // mask) % 2
    other = exchange(values, mask, 0)
    low = jnp.where(side == 0, values, other)
    high = jnp.where(side == 0, other, values)
    return jnp.concatenate([low, high], axis=0)


def reduce_big(total):
    masks = [1 << i for i in range(lax.axis_size("seq").bit_length() - 1)]
    rows = total.shape[0]
    extra = -rows % (2 * lax.axis_size("seq"))
    if extra:
        total = jnp.pad(total, ((0, extra), (0, 0)))
    middle = total.shape[0] // 2
    done = []
    for part, order in ((total[:middle], masks), (total[middle:], masks[1:] + masks[:1])):
        for mask in order:
            part = halve(part, mask)
        for mask in reversed(order):
            part = double(part, mask)
        done.append(part)
    return jnp.concatenate(done, axis=0)[:rows]


def seq_sum(values):
    mask = 1
    while mask < lax.axis_size("seq"):
        values = values + exchange(values, mask, 0)
        mask *= 2
    return values


def reduce_small(mid, small):
    mine = jnp.concatenate([m[0].reshape(-1) for m in mid])
    theirs = jnp.concatenate([m[1].reshape(-1) for m in mid])
    every = jnp.concatenate([s.reshape(-1) for s in small])
    count, extra = every.shape[0], mine.shape[0]
    pad = -(count + extra) % 1024
    got = exchange(jnp.pad(jnp.concatenate([every, theirs]), (0, pad)), 0, 2)
    total = jnp.pad(jnp.concatenate([every, mine]), (0, pad)) + got
    total = seq_sum(total)
    every = total[:count]
    every = every + exchange(every, 0, 1)
    mids, at = [], count
    for m in mid:
        mids.append(total[at : at + m[0].size].reshape(m[0].shape))
        at += m[0].size
    smalls, at = [], 0
    for s in small:
        smalls.append(every[at : at + s.size].reshape(s.shape))
        at += s.size
    return mids, smalls


def on_device(
    hidden_in,
    query_weight,
    key_weight,
    value_weight,
    query_bias,
    value_bias,
    out_weight,
    out_bias,
    conv_taps,
    up_weight,
    up_bias,
    down_weight,
    down_bias,
    gain_one,
    shift_one,
    gain_two,
    shift_two,
    out_grad,
    item_lengths,
):
    tok_row = hidden_in.shape[1] * 2
    half = (conv_taps.shape[2] - 1) // 2
    layout = item_layout(item_lengths, tok_row, half)
    q_bias, v_bias, taps, both_up = fetch_small(query_bias, value_bias, conv_taps, up_bias)
    hidden = hidden_in.astype(jnp.float32)
    x_full, pooled = join_pool(hidden, layout)
    weights, pooled = fetch_weights(
        query_weight, key_weight, value_weight, out_weight, up_weight, down_weight, pooled
    )
    params = []
    for i in range(2):
        params.append(
            dict(
                weights=weights[i],
                half=half,
                offload=i == 1,
                q_bias=q_bias[i],
                v_bias=v_bias[i],
                lines=tap_lines(taps[i]),
                up_bias=both_up[i] if i == 1 else up_bias[:1],
                out_bias=out_bias[i],
                down_bias=down_bias[i],
                gain_one=gain_one[i],
                shift_one=shift_one[i],
                gain_two=gain_two[i],
                shift_two=shift_two[i],
            )
        )
    kept = [None, None]
    for i in range(2):
        joined = (x_full, pooled) if i == 0 else join_pool(hidden, layout)
        ahead = weights[1] if i == 0 else None
        hidden, kept[i] = layer_forward(hidden, params[i], layout, joined, ahead)
    grad = out_grad
    big, mid, small = [None, None], [None, None], [None, None]
    pending = None
    for i in (1, 0):
        grad, grads, mid[i], small[i] = layer_backward(grad, kept[i], params[i], layout, pending)
        if i == 1:
            attn_grad, ffn_grad = grads
            grad, ffn_grad = tied(grad, ffn_grad)
            pending = [seq_gather(across_pick(ffn_grad)), attn_grad]
        else:
            attn_grad, (ffn_one, packed) = grads
            packed = jnp.concatenate([across_pick(packed[:2])[None], packed[2:]], axis=0)
            packed = lax.all_gather(packed, "seq", axis=1, tiled=True)
            big[0] = (reduce_big(attn_grad), packed[1:].reshape(-1, packed.shape[2]))
            big[1] = (packed[0], ffn_one)
    mids, smalls = reduce_small(
        [[jnp.stack(m) for m in zip(*pairs)] for pairs in zip(*mid)],
        [jnp.stack(pair) for pair in zip(*small)],
    )
    width = query_weight.shape[2]
    attn = jnp.stack([big[0][0], big[1][0]]).reshape(2, 4, width, -1)
    qkv = [jnp.swapaxes(attn[:, i], 1, 2).astype(jnp.float32) for i in range(3)]
    outs = attn[:, 3].astype(jnp.float32)
    both = [big[0][1], big[1][1]]
    rows = up_weight.shape[1]
    ups = jnp.stack([one[:rows] for one in both]).astype(jnp.float32)
    downs = jnp.stack([one[rows:] for one in both]).astype(jnp.float32)
    return (
        hidden.astype(LOW),
        grad,
        qkv[0],
        qkv[1],
        qkv[2],
        mids[0],
        mids[1],
        outs,
        smalls[0],
        mids[2].reshape(conv_taps.shape),
        ups,
        mids[3],
        downs,
        smalls[1],
        smalls[2],
        smalls[3],
        smalls[4],
        smalls[5],
    )


def solution(mesh):
    placed = (
        P(None, ("seq", "head"), None),
        P(None, None, "head"),
        P(None, None, "head"),
        P(None, None, "head"),
        P(None, "head"),
        P(None, "head"),
        P(None, "head", None),
        P(),
        P(None, "head", None),
        P(None, None, "head"),
        P(None, "head"),
        P(None, "head", None),
        P(),
        P(),
        P(),
        P(),
        P(),
        P(None, ("seq", "head"), None),
        P(),
    )
    return jax.shard_map(
        on_device,
        mesh=mesh,
        in_specs=placed,
        out_specs=(
            P(None, ("seq", "head"), None),
            P(None, ("seq", "head"), None),
            P(None, None, "head"),
            P(None, None, "head"),
            P(None, None, "head"),
            P(None, "head"),
            P(None, "head"),
            P(None, "head", None),
            P(),
            P(None, "head", None),
            P(None, None, "head"),
            P(None, "head"),
            P(None, "head", None),
            P(),
            P(),
            P(),
            P(),
            P(),
        ),
        check_vma=False,
    )
```
